32 devices in a mesh: tm: 2 (over x), height: 2 (over y), seq: 8 (over z, core).
Axes of the slice: x: 2, y: 2, z: 4, core: 2. Of those that a mesh axis runs over, the one named last changes fastest.
Arguments:
- queries: bfloat16 [16384, 2048], P(('tm', 'height', 'seq')), may hold values from -170 to 170
- key_states: bfloat16 [16384, 2048], P(('tm', 'height', 'seq')), may hold values from -6.5 to 6.5
- value_states: bfloat16 [16384, 2048], P(('tm', 'height', 'seq')), may hold values from -6 to 6
- out_grad: bfloat16 [16384, 2048], P(('tm', 'height', 'seq')), may hold values from -6 to 6
- tile_valid: int32 [2, 8, 16], replicated, may hold values 0 or 1
- width_shift: int32 [2, 8, 16], replicated, may hold values from -1 to 1, as said below
Outputs:
- query_grad: bfloat16 [16384, 2048], P(('tm', 'height', 'seq'))
- key_grad: bfloat16 [16384, 2048], P(('tm', 'height', 'seq'))
- value_grad: bfloat16 [16384, 2048], P(('tm', 'height', 'seq'))
The draws below stay inside these ranges and needn't reach their ends.
Inputs may be any that keep to these rules, and one draw needn't show every extreme that they name: `width_shift`: each query tile's window of three column tiles, from l + shift - 1 to l + shift + 1, lies inside the columns 0 to 15.
All inputs are finite; a program needn't handle non-finite values.
Results may differ from the reference program's by a relative error of at most 0.005.
Values may be sent and summed in bfloat16 or wider, within the bound.
No kernel may reach another device: no remote copies, remote signals or barrier semaphores. Data moves between devices by JAX's collectives and lax.ppermute only.
A program may use at most 448 MiB of HBM per device.

```python
from functools import partial
import jax
import jax.numpy as jnp
from jax import lax

D_HEAD = 128
HEADS = 16
TILE = 4
TH_DEV = 4
TW = 16
NTT = 2
NHT = 8
TOKENS = 16384
N_HEIGHT = 2


def shared_base(key):
    values = jax.random.normal(key, (TOKENS, HEADS * D_HEAD), jnp.float32)
    return jnp.clip(values, -6.0, 6.0)


def draw_queries(key, part):
    key = jax.random.fold_in(key, 7)
    values = jnp.clip(jax.random.normal(key, (TOKENS, HEADS * D_HEAD), jnp.float32), -6.0, 6.0)
    return values.astype(jnp.bfloat16)


def draw_key_states(key, part):
    base_rows = shared_base(key)
    return base_rows.astype(jnp.bfloat16)


def draw_width_shift(key, part):
    key = jax.random.fold_in(key, 11)
    raw_shift = jax.random.randint(key, (NTT, NHT, TW), -1, 2)
    columns = jnp.arange(TW)[None, None, :]
    return jnp.clip(raw_shift, 1 - columns, TW - 2 - columns).astype(jnp.int32)


def place_ends(array, own_key, smallest, largest):
    spot = [jax.random.randint(jax.random.fold_in(own_key, axis), (), 0, length) for axis, length in enumerate(array.shape)]
    widest = array.shape.index(max(array.shape))
    neighbour = spot[:widest] + [(spot[widest] + 1) % array.shape[widest]] + spot[widest + 1:]
    return array.at[tuple(spot)].set(smallest).at[tuple(neighbour)].set(largest)


def block_scale(rng, shape, split, least, top_value):
    loudness, own = 1.0, jax.random.fold_in(rng, 6)
    for dim, blocks in split:
        steps = jnp.exp(jax.random.uniform(jax.random.fold_in(own, dim), (blocks,), jnp.float32, least / len(split), top_value / len(split)))
        loudness = loudness * jnp.repeat(steps, shape[dim] // blocks).reshape([-1 if axis == dim else 1 for axis in range(len(shape))])
    return loudness


def gaussian(own_key, extent, scale, most, pieces=(), dtype=jnp.bfloat16):
    entries = jax.random.normal(own_key, extent, jnp.float32) * scale
    if len(pieces) > 0:
        entries = block_scale(own_key, extent, pieces, -0.22, 0.18) * entries
    return jnp.clip(entries, min=-most, max=most).astype(dtype)


def setup_inputs(seed: int = 0) -> dict:
    keys = jax.random.split(jax.random.key(seed), 7)
    return {
        "queries": draw_queries(jax.random.fold_in(keys[6], 71), 0),
        "key_states": draw_key_states(jax.random.fold_in(keys[6], 71), 0),
        "value_states": gaussian(keys[2], (TOKENS, HEADS * D_HEAD), 1.0, 6.0, ((0, 32),)),
        "out_grad": gaussian(keys[3], (TOKENS, HEADS * D_HEAD), 1.0, 6.0, ((0, 32),)),
        "tile_valid": place_ends((jax.random.randint(keys[4], (NTT, NHT, TW), 0, 6) < 5).astype(jnp.int32), jax.random.fold_in(keys[4], 1), 0, 1),
        "width_shift": draw_width_shift(jax.random.fold_in(keys[6], 71), 0),
    }


MASKED_SCORE = -1e30
HIGHEST = lax.Precision.HIGHEST


def grid_tiles(rows_in):
    blocks = rows_in.reshape(NTT, N_HEIGHT, TILE, TH_DEV, TILE, TW, TILE, HEADS, D_HEAD)
    blocks = blocks.transpose(7, 0, 1, 3, 5, 2, 4, 6, 8)
    return blocks.reshape(HEADS, NTT, NHT, TW, TILE ** 3, D_HEAD)


def grid_rows(tiles_in):
    blocks = tiles_in.reshape(HEADS, NTT, N_HEIGHT, TH_DEV, TW, TILE, TILE, TILE, D_HEAD)
    blocks = blocks.transpose(1, 2, 5, 3, 6, 4, 7, 0, 8)
    return blocks.reshape(TOKENS, HEADS * D_HEAD)


def head_grads(valid_pad, width_shift, score_scale, packed):
    query_tiles, key_tiles, value_tiles, grad_tiles = packed
    tile_cells = TILE ** 3
    padding = ((1, 1), (1, 1), (0, 0), (0, 0), (0, 0))
    key_pad = jnp.pad(key_tiles, padding).astype(jnp.float32)
    value_pad = jnp.pad(value_tiles, padding).astype(jnp.float32)
    key_total = jnp.zeros(key_pad.shape, jnp.float32)
    value_total = jnp.zeros(value_pad.shape, jnp.float32)
    triple = jnp.arange(3)
    height_query = jnp.arange(NHT)[:, None, None, None, None]
    width_query = jnp.arange(TW)[None, :, None, None, None]
    window_shape = (NHT, TW, 3, 3, 3)
    query_count = NHT * TW
    query_parts = []
    for frame_tile in range(NTT):
        time_index = jnp.broadcast_to(frame_tile + triple[None, None, :, None, None], window_shape)
        height_index = jnp.broadcast_to(height_query + triple[None, None, None, :, None], window_shape)
        starts = width_query + width_shift[frame_tile][:, :, None, None, None] - 1
        width_index = jnp.broadcast_to(starts + triple[None, None, None, None, :], window_shape)
        key_win = key_pad[time_index, height_index, width_index].reshape(query_count, 27 * tile_cells, D_HEAD)
        value_win = value_pad[time_index, height_index, width_index].reshape(query_count, 27 * tile_cells, D_HEAD)
        own_tile = (time_index == frame_tile + 1) & (height_index == height_query + 1) & (width_index == width_query)
        allowed = (valid_pad[time_index, height_index, width_index] == 1) | own_tile
        key_mask = jnp.broadcast_to(allowed.reshape(query_count, 1, 27, 1), (query_count, 1, 27, tile_cells))
        key_mask = key_mask.reshape(query_count, 1, 27 * tile_cells)
        query_rows = query_tiles[frame_tile].reshape(query_count, tile_cells, D_HEAD).astype(jnp.float32)
        grad_rows = grad_tiles[frame_tile].reshape(query_count, tile_cells, D_HEAD).astype(jnp.float32)
        scores = score_scale * jnp.einsum("qid,qjd->qij", query_rows, key_win, precision=HIGHEST)
        row_max = jnp.max(jnp.where(key_mask, scores, MASKED_SCORE), axis=-1, keepdims=True)
        exp_total = jnp.sum(jnp.exp(jnp.where(key_mask, scores - row_max, MASKED_SCORE)), axis=-1, keepdims=True)
        log_total = row_max + jnp.log(exp_total)
        weights = jnp.exp(jnp.where(key_mask, scores - log_total, MASKED_SCORE))
        weights_low = lax.optimization_barrier(weights.astype(jnp.bfloat16)).astype(jnp.float32)
        grad_weights = jnp.einsum("qid,qjd->qij", grad_rows, value_win, precision=HIGHEST)
        delta_row = jnp.sum(weights * grad_weights, axis=-1, keepdims=True)
        dscore = lax.optimization_barrier((weights * (grad_weights - delta_row)).astype(jnp.bfloat16))
        dscore = dscore.astype(jnp.float32)
        query_part = score_scale * jnp.einsum("qij,qjd->qid", dscore, key_win, precision=HIGHEST)
        query_parts.append(query_part.reshape(NHT, TW, tile_cells, D_HEAD))
        key_part = score_scale * jnp.einsum("qij,qid->qjd", dscore, query_rows, precision=HIGHEST)
        value_part = jnp.einsum("qij,qid->qjd", weights_low, grad_rows, precision=HIGHEST)
        key_total = key_total.at[time_index, height_index, width_index].add(
            key_part.reshape(NHT, TW, 3, 3, 3, tile_cells, D_HEAD))
        value_total = value_total.at[time_index, height_index, width_index].add(
            value_part.reshape(NHT, TW, 3, 3, 3, tile_cells, D_HEAD))
    query_total = jnp.stack(query_parts).astype(jnp.bfloat16)
    return (query_total, key_total[1:-1, 1:-1].astype(jnp.bfloat16),
            value_total[1:-1, 1:-1].astype(jnp.bfloat16))


def reference(queries, key_states, value_states, out_grad, tile_valid, width_shift):
    score_scale = D_HEAD ** -0.5
    valid_pad = jnp.pad(tile_valid, ((1, 1), (1, 1), (0, 0)))
    packed = (grid_tiles(queries), grid_tiles(key_states), grid_tiles(value_states), grid_tiles(out_grad))
    query_tiles, key_tiles, value_tiles = lax.map(partial(head_grads, valid_pad, width_shift, score_scale), packed)
    return grid_rows(query_tiles), grid_rows(key_tiles), grid_rows(value_tiles)
```

```python
from functools import partial

import jax
import jax.numpy as jnp
from jax import lax
from jax.experimental import pallas as pl
from jax.experimental.pallas import tpu as pltpu
from jax.sharding import PartitionSpec as P

D_HEAD = 128
HEADS = 16
TILE = 4
TH_DEV = 4
TW = 16


MASKED_SCORE = -1e30


def passed_along(block, axis, distance):
    devices = range(lax.axis_size(axis))
    route = [((i - distance) % len(devices), i) for i in devices]
    return lax.ppermute(block, axis, route)


def with_halo(cells, sides, width):
    for axis, dim in sides:
        count = lax.axis_size(axis)
        ends = count - 1
        head = lax.slice_in_dim(cells, 0, width, axis=dim)
        tail = lax.slice_in_dim(cells, cells.shape[dim] - width, cells.shape[dim], axis=dim)
        cells = jnp.concatenate(
            [
                lax.ppermute(tail, axis, [(i, (i + 1) % count) for i in range(ends)]),
                cells,
                lax.ppermute(head, axis, [((i + 1) % count, i) for i in range(ends)]),
            ],
            axis=dim,
        )
    return cells


def shifted(value, axis, steps):
    count = lax.axis_size(axis)
    initial, last = (max(0, -steps), min(count, count - steps))
    return lax.ppermute(value, axis, [(source, source + steps) for source in range(initial, last)])


def to_tiles(grid_in, tile_edge):
    groups, frames, grid_rows, grid_cols = grid_in.shape[:4]
    trailing = grid_in.shape[4:]
    split_grid = grid_in.reshape(
        (
            groups,
            frames // tile_edge,
            tile_edge,
            grid_rows // tile_edge,
            tile_edge,
            grid_cols // tile_edge,
            tile_edge,
        )
        + trailing
    )
    axis_order = (0, 1, 3, 5, 2, 4, 6) + tuple(range(7, 7 + len(trailing)))
    return split_grid.transpose(axis_order).reshape(
        (groups, frames // tile_edge, grid_rows // tile_edge, grid_cols // tile_edge, tile_edge**3)
        + trailing
    )


def from_tiles(tiles_in, tile_edge):
    groups, frame_tiles, row_tiles, col_tiles = tiles_in.shape[:4]
    trailing = tiles_in.shape[5:]
    split_grid = tiles_in.reshape(
        (groups, frame_tiles, row_tiles, col_tiles, tile_edge, tile_edge, tile_edge) + trailing
    )
    axis_order = (0, 1, 4, 2, 5, 3, 6) + tuple(range(7, 7 + len(trailing)))
    return split_grid.transpose(axis_order).reshape(
        (groups, frame_tiles * tile_edge, row_tiles * tile_edge, col_tiles * tile_edge) + trailing
    )


def edge_tiles(piece_own, half_index):
    return jnp.where(half_index == 0, piece_own[:, :, :, -2:], piece_own[:, :, :, :2])


def widen_rim(piece_own, received, half_index):
    left_side = jnp.concatenate([piece_own, received], axis=3)
    right_side = jnp.concatenate([received, piece_own], axis=3)
    return jnp.where(half_index == 0, left_side, right_side)


def shards(queries, key_states, value_states, out_grad, tile_valid, width_shift):
    seq_count = lax.axis_size("seq")
    groups = 2 * HEADS // seq_count
    half_width = TW * TILE // 2
    lines_dev = queries.shape[0] // (TW * TILE)
    tiles_half = TW // 2
    tile_cells = TILE**3
    score_scale = D_HEAD ** (-0.5)
    time_index = lax.axis_index("tm")
    height_index = lax.axis_index("height")
    half_index = lax.axis_index("seq") * groups // HEADS
    anchor = half_index * (tiles_half - 2)

    def to_heads(rows_in):
        split_rows = rows_in.reshape(lines_dev, 2, half_width, HEADS, D_HEAD)
        return split_rows.transpose(1, 3, 0, 2, 4).reshape(2 * HEADS, lines_dev, half_width, D_HEAD)

    moved = (
        lax.all_to_all(to_heads(queries), "seq", split_axis=0, concat_axis=1, tiled=True),
        lax.all_to_all(to_heads(key_states), "seq", split_axis=0, concat_axis=1, tiled=True),
        lax.all_to_all(to_heads(value_states), "seq", split_axis=0, concat_axis=1, tiled=True),
        lax.all_to_all(to_heads(out_grad), "seq", split_axis=0, concat_axis=1, tiled=True),
    )

    def own_tiles(grid_part):
        return to_tiles(grid_part.reshape(groups, TILE, TILE * TH_DEV, half_width, D_HEAD), TILE)

    query_own, keys_own, values_own, grads_own = [own_tiles(grid_part) for grid_part in moved]
    key_edges = passed_along(
        (edge_tiles(keys_own, half_index), edge_tiles(values_own, half_index)),
        "seq",
        seq_count // 2,
    )
    keys_wide = widen_rim(keys_own, key_edges[0], half_index)
    values_wide = widen_rim(values_own, key_edges[1], half_index)
    keys_ext, values_ext = (
        with_halo(keys_wide, (("tm", 1), ("height", 2)), 1),
        with_halo(values_wide, (("tm", 1), ("height", 2)), 1),
    )
    table_start = (time_index, height_index * TH_DEV, anchor)
    table_span = (3, TH_DEV + 2, tiles_half + 2)
    table_pad = ((1, 1), (1, 1), (0, 0))
    valid_ext = lax.dynamic_slice(jnp.pad(tile_valid, table_pad), table_start, table_span)
    shift_ext = lax.dynamic_slice(jnp.pad(width_shift, table_pad), table_start, table_span)
    triple = jnp.arange(3)
    query_cols = jnp.arange(tiles_half) + 2 * half_index

    def query_row(keep_grads, carry, row_index):
        query_tiles = lax.dynamic_index_in_dim(query_own[:, 0], row_index, 1, keepdims=False)
        grad_tiles = lax.dynamic_index_in_dim(grads_own[:, 0], row_index, 1, keepdims=False)
        key_rows = lax.dynamic_slice_in_dim(keys_ext, row_index, 3, 2)
        value_rows = lax.dynamic_slice_in_dim(values_ext, row_index, 3, 2)
        shift_row = lax.dynamic_index_in_dim(shift_ext[1], row_index + 1, 0, keepdims=False)
        starts = query_cols + lax.dynamic_slice_in_dim(shift_row, 2 * half_index, tiles_half) - 1
        window_cols = starts[:, None] + triple[None, :]
        key_win = key_rows[:, :, :, window_cols].transpose(0, 3, 1, 2, 4, 5, 6)
        key_win = key_win.reshape(groups, tiles_half, 27 * tile_cells, D_HEAD)
        value_win = value_rows[:, :, :, window_cols].transpose(0, 3, 1, 2, 4, 5, 6)
        value_win = value_win.reshape(groups, tiles_half, 27 * tile_cells, D_HEAD)
        valid_rows = lax.dynamic_slice_in_dim(valid_ext, row_index, 3, 1)[:, :, window_cols]
        own_tile = (
            (triple[:, None, None, None] == 1)
            & (triple[None, :, None, None] == 1)
            & (window_cols[None, None] == query_cols[None, None, :, None])
        )
        allowed = ((valid_rows == 1) | own_tile).transpose(2, 0, 1, 3)
        tile_bias = jnp.where(allowed.reshape(tiles_half, 27, 1), 0.0, MASKED_SCORE).astype(
            jnp.float32
        )
        mask_bias = jnp.broadcast_to(tile_bias, (tiles_half, 27, tile_cells)).reshape(
            1, tiles_half, 1, 27 * tile_cells
        )
        scores = (
            score_scale
            * jnp.einsum(
                "gwid,gwjd->gwij", query_tiles, key_win, preferred_element_type=jnp.float32
            )
            + mask_bias
        )
        row_max = jnp.max(scores, axis=-1, keepdims=True)
        probs = jnp.exp(scores - row_max)
        exp_total = jnp.sum(probs, axis=-1, keepdims=True)
        log_total = row_max + jnp.log(exp_total)
        weights = probs / exp_total
        grad_weights = jnp.einsum(
            "gwid,gwjd->gwij", grad_tiles, value_win, preferred_element_type=jnp.float32
        )
        delta_row = jnp.sum(weights * grad_weights, axis=-1, keepdims=True)
        dscore = (weights * (grad_weights - delta_row)).astype(jnp.bfloat16)
        query_part = score_scale * jnp.einsum(
            "gwij,gwjd->gwid", dscore, key_win, preferred_element_type=jnp.float32
        )
        key_acc, value_acc = carry
        key_part = score_scale * jnp.einsum(
            "gwij,gwid->gwjd", dscore, query_tiles, preferred_element_type=jnp.float32
        )
        value_part = jnp.einsum(
            "gwij,gwid->gwjd",
            weights.astype(jnp.bfloat16),
            grad_tiles,
            preferred_element_type=jnp.float32,
        )
        time_pick = triple[None, :, None, None]
        row_pick = triple[None, None, :, None]
        col_pick = window_cols[:, None, None, :]

        def spread(acc_grid, part_grad):
            shaped = part_grad.reshape(groups, tiles_half, 3, 3, 3, tile_cells, D_HEAD)
            rows_now = lax.dynamic_slice_in_dim(acc_grid, row_index, 3, 2)
            rows_now = rows_now.at[:, time_pick, row_pick, col_pick].add(shaped)
            return lax.dynamic_update_slice_in_dim(acc_grid, rows_now, row_index, 2)

        carry = (spread(key_acc, key_part), spread(value_acc, value_part))
        return (carry, (query_part, log_total[..., 0], delta_row[..., 0]))

    zero_grads = jnp.zeros(keys_ext.shape, jnp.float32)
    (key_acc, value_acc), row_outputs = lax.scan(
        partial(query_row, True), (zero_grads, zero_grads), jnp.arange(TH_DEV)
    )
    from_below = (
        shifted(key_acc[:, :, -1:].astype(jnp.bfloat16), "height", 1).astype(jnp.float32),
        shifted(value_acc[:, :, -1:].astype(jnp.bfloat16), "height", 1).astype(jnp.float32),
    )
    from_above = (
        shifted(key_acc[:, :, :1].astype(jnp.bfloat16), "height", -1).astype(jnp.float32),
        shifted(value_acc[:, :, :1].astype(jnp.bfloat16), "height", -1).astype(jnp.float32),
    )

    def fold_rows(acc_grid, lower_in, upper_in):
        acc_grid = acc_grid.at[:, :, 1:2].add(lower_in)
        acc_grid = acc_grid.at[:, :, TH_DEV : TH_DEV + 1].add(upper_in)
        return acc_grid[:, :, 1 : TH_DEV + 1]

    key_core = fold_rows(key_acc, from_below[0], from_above[0])
    value_core = fold_rows(value_acc, from_below[1], from_above[1])
    from_before = shifted((key_core[:, 2:3], value_core[:, 2:3]), "tm", 1)
    from_after = shifted((key_core[:, 0:1], value_core[:, 0:1]), "tm", -1)
    key_mid = key_core[:, 1] + from_before[0][:, 0] + from_after[0][:, 0]
    value_mid = value_core[:, 1] + from_before[1][:, 0] + from_after[1][:, 0]

    def rim_of(mid_grid):
        return jnp.where(half_index == 0, mid_grid[:, :, -2:], mid_grid[:, :, :2])

    rim_back = (
        passed_along(rim_of(key_mid).astype(jnp.bfloat16), "seq", seq_count // 2).astype(
            jnp.float32
        ),
        passed_along(rim_of(value_mid).astype(jnp.bfloat16), "seq", seq_count // 2).astype(
            jnp.float32
        ),
    )

    def settle(mid_grid, received):
        left_side = jnp.concatenate(
            [
                mid_grid[:, :, : tiles_half - 2],
                mid_grid[:, :, tiles_half - 2 : tiles_half] + received,
            ],
            axis=2,
        )
        right_side = jnp.concatenate([mid_grid[:, :, 2:4] + received, mid_grid[:, :, 4:]], axis=2)
        return jnp.where(half_index == 0, left_side, right_side)

    key_grid = from_tiles(settle(key_mid, rim_back[0])[:, None], TILE).astype(jnp.bfloat16)
    value_grid = from_tiles(settle(value_mid, rim_back[1])[:, None], TILE).astype(jnp.bfloat16)
    query_grid = from_tiles(jnp.moveaxis(row_outputs[0], 0, 1)[:, None], TILE).astype(jnp.bfloat16)

    def to_lines(grid_part):
        return grid_part.reshape(groups, TILE * TILE * TH_DEV, half_width, D_HEAD)

    returned = (
        lax.all_to_all(to_lines(query_grid), "seq", split_axis=1, concat_axis=0, tiled=True),
        lax.all_to_all(to_lines(key_grid), "seq", split_axis=1, concat_axis=0, tiled=True),
        lax.all_to_all(to_lines(value_grid), "seq", split_axis=1, concat_axis=0, tiled=True),
    )

    def to_rows(grid_part):
        split_rows = grid_part.reshape(2, HEADS, lines_dev, half_width, D_HEAD)
        return split_rows.transpose(2, 0, 3, 1, 4).reshape(
            lines_dev * 2 * half_width, HEADS * D_HEAD
        )

    return (to_rows(returned[0]), to_rows(returned[1]), to_rows(returned[2]))


TOK = TILE * TILE
SPAN = 5
LANES = 2 * D_HEAD
LOG2_E = 1.4426950408889634
VMEM_BYTES = 56 * 1024 * 1024
NT = (((1,), (1,)), ((), ()))
NN = (((1,), (0,)), ((), ()))
TN = (((0,), (0,)), ((), ()))


def row_order(inverse):
    lines = TILE * TW * TILE
    target = lax.broadcasted_iota(jnp.int32, (lines, lines), 0)
    source = lax.broadcasted_iota(jnp.int32, (lines, lines), 1)
    if inverse:
        target, source = source, target
    col, line, x = target // TOK, (target // TILE) % TILE, target % TILE
    return (source == line * (TW * TILE) + col * TILE + x).astype(jnp.bfloat16)


def split_kernel(first_ref, second_ref, out_ref):
    order = row_order(False)
    lines = order.shape[0]
    heads = out_ref.shape[0]
    for row in range(first_ref.shape[0] // lines):
        rows = slice(row * lines, (row + 1) * lines)
        for side, ref in enumerate((first_ref, second_ref)):
            moved = lax.dot_general(order, ref[rows, :], NN, preferred_element_type=jnp.float32)
            moved = moved.astype(jnp.bfloat16)
            for head in range(heads):
                out_ref[head, rows, side * D_HEAD : (side + 1) * D_HEAD] = moved[
                    :, head * D_HEAD : (head + 1) * D_HEAD
                ]


def split_heads(first, second):
    rows = first.shape[0]
    step = 4
    return pl.pallas_call(
        split_kernel,
        grid=(HEADS // step,),
        in_specs=[pl.BlockSpec((rows, step * D_HEAD), lambda g: (0, g))] * 2,
        out_specs=pl.BlockSpec((step, rows, LANES), lambda g: (g, 0, 0)),
        out_shape=jax.ShapeDtypeStruct((HEADS, rows, LANES), jnp.bfloat16),
        compiler_params=pltpu.CompilerParams(vmem_limit_bytes=VMEM_BYTES),
    )(first, second)


def join_kernel(moved_ref, *out_refs):
    order = row_order(True)
    lines = order.shape[0]
    for row in range(moved_ref.shape[1] // lines):
        rows = slice(row * lines, (row + 1) * lines)
        for head in range(moved_ref.shape[0]):
            back = lax.dot_general(
                order, moved_ref[head, rows, :], NN, preferred_element_type=jnp.float32
            ).astype(jnp.bfloat16)
            for side, ref in enumerate(out_refs):
                ref[rows, head * D_HEAD : (head + 1) * D_HEAD] = back[
                    :, side * D_HEAD : (side + 1) * D_HEAD
                ]


def join_heads(moved):
    rows, lanes = moved.shape[1:]
    count = lanes // D_HEAD
    step = 4
    return pl.pallas_call(
        join_kernel,
        grid=(HEADS // step,),
        in_specs=[pl.BlockSpec((step, rows, lanes), lambda g: (g, 0, 0))],
        out_specs=[pl.BlockSpec((rows, step * D_HEAD), lambda g: (0, g))] * count,
        out_shape=[jax.ShapeDtypeStruct((rows, HEADS * D_HEAD), jnp.bfloat16)] * count,
        compiler_params=pltpu.CompilerParams(vmem_limit_bytes=VMEM_BYTES),
    )(moved)


def grad_kernel(
    side_ref, bias_ref, query_ref, kv_hbm, halo_hbm,
    dq_ref, dkv_ref, edge_ref, halo_out_ref,
    kv, acc, scores, low, sem,
):
    frames = kv.shape[1]
    rows_own = kv.shape[0] - 2
    cols = query_ref.shape[4] // TOK
    key_cols = kv.shape[3] // TOK
    side = side_ref[0]
    halo_slot = jnp.where(side == 0, rows_own + 1, 0)
    blank_slot = rows_own + 1 - halo_slot
    copies = [
        pltpu.make_async_copy(kv_hbm.at[:, :, row // 2, row % 2], kv.at[1 + row], sem.at[row])
        for row in range(rows_own)
    ]
    copies.append(pltpu.make_async_copy(halo_hbm, kv.at[halo_slot], sem.at[rows_own]))
    for copy in copies:
        copy.start()
    kv[blank_slot] = jnp.zeros(kv.shape[1:], kv.dtype)
    acc[...] = jnp.zeros(acc.shape, acc.dtype)
    for copy in copies:
        copy.wait()
    scale = D_HEAD**-0.5
    part = frames * TILE * SPAN * TOK
    piece = SPAN * TOK

    def group(index, _):
        row, col = index // cols, index % cols
        start = pl.multiple_of(jnp.clip(col - 2, 0, key_cols - SPAN) * TOK, TOK)
        here = pl.multiple_of(col * TOK, TOK)
        own = query_ref[:, :, row // 2, row % 2, pl.ds(here, TOK), :].reshape(-1, LANES)
        blank = jnp.zeros((own.shape[0], D_HEAD), own.dtype)
        pair = jnp.concatenate(
            [
                jnp.concatenate([own[:, :D_HEAD], blank], axis=1),
                jnp.concatenate([blank, own[:, D_HEAD:]], axis=1),
            ],
            axis=0,
        )
        top = None
        for near in range(3):
            keys = kv[row + near, :, :, pl.ds(start, piece), :].reshape(part, LANES)
            both = lax.dot_general(keys, pair, NT, preferred_element_type=jnp.float32)
            for frame in range(frames):
                first = (near * frames + frame) * SPAN
                bias = jnp.concatenate(
                    [
                        jnp.broadcast_to(bias_ref[index, first + c : first + c + 1, :], (TOK, D_HEAD))
                        for c in range(SPAN)
                    ],
                    axis=0,
                )
                for sub in range(TILE):
                    at = (frame * TILE + sub) * piece
                    score = both[at : at + piece, :D_HEAD] * (scale * LOG2_E) + bias
                    scores[near, at : at + piece, :D_HEAD] = score
                    scores[near, at : at + piece, D_HEAD:] = both[at : at + piece, D_HEAD:]
                    most = jnp.max(score.reshape(-1, 8, D_HEAD), axis=0)
                    top = most if top is None else jnp.maximum(top, most)
        top = jnp.max(top, axis=0, keepdims=True)
        total = jnp.zeros((8, D_HEAD), jnp.float32)
        delta = jnp.zeros((8, D_HEAD), jnp.float32)
        for near in range(3):
            for at in range(0, part, piece):
                prob = jnp.exp2(scores[near, at : at + piece, :D_HEAD] - top)
                scores[near, at : at + piece, :D_HEAD] = prob
                total = total + jnp.sum(prob.reshape(-1, 8, D_HEAD), axis=0)
                grad = prob * scores[near, at : at + piece, D_HEAD:]
                delta = delta + jnp.sum(grad.reshape(-1, 8, D_HEAD), axis=0)
        inverse = 1.0 / jnp.sum(total, axis=0, keepdims=True)
        delta = jnp.sum(delta, axis=0, keepdims=True) * inverse
        query_grad = None
        for near in range(3):
            for at in range(0, part, piece):
                weight = scores[near, at : at + piece, :D_HEAD] * inverse
                dscore = weight * (scores[near, at : at + piece, D_HEAD:] - delta)
                low[at : at + piece, :D_HEAD] = dscore.astype(jnp.bfloat16)
                low[at : at + piece, D_HEAD:] = weight.astype(jnp.bfloat16)
            added = lax.dot_general(low[...], pair, NN, preferred_element_type=jnp.float32)
            window = (row + near, slice(None), slice(None), pl.ds(start, piece), slice(None))
            acc[window] = acc[window] + added.reshape(frames, TILE, piece, LANES)
            keys = kv[row + near, :, :, pl.ds(start, piece), :].reshape(part, LANES)
            more = lax.dot_general(
                low[:, :D_HEAD], keys[:, :D_HEAD], TN, preferred_element_type=jnp.float32
            )
            query_grad = more if query_grad is None else query_grad + more
        dq_ref[:, :, row // 2, row % 2, pl.ds(here, TOK), :] = (
            (query_grad * scale).astype(jnp.bfloat16).reshape(frames, TILE, TOK, D_HEAD)
        )
        return 0

    lax.fori_loop(0, rows_own * cols, group, 0)
    lane = lax.broadcasted_iota(jnp.int32, (1, 1, 1, LANES), 3)
    factor = jnp.where(lane < D_HEAD, scale, 1.0)
    for row in range(rows_own):
        dkv_ref[:, :, row // 2, row % 2] = (acc[1 + row] * factor).astype(jnp.bfloat16)
    edge_ref[...] = acc[jnp.where(side == 0, rows_own, 1)] * factor
    halo_out_ref[...] = (acc[halo_slot] * factor).astype(jnp.bfloat16)


def window_bias(tile_valid, width_shift, side):
    frames, tile_rows, cols = tile_valid.shape
    row = (side * TH_DEV + jnp.arange(TH_DEV)).reshape(-1, 1, 1, 1, 1, 1)
    col = jnp.arange(cols).reshape(1, -1, 1, 1, 1, 1)
    near = jnp.arange(3).reshape(1, 1, -1, 1, 1, 1) - 1
    key_frame = jnp.arange(frames).reshape(1, 1, 1, -1, 1, 1)
    key_col = jnp.clip(col - 2, 0, cols - SPAN) + jnp.arange(SPAN).reshape(1, 1, 1, 1, -1, 1)
    frame = jnp.arange(frames).reshape(1, 1, 1, 1, 1, -1)
    shift_own = lax.dynamic_slice_in_dim(width_shift, side * TH_DEV, TH_DEV, 1)
    shift_own = shift_own.transpose(1, 2, 0).reshape(TH_DEV, cols, 1, 1, 1, frames)
    valid_near = lax.dynamic_slice_in_dim(
        jnp.pad(tile_valid, ((0, 0), (1, 1), (0, 0))), side * TH_DEV, TH_DEV + 2, 1
    )
    valid_rows = jnp.stack([valid_near[:, n : n + TH_DEV] for n in range(3)])
    starts = [min(max(c - 2, 0), cols - SPAN) for c in range(cols)]
    valid_cols = jnp.stack([valid_rows[:, :, :, s : s + SPAN] for s in starts])
    valid = valid_cols.transpose(3, 0, 1, 2, 4).reshape(TH_DEV, cols, 3, frames, SPAN, 1)
    own = (near == 0) & (key_frame == frame) & (key_col == col)
    inside = jnp.abs(key_col - col - shift_own) <= 1
    there = (row + near >= 0) & (row + near < tile_rows)
    bias = jnp.where(inside & there & ((valid == 1) | own), 0.0, MASKED_SCORE).astype(jnp.float32)
    bias = bias.reshape(TH_DEV * cols, 3 * frames * SPAN, frames, 1)
    bias = jnp.broadcast_to(bias, bias.shape[:3] + (TILE**3,))
    return bias.reshape(TH_DEV * cols, 3 * frames * SPAN, frames * TILE**3)


def head_shards(queries, key_states, value_states, out_grad, tile_valid, width_shift):
    frames, _, cols = tile_valid.shape
    group = ("tm", "seq")
    side = lax.axis_index("height")
    swap = [(0, 1), (1, 0)]
    span = cols * TOK

    def spread(first, second):
        moved = lax.all_to_all(split_heads(first, second), group, 0, 0, tiled=True)
        return moved.reshape(frames, TILE, 2, 2, span, LANES)

    kv = spread(key_states, value_states)
    edge = jnp.where(side == 0, kv[:, :, 1, 1], kv[:, :, 0, 0])
    halo = lax.ppermute(edge, "height", swap)
    query = spread(queries, out_grad)
    bias = window_bias(tile_valid, width_shift, side)
    part = frames * TILE * SPAN * TOK
    whole = pl.BlockSpec(memory_space=pltpu.VMEM)
    dq, dkv, edge_own, halo_grad = pl.pallas_call(
        grad_kernel,
        in_specs=[
            pl.BlockSpec(memory_space=pltpu.SMEM),
            whole,
            whole,
            pl.BlockSpec(memory_space=pl.ANY),
            pl.BlockSpec(memory_space=pl.ANY),
        ],
        out_specs=[whole] * 4,
        out_shape=[
            jax.ShapeDtypeStruct((frames, TILE, 2, 2, span, D_HEAD), jnp.bfloat16),
            jax.ShapeDtypeStruct((frames, TILE, 2, 2, span, LANES), jnp.bfloat16),
            jax.ShapeDtypeStruct((frames, TILE, span, LANES), jnp.float32),
            jax.ShapeDtypeStruct((frames, TILE, span, LANES), jnp.bfloat16),
        ],
        scratch_shapes=[
            pltpu.VMEM((TH_DEV + 2, frames, TILE, span, LANES), jnp.bfloat16),
            pltpu.VMEM((TH_DEV + 2, frames, TILE, span, LANES), jnp.float32),
            pltpu.VMEM((3, part, LANES), jnp.float32),
            pltpu.VMEM((part, LANES), jnp.bfloat16),
            pltpu.SemaphoreType.DMA((TH_DEV + 1,)),
        ],
        compiler_params=pltpu.CompilerParams(vmem_limit_bytes=VMEM_BYTES),
    )(side.reshape(1), bias, query, kv, halo)

    def gather(grads):
        lanes = grads.shape[-1]
        moved = grads.reshape(HEADS, 2 * span, lanes)
        return join_heads(lax.all_to_all(moved, group, 0, 0, tiled=True))

    received = lax.ppermute(halo_grad, "height", swap)
    (query_out,) = gather(dq)
    edge_sum = (edge_own + received.astype(jnp.float32)).astype(jnp.bfloat16)[:, :, None, None]
    dkv = lax.dynamic_update_slice(dkv, edge_sum, (0, 0, 1 - side, 1 - side, 0, 0))
    key_out, value_out = gather(dkv)
    return query_out, key_out, value_out


def solution(mesh):
    frames = mesh.shape["tm"]
    tall = mesh.shape["height"] == 2 and frames == 2 and mesh.shape["seq"] == 2 * TILE
    one_head = tall and frames * mesh.shape["seq"] == HEADS
    placed = (
        P(("tm", "height", "seq"), None),
        P(("tm", "height", "seq"), None),
        P(("tm", "height", "seq"), None),
        P(("tm", "height", "seq"), None),
        P(),
        P(),
    )
    return jax.shard_map(
        head_shards if one_head else shards,
        mesh=mesh,
        in_specs=placed,
        out_specs=(
            P(("tm", "height", "seq"), None),
            P(("tm", "height", "seq"), None),
            P(("tm", "height", "seq"), None),
        ),
        check_vma=False,
    )
```

```python
from functools import partial

import jax
import jax.numpy as jnp
from jax import lax
from jax.experimental import pallas as pl
from jax.experimental.pallas import tpu as pltpu
from jax.sharding import PartitionSpec as P

D_HEAD = 128
HEADS = 16
TILE = 4
TH_DEV = 4
TW = 16


MASKED_SCORE = -1e30


def passed_along(block, axis, distance):
    devices = range(lax.axis_size(axis))
    route = [((i - distance) % len(devices), i) for i in devices]
    return lax.ppermute(block, axis, route)


def with_halo(cells, sides, width):
    for axis, dim in sides:
        count = lax.axis_size(axis)
        ends = count - 1
        head = lax.slice_in_dim(cells, 0, width, axis=dim)
        tail = lax.slice_in_dim(cells, cells.shape[dim] - width, cells.shape[dim], axis=dim)
        cells = jnp.concatenate(
            [
                lax.ppermute(tail, axis, [(i, (i + 1) % count) for i in range(ends)]),
                cells,
                lax.ppermute(head, axis, [((i + 1) % count, i) for i in range(ends)]),
            ],
            axis=dim,
        )
    return cells


def shifted(value, axis, steps):
    count = lax.axis_size(axis)
    initial, last = (max(0, -steps), min(count, count - steps))
    return lax.ppermute(value, axis, [(source, source + steps) for source in range(initial, last)])


def to_tiles(grid_in, tile_edge):
    groups, frames, grid_rows, grid_cols = grid_in.shape[:4]
    trailing = grid_in.shape[4:]
    split_grid = grid_in.reshape(
        (
            groups,
            frames // tile_edge,
            tile_edge,
            grid_rows // tile_edge,
            tile_edge,
            grid_cols // tile_edge,
            tile_edge,
        )
        + trailing
    )
    axis_order = (0, 1, 3, 5, 2, 4, 6) + tuple(range(7, 7 + len(trailing)))
    return split_grid.transpose(axis_order).reshape(
        (groups, frames // tile_edge, grid_rows // tile_edge, grid_cols // tile_edge, tile_edge**3)
        + trailing
    )


def from_tiles(tiles_in, tile_edge):
    groups, frame_tiles, row_tiles, col_tiles = tiles_in.shape[:4]
    trailing = tiles_in.shape[5:]
    split_grid = tiles_in.reshape(
        (groups, frame_tiles, row_tiles, col_tiles, tile_edge, tile_edge, tile_edge) + trailing
    )
    axis_order = (0, 1, 4, 2, 5, 3, 6) + tuple(range(7, 7 + len(trailing)))
    return split_grid.transpose(axis_order).reshape(
        (groups, frame_tiles * tile_edge, row_tiles * tile_edge, col_tiles * tile_edge) + trailing
    )


def edge_tiles(piece_own, half_index):
    return jnp.where(half_index == 0, piece_own[:, :, :, -2:], piece_own[:, :, :, :2])


def widen_rim(piece_own, received, half_index):
    left_side = jnp.concatenate([piece_own, received], axis=3)
    right_side = jnp.concatenate([received, piece_own], axis=3)
    return jnp.where(half_index == 0, left_side, right_side)


def shards(queries, key_states, value_states, out_grad, tile_valid, width_shift):
    seq_count = lax.axis_size("seq")
    groups = 2 * HEADS // seq_count
    half_width = TW * TILE // 2
    lines_dev = queries.shape[0] // (TW * TILE)
    tiles_half = TW // 2
    tile_cells = TILE**3
    score_scale = D_HEAD ** (-0.5)
    time_index = lax.axis_index("tm")
    height_index = lax.axis_index("height")
    half_index = lax.axis_index("seq") * groups // HEADS
    anchor = half_index * (tiles_half - 2)

    def to_heads(rows_in):
        split_rows = rows_in.reshape(lines_dev, 2, half_width, HEADS, D_HEAD)
        return split_rows.transpose(1, 3, 0, 2, 4).reshape(2 * HEADS, lines_dev, half_width, D_HEAD)

    moved = (
        lax.all_to_all(to_heads(queries), "seq", split_axis=0, concat_axis=1, tiled=True),
        lax.all_to_all(to_heads(key_states), "seq", split_axis=0, concat_axis=1, tiled=True),
        lax.all_to_all(to_heads(value_states), "seq", split_axis=0, concat_axis=1, tiled=True),
        lax.all_to_all(to_heads(out_grad), "seq", split_axis=0, concat_axis=1, tiled=True),
    )

    def own_tiles(grid_part):
        return to_tiles(grid_part.reshape(groups, TILE, TILE * TH_DEV, half_width, D_HEAD), TILE)

    query_own, keys_own, values_own, grads_own = [own_tiles(grid_part) for grid_part in moved]
    key_edges = passed_along(
        (edge_tiles(keys_own, half_index), edge_tiles(values_own, half_index)),
        "seq",
        seq_count // 2,
    )
    keys_wide = widen_rim(keys_own, key_edges[0], half_index)
    values_wide = widen_rim(values_own, key_edges[1], half_index)
    keys_ext, values_ext = (
        with_halo(keys_wide, (("tm", 1), ("height", 2)), 1),
        with_halo(values_wide, (("tm", 1), ("height", 2)), 1),
    )
    table_start = (time_index, height_index * TH_DEV, anchor)
    table_span = (3, TH_DEV + 2, tiles_half + 2)
    table_pad = ((1, 1), (1, 1), (0, 0))
    valid_ext = lax.dynamic_slice(jnp.pad(tile_valid, table_pad), table_start, table_span)
    shift_ext = lax.dynamic_slice(jnp.pad(width_shift, table_pad), table_start, table_span)
    triple = jnp.arange(3)
    query_cols = jnp.arange(tiles_half) + 2 * half_index

    def query_row(keep_grads, carry, row_index):
        query_tiles = lax.dynamic_index_in_dim(query_own[:, 0], row_index, 1, keepdims=False)
        grad_tiles = lax.dynamic_index_in_dim(grads_own[:, 0], row_index, 1, keepdims=False)
        key_rows = lax.dynamic_slice_in_dim(keys_ext, row_index, 3, 2)
        value_rows = lax.dynamic_slice_in_dim(values_ext, row_index, 3, 2)
        shift_row = lax.dynamic_index_in_dim(shift_ext[1], row_index + 1, 0, keepdims=False)
        starts = query_cols + lax.dynamic_slice_in_dim(shift_row, 2 * half_index, tiles_half) - 1
        window_cols = starts[:, None] + triple[None, :]
        key_win = key_rows[:, :, :, window_cols].transpose(0, 3, 1, 2, 4, 5, 6)
        key_win = key_win.reshape(groups, tiles_half, 27 * tile_cells, D_HEAD)
        value_win = value_rows[:, :, :, window_cols].transpose(0, 3, 1, 2, 4, 5, 6)
        value_win = value_win.reshape(groups, tiles_half, 27 * tile_cells, D_HEAD)
        valid_rows = lax.dynamic_slice_in_dim(valid_ext, row_index, 3, 1)[:, :, window_cols]
        own_tile = (
            (triple[:, None, None, None] == 1)
            & (triple[None, :, None, None] == 1)
            & (window_cols[None, None] == query_cols[None, None, :, None])
        )
        allowed = ((valid_rows == 1) | own_tile).transpose(2, 0, 1, 3)
        tile_bias = jnp.where(allowed.reshape(tiles_half, 27, 1), 0.0, MASKED_SCORE).astype(
            jnp.float32
        )
        mask_bias = jnp.broadcast_to(tile_bias, (tiles_half, 27, tile_cells)).reshape(
            1, tiles_half, 1, 27 * tile_cells
        )
        scores = (
            score_scale
            * jnp.einsum(
                "gwid,gwjd->gwij", query_tiles, key_win, preferred_element_type=jnp.float32
            )
            + mask_bias
        )
        row_max = jnp.max(scores, axis=-1, keepdims=True)
        probs = jnp.exp(scores - row_max)
        exp_total = jnp.sum(probs, axis=-1, keepdims=True)
        log_total = row_max + jnp.log(exp_total)
        weights = probs / exp_total
        grad_weights = jnp.einsum(
            "gwid,gwjd->gwij", grad_tiles, value_win, preferred_element_type=jnp.float32
        )
        delta_row = jnp.sum(weights * grad_weights, axis=-1, keepdims=True)
        dscore = (weights * (grad_weights - delta_row)).astype(jnp.bfloat16)
        query_part = score_scale * jnp.einsum(
            "gwij,gwjd->gwid", dscore, key_win, preferred_element_type=jnp.float32
        )
        key_acc, value_acc = carry
        key_part = score_scale * jnp.einsum(
            "gwij,gwid->gwjd", dscore, query_tiles, preferred_element_type=jnp.float32
        )
        value_part = jnp.einsum(
            "gwij,gwid->gwjd",
            weights.astype(jnp.bfloat16),
            grad_tiles,
            preferred_element_type=jnp.float32,
        )
        time_pick = triple[None, :, None, None]
        row_pick = triple[None, None, :, None]
        col_pick = window_cols[:, None, None, :]

        def spread(acc_grid, part_grad):
            shaped = part_grad.reshape(groups, tiles_half, 3, 3, 3, tile_cells, D_HEAD)
            rows_now = lax.dynamic_slice_in_dim(acc_grid, row_index, 3, 2)
            rows_now = rows_now.at[:, time_pick, row_pick, col_pick].add(shaped)
            return lax.dynamic_update_slice_in_dim(acc_grid, rows_now, row_index, 2)

        carry = (spread(key_acc, key_part), spread(value_acc, value_part))
        return (carry, (query_part, log_total[..., 0], delta_row[..., 0]))

    zero_grads = jnp.zeros(keys_ext.shape, jnp.float32)
    (key_acc, value_acc), row_outputs = lax.scan(
        partial(query_row, True), (zero_grads, zero_grads), jnp.arange(TH_DEV)
    )
    from_below = (
        shifted(key_acc[:, :, -1:].astype(jnp.bfloat16), "height", 1).astype(jnp.float32),
        shifted(value_acc[:, :, -1:].astype(jnp.bfloat16), "height", 1).astype(jnp.float32),
    )
    from_above = (
        shifted(key_acc[:, :, :1].astype(jnp.bfloat16), "height", -1).astype(jnp.float32),
        shifted(value_acc[:, :, :1].astype(jnp.bfloat16), "height", -1).astype(jnp.float32),
    )

    def fold_rows(acc_grid, lower_in, upper_in):
        acc_grid = acc_grid.at[:, :, 1:2].add(lower_in)
        acc_grid = acc_grid.at[:, :, TH_DEV : TH_DEV + 1].add(upper_in)
        return acc_grid[:, :, 1 : TH_DEV + 1]

    key_core = fold_rows(key_acc, from_below[0], from_above[0])
    value_core = fold_rows(value_acc, from_below[1], from_above[1])
    from_before = shifted((key_core[:, 2:3], value_core[:, 2:3]), "tm", 1)
    from_after = shifted((key_core[:, 0:1], value_core[:, 0:1]), "tm", -1)
    key_mid = key_core[:, 1] + from_before[0][:, 0] + from_after[0][:, 0]
    value_mid = value_core[:, 1] + from_before[1][:, 0] + from_after[1][:, 0]

    def rim_of(mid_grid):
        return jnp.where(half_index == 0, mid_grid[:, :, -2:], mid_grid[:, :, :2])

    rim_back = (
        passed_along(rim_of(key_mid).astype(jnp.bfloat16), "seq", seq_count // 2).astype(
            jnp.float32
        ),
        passed_along(rim_of(value_mid).astype(jnp.bfloat16), "seq", seq_count // 2).astype(
            jnp.float32
        ),
    )

    def settle(mid_grid, received):
        left_side = jnp.concatenate(
            [
                mid_grid[:, :, : tiles_half - 2],
                mid_grid[:, :, tiles_half - 2 : tiles_half] + received,
            ],
            axis=2,
        )
        right_side = jnp.concatenate([mid_grid[:, :, 2:4] + received, mid_grid[:, :, 4:]], axis=2)
        return jnp.where(half_index == 0, left_side, right_side)

    key_grid = from_tiles(settle(key_mid, rim_back[0])[:, None], TILE).astype(jnp.bfloat16)
    value_grid = from_tiles(settle(value_mid, rim_back[1])[:, None], TILE).astype(jnp.bfloat16)
    query_grid = from_tiles(jnp.moveaxis(row_outputs[0], 0, 1)[:, None], TILE).astype(jnp.bfloat16)

    def to_lines(grid_part):
        return grid_part.reshape(groups, TILE * TILE * TH_DEV, half_width, D_HEAD)

    returned = (
        lax.all_to_all(to_lines(query_grid), "seq", split_axis=1, concat_axis=0, tiled=True),
        lax.all_to_all(to_lines(key_grid), "seq", split_axis=1, concat_axis=0, tiled=True),
        lax.all_to_all(to_lines(value_grid), "seq", split_axis=1, concat_axis=0, tiled=True),
    )

    def to_rows(grid_part):
        split_rows = grid_part.reshape(2, HEADS, lines_dev, half_width, D_HEAD)
        return split_rows.transpose(2, 0, 3, 1, 4).reshape(
            lines_dev * 2 * half_width, HEADS * D_HEAD
        )

    return (to_rows(returned[0]), to_rows(returned[1]), to_rows(returned[2]))


TOK = TILE * TILE
SPAN = 5
LANES = 2 * D_HEAD
LINES = TW * TOK
LOG2_E = 1.4426950408889634
VMEM_BYTES = 56 * 1024 * 1024
NT = (((1,), (1,)), ((), ()))
NN = (((1,), (0,)), ((), ()))
TN = (((0,), (0,)), ((), ()))
ANYWHERE = pl.BlockSpec(memory_space=pl.ANY)
SCALARS = pl.BlockSpec(memory_space=pltpu.SMEM)
WHOLE = pl.BlockSpec(memory_space=pltpu.VMEM)
PARAMS = pltpu.CompilerParams(vmem_limit_bytes=VMEM_BYTES)


def row_order(inverse):
    target = lax.broadcasted_iota(jnp.int32, (LINES, LINES), 0)
    source = lax.broadcasted_iota(jnp.int32, (LINES, LINES), 1)
    if inverse:
        target, source = source, target
    col, line, x = target // TOK, (target // TILE) % TILE, target % TILE
    return (source == line * (TW * TILE) + col * TILE + x).astype(jnp.bfloat16)


def split_kernel(places, turn, place_ref, *refs):
    arrays, outs = refs[:4], refs[4 : 4 + places]
    taken, ready, in_sem, out_sem = refs[4 + places :]
    turns = HEADS // places
    loads = []
    for k in range(places):
        first = pl.multiple_of(((place_ref[0] ^ k) * turns + turn) * D_HEAD, D_HEAD)
        loads.append(
            [
                pltpu.make_async_copy(
                    ref.at[:, pl.ds(first, D_HEAD)], taken.at[k, which], in_sem.at[k, which]
                )
                for which, ref in enumerate(arrays)
            ]
        )
        for copy in loads[k]:
            copy.start()
    order = row_order(False)
    stores = []
    for k in range(places):
        for copy in loads[k]:
            copy.wait()
        for pair in range(2):
            for row in range(2):
                lines = slice(row * LINES, (row + 1) * LINES)
                rows = jnp.concatenate(
                    [taken[k, 2 * pair, lines, :], taken[k, 2 * pair + 1, lines, :]], axis=1
                )
                moved = lax.dot_general(order, rows, NN, preferred_element_type=jnp.float32)
                ready[k, pair, row] = moved.astype(jnp.bfloat16)
        stores.append(pltpu.make_async_copy(ready.at[k], outs[k], out_sem.at[k]))
        stores[k].start()
    for copy in stores:
        copy.wait()


def split_heads(places, turn, place, arrays):
    rows = arrays[0].shape[0]
    return pl.pallas_call(
        lambda *refs: split_kernel(places, turn, *refs),
        in_specs=[SCALARS] + [ANYWHERE] * 4,
        out_specs=[ANYWHERE] * places,
        out_shape=[jax.ShapeDtypeStruct((2, 2, LINES, LANES), jnp.bfloat16)] * places,
        scratch_shapes=[
            pltpu.VMEM((places, 4, rows, D_HEAD), jnp.bfloat16),
            pltpu.VMEM((places, 2, 2, LINES, LANES), jnp.bfloat16),
            pltpu.SemaphoreType.DMA((places, 4)),
            pltpu.SemaphoreType.DMA((places,)),
        ],
        compiler_params=PARAMS,
    )(place, *arrays)


def join_kernel(places, turn, widths, kept, place_ref, *refs):
    count = len(widths)
    groups = [refs[n * places : (n + 1) * places] for n in range(count)]
    refs = refs[count * places + kept :]
    outs, taken, (ready, in_sem, out_sem) = refs[:3], refs[3 : 3 + count], refs[3 + count :]
    turns = HEADS // places
    loads = []
    for k in range(places):
        loads.append(
            [
                pltpu.make_async_copy(groups[n][k], taken[n].at[k], in_sem.at[k, n])
                for n in range(count)
            ]
        )
        for copy in loads[k]:
            copy.start()
    order = row_order(True)
    stores = []
    for k in range(places):
        for copy in loads[k]:
            copy.wait()
        for row in range(2):
            which = 0
            for n in range(count):
                back = lax.dot_general(
                    order, taken[n][k, row], NN, preferred_element_type=jnp.float32
                ).astype(jnp.bfloat16)
                for lane in range(0, widths[n], D_HEAD):
                    ready[k, which, row * LINES : (row + 1) * LINES, :] = back[
                        :, lane : lane + D_HEAD
                    ]
                    which += 1
        first = pl.multiple_of(((place_ref[0] ^ k) * turns + turn) * D_HEAD, D_HEAD)
        for which in range(3):
            copy = pltpu.make_async_copy(
                ready.at[k, which], outs[which].at[:, pl.ds(first, D_HEAD)], out_sem.at[k, which]
            )
            copy.start()
            stores.append(copy)
    for copy in stores:
        copy.wait()


def join_heads(places, turn, place, groups, earlier):
    rows = 2 * LINES
    widths = [group[0].shape[-1] for group in groups]
    count = len(widths)
    return pl.pallas_call(
        lambda *refs: join_kernel(places, turn, widths, len(earlier), *refs),
        in_specs=[SCALARS] + [ANYWHERE] * (count * places + len(earlier)),
        out_specs=[ANYWHERE] * 3,
        out_shape=[jax.ShapeDtypeStruct((rows, HEADS * D_HEAD), jnp.bfloat16)] * 3,
        scratch_shapes=[pltpu.VMEM((places, 2, LINES, width), jnp.bfloat16) for width in widths]
        + [
            pltpu.VMEM((places, 3, rows, D_HEAD), jnp.bfloat16),
            pltpu.SemaphoreType.DMA((places, count)),
            pltpu.SemaphoreType.DMA((places, 3)),
        ],
        input_output_aliases={1 + count * places + n: n for n in range(len(earlier))},
        compiler_params=PARAMS,
    )(place, *[block for group in groups for block in group], *earlier)


def edge_kernel(places, *refs):
    blocks, (first_ref, last_ref), sem = refs[:places], refs[places : places + 2], refs[-1]
    copies = []
    for k in range(places):
        for row, ref in enumerate((first_ref, last_ref)):
            copies.append(pltpu.make_async_copy(blocks[k].at[0, row], ref.at[k], sem.at[k, row]))
    for copy in copies:
        copy.start()
    for copy in copies:
        copy.wait()


def edge_rows(places, blocks):
    return pl.pallas_call(
        lambda *refs: edge_kernel(places, *refs),
        in_specs=[ANYWHERE] * places,
        out_specs=[WHOLE] * 2,
        out_shape=[jax.ShapeDtypeStruct((places, LINES, LANES), jnp.bfloat16)] * 2,
        scratch_shapes=[pltpu.SemaphoreType.DMA((places, 2))],
        compiler_params=PARAMS,
    )(*blocks)


def grad_kernel(places, place_ref, bias_ref, *refs):
    blocks, (from_above, from_below) = refs[:places], refs[places : places + 2]
    outs = refs[places + 2 :]
    dq_refs, acc_out, above_ref, below_ref = outs[:places], *outs[places : places + 3]
    kv, own_rows, acc, dq, scores, low, in_sem, halo_sem, out_sem = outs[places + 3 :]
    frames = places // TILE
    scale = D_HEAD**-0.5
    copies = []
    for k in range(places):
        seat = place_ref[0] ^ k
        spot = (seat // TILE, seat % TILE)
        copies += [
            pltpu.make_async_copy(blocks[k].at[0], kv.at[pl.ds(1, 2), *spot], in_sem.at[k, 0]),
            pltpu.make_async_copy(blocks[k].at[1], own_rows.at[:, *spot], in_sem.at[k, 1]),
            pltpu.make_async_copy(from_above.at[k], kv.at[0, *spot], halo_sem.at[k, 0]),
            pltpu.make_async_copy(from_below.at[k], kv.at[3, *spot], halo_sem.at[k, 1]),
        ]
    for copy in copies:
        copy.start()
    acc[...] = jnp.zeros(acc.shape, acc.dtype)
    for copy in copies:
        copy.wait()
    part = places * SPAN * TOK
    piece = SPAN * TOK

    def group(col, _):
        start = pl.multiple_of(jnp.clip(col - 2, 0, TW - SPAN) * TOK, TOK)
        here = pl.multiple_of(col * TOK, TOK)
        window = pl.ds(start, piece)
        pairs, tops = [], []
        for row in range(2):
            own = own_rows[row, :, :, pl.ds(here, TOK), :].reshape(-1, LANES)
            blank = jnp.zeros((own.shape[0], D_HEAD), own.dtype)
            pair = jnp.concatenate(
                [
                    jnp.concatenate([own[:, :D_HEAD], blank], axis=1),
                    jnp.concatenate([blank, own[:, D_HEAD:]], axis=1),
                ],
                axis=0,
            )
            pairs.append(pair)
            top = None
            for near in range(3):
                keys = kv[row + near, :, :, window, :].reshape(part, LANES)
                both = lax.dot_general(keys, pair, NT, preferred_element_type=jnp.float32)
                for frame in range(frames):
                    first = (near * frames + frame) * SPAN
                    bias = jnp.concatenate(
                        [
                            jnp.broadcast_to(
                                bias_ref[row, col, first + c : first + c + 1, :], (TOK, D_HEAD)
                            )
                            for c in range(SPAN)
                        ],
                        axis=0,
                    )
                    for sub in range(TILE):
                        at = (frame * TILE + sub) * piece
                        score = both[at : at + piece, :D_HEAD] * (scale * LOG2_E) + bias
                        scores[row, near, at : at + piece, :D_HEAD] = score
                        scores[row, near, at : at + piece, D_HEAD:] = both[at : at + piece, D_HEAD:]
                        most = jnp.max(score.reshape(-1, 8, D_HEAD), axis=0)
                        top = most if top is None else jnp.maximum(top, most)
            tops.append(jnp.max(top, axis=0, keepdims=True))
        sums = []
        for row in range(2):
            total = jnp.zeros((8, D_HEAD), jnp.float32)
            delta = jnp.zeros((8, D_HEAD), jnp.float32)
            for near in range(3):
                for at in range(0, part, piece):
                    prob = jnp.exp2(scores[row, near, at : at + piece, :D_HEAD] - tops[row])
                    scores[row, near, at : at + piece, :D_HEAD] = prob
                    total = total + jnp.sum(prob.reshape(-1, 8, D_HEAD), axis=0)
                    grad = prob * scores[row, near, at : at + piece, D_HEAD:]
                    delta = delta + jnp.sum(grad.reshape(-1, 8, D_HEAD), axis=0)
            inverse = 1.0 / jnp.sum(total, axis=0, keepdims=True)
            sums.append((inverse, jnp.sum(delta, axis=0, keepdims=True) * inverse))
        for row in range(2):
            inverse, delta = sums[row]
            query_grad = None
            for near in range(3):
                for at in range(0, part, piece):
                    weight = scores[row, near, at : at + piece, :D_HEAD] * inverse
                    dscore = weight * (scores[row, near, at : at + piece, D_HEAD:] - delta)
                    low[row, near, at : at + piece, :D_HEAD] = dscore.astype(jnp.bfloat16)
                    low[row, near, at : at + piece, D_HEAD:] = weight.astype(jnp.bfloat16)
                added = lax.dot_general(
                    low[row, near], pairs[row], NN, preferred_element_type=jnp.float32
                )
                spot = (row + near, slice(None), slice(None), window, slice(None))
                acc[spot] = acc[spot] + added.reshape(frames, TILE, piece, LANES)
                keys = kv[row + near, :, :, window, :D_HEAD].reshape(part, D_HEAD)
                more = lax.dot_general(
                    low[row, near, :, :D_HEAD], keys, TN, preferred_element_type=jnp.float32
                )
                query_grad = more if query_grad is None else query_grad + more
            dq[row, :, :, pl.ds(here, TOK), :] = (
                (query_grad * scale).astype(jnp.bfloat16).reshape(frames, TILE, TOK, D_HEAD)
            )
        return 0

    lax.fori_loop(0, TW, group, 0)
    copies = []
    for k in range(places):
        seat = place_ref[0] ^ k
        spot = (seat // TILE, seat % TILE)
        copies += [
            pltpu.make_async_copy(dq.at[:, *spot], dq_refs[k], out_sem.at[k, 0]),
            pltpu.make_async_copy(acc.at[pl.ds(1, 2), *spot], acc_out.at[k], out_sem.at[k, 1]),
        ]
    for copy in copies:
        copy.start()
    for k in range(places):
        seat = place_ref[0] ^ k
        spot = (seat // TILE, seat % TILE)
        above_ref[k] = acc[0, *spot].astype(jnp.bfloat16)
        below_ref[k] = acc[3, *spot].astype(jnp.bfloat16)
    for copy in copies:
        copy.wait()


def head_grads(places, place, bias, blocks, from_above, from_below):
    frames = places // TILE
    part = places * SPAN * TOK
    results = pl.pallas_call(
        lambda *refs: grad_kernel(places, *refs),
        in_specs=[SCALARS, WHOLE] + [ANYWHERE] * (places + 2),
        out_specs=[ANYWHERE] * (places + 1) + [WHOLE] * 2,
        out_shape=[jax.ShapeDtypeStruct((2, LINES, D_HEAD), jnp.bfloat16)] * places
        + [jax.ShapeDtypeStruct((places, 2, LINES, LANES), jnp.float32)]
        + [jax.ShapeDtypeStruct((places, LINES, LANES), jnp.bfloat16)] * 2,
        scratch_shapes=[
            pltpu.VMEM((4, frames, TILE, LINES, LANES), jnp.bfloat16),
            pltpu.VMEM((2, frames, TILE, LINES, LANES), jnp.bfloat16),
            pltpu.VMEM((4, frames, TILE, LINES, LANES), jnp.float32),
            pltpu.VMEM((2, frames, TILE, LINES, D_HEAD), jnp.bfloat16),
            pltpu.VMEM((2, 3, part, LANES), jnp.float32),
            pltpu.VMEM((2, 3, part, LANES), jnp.bfloat16),
            pltpu.SemaphoreType.DMA((places, 2)),
            pltpu.SemaphoreType.DMA((places, 2)),
            pltpu.SemaphoreType.DMA((places, 2)),
        ],
        compiler_params=PARAMS,
        cost_estimate=pl.CostEstimate(
            flops=60_000_000_000, bytes_accessed=0, transcendentals=0
        ),
    )(place, bias, *blocks, from_above, from_below)
    return results[:places], *results[places:]


def finish_kernel(places, acc_ref, above_ref, below_ref, *refs):
    with_query = len(refs) > places
    outs = refs[-places:]
    lane = lax.broadcasted_iota(jnp.int32, (1, LANES), 1)
    factor = jnp.where(lane < D_HEAD, D_HEAD**-0.5, 1.0)
    for k in range(places):
        for row, ref in enumerate((above_ref, below_ref)):
            total = acc_ref[k, row] + ref[k].astype(jnp.float32)
            outs[k][row, :, :LANES] = (total * factor).astype(jnp.bfloat16)
        if with_query:
            outs[k][:, :, LANES:] = refs[k][...]


def finish_pairs(places, acc, above, below, query=()):
    lanes = LANES + (D_HEAD if query else 0)
    return pl.pallas_call(
        lambda *refs: finish_kernel(places, *refs),
        in_specs=[WHOLE] * (3 + len(query)),
        out_specs=[WHOLE] * places,
        out_shape=[jax.ShapeDtypeStruct((2, LINES, lanes), jnp.bfloat16)] * places,
        compiler_params=PARAMS,
    )(acc, above, below, *query)


def window_bias(tile_valid, width_shift, first_row):
    frames, tile_rows, cols = tile_valid.shape
    row = (first_row + jnp.arange(2)).reshape(-1, 1, 1, 1, 1, 1)
    col = jnp.arange(cols).reshape(1, -1, 1, 1, 1, 1)
    near = jnp.arange(3).reshape(1, 1, -1, 1, 1, 1) - 1
    key_frame = jnp.arange(frames).reshape(1, 1, 1, -1, 1, 1)
    key_col = jnp.clip(col - 2, 0, cols - SPAN) + jnp.arange(SPAN).reshape(1, 1, 1, 1, -1, 1)
    frame = jnp.arange(frames).reshape(1, 1, 1, 1, 1, -1)
    shift_own = lax.dynamic_slice_in_dim(width_shift, first_row, 2, 1)
    shift_own = shift_own.transpose(1, 2, 0).reshape(2, cols, 1, 1, 1, frames)
    valid_near = lax.dynamic_slice_in_dim(
        jnp.pad(tile_valid, ((0, 0), (1, 1), (0, 0))), first_row, 4, 1
    )
    valid_rows = jnp.stack([valid_near[:, n : n + 2] for n in range(3)])
    starts = [min(max(c - 2, 0), cols - SPAN) for c in range(cols)]
    valid_cols = jnp.stack([valid_rows[:, :, :, s : s + SPAN] for s in starts])
    valid = valid_cols.transpose(3, 0, 1, 2, 4).reshape(2, cols, 3, frames, SPAN, 1)
    own = (near == 0) & (key_frame == frame) & (key_col == col)
    inside = jnp.abs(key_col - col - shift_own) <= 1
    there = (row + near >= 0) & (row + near < tile_rows)
    bias = jnp.where(inside & there & ((valid == 1) | own), 0.0, MASKED_SCORE).astype(jnp.float32)
    bias = bias.reshape(2, cols, 3 * frames * SPAN, frames, 1)
    bias = jnp.broadcast_to(bias, bias.shape[:4] + (TILE**3,))
    return bias.reshape(2, cols, 3 * frames * SPAN, frames * TILE**3)


def place_shards(queries, key_states, value_states, out_grad, tile_valid, width_shift):
    frames = tile_valid.shape[0]
    places = frames * TILE
    turns = HEADS // places
    seq_count = lax.axis_size("seq")
    heights = lax.axis_size("height")
    seq_index = lax.axis_index("seq")
    place = (lax.axis_index("tm") * TILE + seq_index // 2).reshape(1)
    first_row = lax.axis_index("height") * TH_DEV + seq_index % 2 * 2
    bias = window_bias(tile_valid, width_shift, first_row)
    chain = [
        [h * seq_count + frame * 2 + half for h in range(heights) for half in range(2)]
        for frame in range(TILE)
    ]
    down = [pair for line in chain for pair in zip(line[:-1], line[1:])]
    up = [(b, a) for a, b in down]

    def send(block, k):
        return lax.ppermute(block, ("tm", "seq"), [(i, i ^ (2 * k)) for i in range(2 * places)])

    def step(block, route):
        return lax.ppermute(block, ("height", "seq"), route)

    def exchange(blocks, order):
        moved = dict(enumerate(blocks))
        for k in order:
            moved[k] = send(blocks[k], k)
        return [moved[k] for k in range(places)]

    natural = list(range(1, places))
    far, near = [k for k in natural if k & 2], [k for k in natural if not k & 2]
    held = [far[-1], near[0]]
    mixed = far[:-1] + near[1:] + held

    def after(blocks, results):
        kept, results = lax.optimization_barrier(([blocks[k] for k in held], results))
        blocks = list(blocks)
        for k, block in zip(held, kept):
            blocks[k] = block
        return blocks, results

    def ordered(first, then):
        return lax.optimization_barrier((first, then))

    def ordered(first, then):
        return lax.optimization_barrier((first, then))

    arrays = (key_states, value_states, queries, out_grad)
    outs = ()
    blocks = exchange(split_heads(places, 0, place, arrays), natural)
    leaving = None
    for turn in range(turns):
        more = turn + 1 < turns
        if more:
            coming = split_heads(places, turn + 1, place, arrays)
            blocks[1:6], coming = ordered(blocks[1:6], coming)
        first, last = edge_rows(places, blocks)
        grads = head_grads(places, place, bias, blocks, step(last, down), step(first, up))
        if leaving is not None:
            leaving, grads = after(leaving, grads)
            left = exchange(leaving, mixed)
            passed, grads = ordered([left[k] for k in mixed[:-2]], grads)
            for k, block in zip(mixed, passed):
                left[k] = block
            outs = join_heads(places, turn - 1, place, [left], outs)
        if more:
            coming, grads = after(coming, grads)
            blocks = exchange(coming, mixed)
        dq, acc, above, below = grads
        leaving = finish_pairs(places, acc, step(below, down), step(above, up), dq)
    outs = join_heads(places, turns - 1, place, [exchange(leaving, natural)], outs)
    key_out, value_out, query_out = outs
    return query_out, key_out, value_out


def solution(mesh):
    frames, seq_count = mesh.shape["tm"], mesh.shape["seq"]
    by_place = frames == 2 and seq_count == 2 * TILE
    placed = (
        P(("tm", "height", "seq"), None),
        P(("tm", "height", "seq"), None),
        P(("tm", "height", "seq"), None),
        P(("tm", "height", "seq"), None),
        P(),
        P(),
    )
    return jax.shard_map(
        place_shards if by_place else shards,
        mesh=mesh,
        in_specs=placed,
        out_specs=(
            P(("tm", "height", "seq"), None),
            P(("tm", "height", "seq"), None),
            P(("tm", "height", "seq"), None),
        ),
        check_vma=False,
    )
```

```python
from functools import partial

import jax
import jax.numpy as jnp
from jax import lax
from jax.experimental import pallas as pl
from jax.experimental.pallas import tpu as pltpu
from jax.sharding import PartitionSpec as P

D_HEAD = 128
HEADS = 16
TILE = 4
TH_DEV = 4
TW = 16


MASKED_SCORE = -1e30


def passed_along(block, axis, distance):
    devices = range(lax.axis_size(axis))
    route = [((i - distance) % len(devices), i) for i in devices]
    return lax.ppermute(block, axis, route)


def with_halo(cells, sides, width):
    for axis, dim in sides:
        count = lax.axis_size(axis)
        ends = count - 1
        head = lax.slice_in_dim(cells, 0, width, axis=dim)
        tail = lax.slice_in_dim(cells, cells.shape[dim] - width, cells.shape[dim], axis=dim)
        cells = jnp.concatenate(
            [
                lax.ppermute(tail, axis, [(i, (i + 1) % count) for i in range(ends)]),
                cells,
                lax.ppermute(head, axis, [((i + 1) % count, i) for i in range(ends)]),
            ],
            axis=dim,
        )
    return cells


def shifted(value, axis, steps):
    count = lax.axis_size(axis)
    initial, last = (max(0, -steps), min(count, count - steps))
    return lax.ppermute(value, axis, [(source, source + steps) for source in range(initial, last)])


def to_tiles(grid_in, tile_edge):
    groups, frames, grid_rows, grid_cols = grid_in.shape[:4]
    trailing = grid_in.shape[4:]
    split_grid = grid_in.reshape(
        (
            groups,
            frames // tile_edge,
            tile_edge,
            grid_rows // tile_edge,
            tile_edge,
            grid_cols // tile_edge,
            tile_edge,
        )
        + trailing
    )
    axis_order = (0, 1, 3, 5, 2, 4, 6) + tuple(range(7, 7 + len(trailing)))
    return split_grid.transpose(axis_order).reshape(
        (groups, frames // tile_edge, grid_rows // tile_edge, grid_cols // tile_edge, tile_edge**3)
        + trailing
    )


def from_tiles(tiles_in, tile_edge):
    groups, frame_tiles, row_tiles, col_tiles = tiles_in.shape[:4]
    trailing = tiles_in.shape[5:]
    split_grid = tiles_in.reshape(
        (groups, frame_tiles, row_tiles, col_tiles, tile_edge, tile_edge, tile_edge) + trailing
    )
    axis_order = (0, 1, 4, 2, 5, 3, 6) + tuple(range(7, 7 + len(trailing)))
    return split_grid.transpose(axis_order).reshape(
        (groups, frame_tiles * tile_edge, row_tiles * tile_edge, col_tiles * tile_edge) + trailing
    )


def edge_tiles(piece_own, half_index):
    return jnp.where(half_index == 0, piece_own[:, :, :, -2:], piece_own[:, :, :, :2])


def widen_rim(piece_own, received, half_index):
    left_side = jnp.concatenate([piece_own, received], axis=3)
    right_side = jnp.concatenate([received, piece_own], axis=3)
    return jnp.where(half_index == 0, left_side, right_side)


def shards(queries, key_states, value_states, out_grad, tile_valid, width_shift):
    seq_count = lax.axis_size("seq")
    groups = 2 * HEADS // seq_count
    half_width = TW * TILE // 2
    lines_dev = queries.shape[0] // (TW * TILE)
    tiles_half = TW // 2
    tile_cells = TILE**3
    score_scale = D_HEAD ** (-0.5)
    time_index = lax.axis_index("tm")
    height_index = lax.axis_index("height")
    half_index = lax.axis_index("seq") * groups // HEADS
    anchor = half_index * (tiles_half - 2)

    def to_heads(rows_in):
        split_rows = rows_in.reshape(lines_dev, 2, half_width, HEADS, D_HEAD)
        return split_rows.transpose(1, 3, 0, 2, 4).reshape(2 * HEADS, lines_dev, half_width, D_HEAD)

    moved = (
        lax.all_to_all(to_heads(queries), "seq", split_axis=0, concat_axis=1, tiled=True),
        lax.all_to_all(to_heads(key_states), "seq", split_axis=0, concat_axis=1, tiled=True),
        lax.all_to_all(to_heads(value_states), "seq", split_axis=0, concat_axis=1, tiled=True),
        lax.all_to_all(to_heads(out_grad), "seq", split_axis=0, concat_axis=1, tiled=True),
    )

    def own_tiles(grid_part):
        return to_tiles(grid_part.reshape(groups, TILE, TILE * TH_DEV, half_width, D_HEAD), TILE)

    query_own, keys_own, values_own, grads_own = [own_tiles(grid_part) for grid_part in moved]
    key_edges = passed_along(
        (edge_tiles(keys_own, half_index), edge_tiles(values_own, half_index)),
        "seq",
        seq_count // 2,
    )
    keys_wide = widen_rim(keys_own, key_edges[0], half_index)
    values_wide = widen_rim(values_own, key_edges[1], half_index)
    keys_ext, values_ext = (
        with_halo(keys_wide, (("tm", 1), ("height", 2)), 1),
        with_halo(values_wide, (("tm", 1), ("height", 2)), 1),
    )
    table_start = (time_index, height_index * TH_DEV, anchor)
    table_span = (3, TH_DEV + 2, tiles_half + 2)
    table_pad = ((1, 1), (1, 1), (0, 0))
    valid_ext = lax.dynamic_slice(jnp.pad(tile_valid, table_pad), table_start, table_span)
    shift_ext = lax.dynamic_slice(jnp.pad(width_shift, table_pad), table_start, table_span)
    triple = jnp.arange(3)
    query_cols = jnp.arange(tiles_half) + 2 * half_index

    def query_row(keep_grads, carry, row_index):
        query_tiles = lax.dynamic_index_in_dim(query_own[:, 0], row_index, 1, keepdims=False)
        grad_tiles = lax.dynamic_index_in_dim(grads_own[:, 0], row_index, 1, keepdims=False)
        key_rows = lax.dynamic_slice_in_dim(keys_ext, row_index, 3, 2)
        value_rows = lax.dynamic_slice_in_dim(values_ext, row_index, 3, 2)
        shift_row = lax.dynamic_index_in_dim(shift_ext[1], row_index + 1, 0, keepdims=False)
        starts = query_cols + lax.dynamic_slice_in_dim(shift_row, 2 * half_index, tiles_half) - 1
        window_cols = starts[:, None] + triple[None, :]
        key_win = key_rows[:, :, :, window_cols].transpose(0, 3, 1, 2, 4, 5, 6)
        key_win = key_win.reshape(groups, tiles_half, 27 * tile_cells, D_HEAD)
        value_win = value_rows[:, :, :, window_cols].transpose(0, 3, 1, 2, 4, 5, 6)
        value_win = value_win.reshape(groups, tiles_half, 27 * tile_cells, D_HEAD)
        valid_rows = lax.dynamic_slice_in_dim(valid_ext, row_index, 3, 1)[:, :, window_cols]
        own_tile = (
            (triple[:, None, None, None] == 1)
            & (triple[None, :, None, None] == 1)
            & (window_cols[None, None] == query_cols[None, None, :, None])
        )
        allowed = ((valid_rows == 1) | own_tile).transpose(2, 0, 1, 3)
        tile_bias = jnp.where(allowed.reshape(tiles_half, 27, 1), 0.0, MASKED_SCORE).astype(
            jnp.float32
        )
        mask_bias = jnp.broadcast_to(tile_bias, (tiles_half, 27, tile_cells)).reshape(
            1, tiles_half, 1, 27 * tile_cells
        )
        scores = (
            score_scale
            * jnp.einsum(
                "gwid,gwjd->gwij", query_tiles, key_win, preferred_element_type=jnp.float32
            )
            + mask_bias
        )
        row_max = jnp.max(scores, axis=-1, keepdims=True)
        probs = jnp.exp(scores - row_max)
        exp_total = jnp.sum(probs, axis=-1, keepdims=True)
        log_total = row_max + jnp.log(exp_total)
        weights = probs / exp_total
        grad_weights = jnp.einsum(
            "gwid,gwjd->gwij", grad_tiles, value_win, preferred_element_type=jnp.float32
        )
        delta_row = jnp.sum(weights * grad_weights, axis=-1, keepdims=True)
        dscore = (weights * (grad_weights - delta_row)).astype(jnp.bfloat16)
        query_part = score_scale * jnp.einsum(
            "gwij,gwjd->gwid", dscore, key_win, preferred_element_type=jnp.float32
        )
        key_acc, value_acc = carry
        key_part = score_scale * jnp.einsum(
            "gwij,gwid->gwjd", dscore, query_tiles, preferred_element_type=jnp.float32
        )
        value_part = jnp.einsum(
            "gwij,gwid->gwjd",
            weights.astype(jnp.bfloat16),
            grad_tiles,
            preferred_element_type=jnp.float32,
        )
        time_pick = triple[None, :, None, None]
        row_pick = triple[None, None, :, None]
        col_pick = window_cols[:, None, None, :]

        def spread(acc_grid, part_grad):
            shaped = part_grad.reshape(groups, tiles_half, 3, 3, 3, tile_cells, D_HEAD)
            rows_now = lax.dynamic_slice_in_dim(acc_grid, row_index, 3, 2)
            rows_now = rows_now.at[:, time_pick, row_pick, col_pick].add(shaped)
            return lax.dynamic_update_slice_in_dim(acc_grid, rows_now, row_index, 2)

        carry = (spread(key_acc, key_part), spread(value_acc, value_part))
        return (carry, (query_part, log_total[..., 0], delta_row[..., 0]))

    zero_grads = jnp.zeros(keys_ext.shape, jnp.float32)
    (key_acc, value_acc), row_outputs = lax.scan(
        partial(query_row, True), (zero_grads, zero_grads), jnp.arange(TH_DEV)
    )
    from_below = (
        shifted(key_acc[:, :, -1:].astype(jnp.bfloat16), "height", 1).astype(jnp.float32),
        shifted(value_acc[:, :, -1:].astype(jnp.bfloat16), "height", 1).astype(jnp.float32),
    )
    from_above = (
        shifted(key_acc[:, :, :1].astype(jnp.bfloat16), "height", -1).astype(jnp.float32),
        shifted(value_acc[:, :, :1].astype(jnp.bfloat16), "height", -1).astype(jnp.float32),
    )

    def fold_rows(acc_grid, lower_in, upper_in):
        acc_grid = acc_grid.at[:, :, 1:2].add(lower_in)
        acc_grid = acc_grid.at[:, :, TH_DEV : TH_DEV + 1].add(upper_in)
        return acc_grid[:, :, 1 : TH_DEV + 1]

    key_core = fold_rows(key_acc, from_below[0], from_above[0])
    value_core = fold_rows(value_acc, from_below[1], from_above[1])
    from_before = shifted((key_core[:, 2:3], value_core[:, 2:3]), "tm", 1)
    from_after = shifted((key_core[:, 0:1], value_core[:, 0:1]), "tm", -1)
    key_mid = key_core[:, 1] + from_before[0][:, 0] + from_after[0][:, 0]
    value_mid = value_core[:, 1] + from_before[1][:, 0] + from_after[1][:, 0]

    def rim_of(mid_grid):
        return jnp.where(half_index == 0, mid_grid[:, :, -2:], mid_grid[:, :, :2])

    rim_back = (
        passed_along(rim_of(key_mid).astype(jnp.bfloat16), "seq", seq_count // 2).astype(
            jnp.float32
        ),
        passed_along(rim_of(value_mid).astype(jnp.bfloat16), "seq", seq_count // 2).astype(
            jnp.float32
        ),
    )

    def settle(mid_grid, received):
        left_side = jnp.concatenate(
            [
                mid_grid[:, :, : tiles_half - 2],
                mid_grid[:, :, tiles_half - 2 : tiles_half] + received,
            ],
            axis=2,
        )
        right_side = jnp.concatenate([mid_grid[:, :, 2:4] + received, mid_grid[:, :, 4:]], axis=2)
        return jnp.where(half_index == 0, left_side, right_side)

    key_grid = from_tiles(settle(key_mid, rim_back[0])[:, None], TILE).astype(jnp.bfloat16)
    value_grid = from_tiles(settle(value_mid, rim_back[1])[:, None], TILE).astype(jnp.bfloat16)
    query_grid = from_tiles(jnp.moveaxis(row_outputs[0], 0, 1)[:, None], TILE).astype(jnp.bfloat16)

    def to_lines(grid_part):
        return grid_part.reshape(groups, TILE * TILE * TH_DEV, half_width, D_HEAD)

    returned = (
        lax.all_to_all(to_lines(query_grid), "seq", split_axis=1, concat_axis=0, tiled=True),
        lax.all_to_all(to_lines(key_grid), "seq", split_axis=1, concat_axis=0, tiled=True),
        lax.all_to_all(to_lines(value_grid), "seq", split_axis=1, concat_axis=0, tiled=True),
    )

    def to_rows(grid_part):
        split_rows = grid_part.reshape(2, HEADS, lines_dev, half_width, D_HEAD)
        return split_rows.transpose(2, 0, 3, 1, 4).reshape(
            lines_dev * 2 * half_width, HEADS * D_HEAD
        )

    return (to_rows(returned[0]), to_rows(returned[1]), to_rows(returned[2]))


TOK = TILE * TILE
SPAN = 3
LANES = 2 * D_HEAD
LINES = TW * TOK
LOG2_E = 1.4426950408889634
VMEM_BYTES = 56 * 1024 * 1024
NT = (((1,), (1,)), ((), ()))
NN = (((1,), (0,)), ((), ()))
TN = (((0,), (0,)), ((), ()))
ANYWHERE = pl.BlockSpec(memory_space=pl.ANY)
SCALARS = pl.BlockSpec(memory_space=pltpu.SMEM)
WHOLE = pl.BlockSpec(memory_space=pltpu.VMEM)
PARAMS = pltpu.CompilerParams(vmem_limit_bytes=VMEM_BYTES)


def row_order(inverse):
    target = lax.broadcasted_iota(jnp.int32, (LINES, LINES), 0)
    source = lax.broadcasted_iota(jnp.int32, (LINES, LINES), 1)
    if inverse:
        target, source = source, target
    col, line, x = target // TOK, (target // TILE) % TILE, target % TILE
    return (source == line * (TW * TILE) + col * TILE + x).astype(jnp.bfloat16)


def split_kernel(places, turn, pairs, place_ref, *refs):
    arrays, outs = refs[: 2 * pairs], refs[2 * pairs : 2 * pairs + places]
    taken, ready, in_sem, out_sem = refs[2 * pairs + places :]
    turns = HEADS // places
    loads = []
    for k in range(places):
        first = pl.multiple_of(((place_ref[0] ^ k) * turns + turn) * D_HEAD, D_HEAD)
        loads.append(
            [
                pltpu.make_async_copy(
                    ref.at[:, pl.ds(first, D_HEAD)], taken.at[k, which], in_sem.at[k, which]
                )
                for which, ref in enumerate(arrays)
            ]
        )
        for copy in loads[k]:
            copy.start()
    order = row_order(False)
    stores = []
    for k in range(places):
        for copy in loads[k]:
            copy.wait()
        for pair in range(pairs):
            for row in range(2):
                lines = slice(row * LINES, (row + 1) * LINES)
                rows = jnp.concatenate(
                    [taken[k, 2 * pair, lines, :], taken[k, 2 * pair + 1, lines, :]], axis=1
                )
                moved = lax.dot_general(order, rows, NN, preferred_element_type=jnp.float32)
                ready[k, pair, row] = moved.astype(jnp.bfloat16)
        stores.append(pltpu.make_async_copy(ready.at[k], outs[k], out_sem.at[k]))
        stores[k].start()
    for copy in stores:
        copy.wait()


def split_heads(places, turn, place, arrays):
    rows, pairs = arrays[0].shape[0], len(arrays) // 2
    return pl.pallas_call(
        lambda *refs: split_kernel(places, turn, pairs, *refs),
        in_specs=[SCALARS] + [ANYWHERE] * (2 * pairs),
        out_specs=[ANYWHERE] * places,
        out_shape=[jax.ShapeDtypeStruct((pairs, 2, LINES, LANES), jnp.bfloat16)] * places,
        scratch_shapes=[
            pltpu.VMEM((places, 2 * pairs, rows, D_HEAD), jnp.bfloat16),
            pltpu.VMEM((places, pairs, 2, LINES, LANES), jnp.bfloat16),
            pltpu.SemaphoreType.DMA((places, 2 * pairs)),
            pltpu.SemaphoreType.DMA((places,)),
        ],
        compiler_params=PARAMS,
    )(place, *arrays)


def join_kernel(places, turn, widths, kept, place_ref, *refs):
    count = len(widths)
    groups = [refs[n * places : (n + 1) * places] for n in range(count)]
    refs = refs[count * places + kept :]
    outs, taken, (ready, in_sem, out_sem) = refs[:3], refs[3 : 3 + count], refs[3 + count :]
    turns = HEADS // places
    loads = []
    for k in range(places):
        loads.append(
            [
                pltpu.make_async_copy(groups[n][k], taken[n].at[k], in_sem.at[k, n])
                for n in range(count)
            ]
        )
        for copy in loads[k]:
            copy.start()
    order = row_order(True)
    stores = []
    for k in range(places):
        for copy in loads[k]:
            copy.wait()
        for row in range(2):
            which = 0
            for n in range(count):
                back = lax.dot_general(
                    order, taken[n][k, row], NN, preferred_element_type=jnp.float32
                ).astype(jnp.bfloat16)
                for lane in range(0, widths[n], D_HEAD):
                    ready[k, which, row * LINES : (row + 1) * LINES, :] = back[
                        :, lane : lane + D_HEAD
                    ]
                    which += 1
        first = pl.multiple_of(((place_ref[0] ^ k) * turns + turn) * D_HEAD, D_HEAD)
        for which in range(3):
            copy = pltpu.make_async_copy(
                ready.at[k, which], outs[which].at[:, pl.ds(first, D_HEAD)], out_sem.at[k, which]
            )
            copy.start()
            stores.append(copy)
    for copy in stores:
        copy.wait()


def join_heads(places, turn, place, groups, earlier):
    rows = 2 * LINES
    widths = [group[0].shape[-1] for group in groups]
    count = len(widths)
    return pl.pallas_call(
        lambda *refs: join_kernel(places, turn, widths, len(earlier), *refs),
        in_specs=[SCALARS] + [ANYWHERE] * (count * places + len(earlier)),
        out_specs=[ANYWHERE] * 3,
        out_shape=[jax.ShapeDtypeStruct((rows, HEADS * D_HEAD), jnp.bfloat16)] * 3,
        scratch_shapes=[pltpu.VMEM((places, 2, LINES, width), jnp.bfloat16) for width in widths]
        + [
            pltpu.VMEM((places, 3, rows, D_HEAD), jnp.bfloat16),
            pltpu.SemaphoreType.DMA((places, count)),
            pltpu.SemaphoreType.DMA((places, 3)),
        ],
        input_output_aliases={1 + count * places + n: n for n in range(len(earlier))},
        compiler_params=PARAMS,
    )(place, *[block for group in groups for block in group], *earlier)


def edge_kernel(places, *refs):
    blocks, (first_ref, last_ref), sem = refs[:places], refs[places : places + 2], refs[-1]
    copies = []
    for k in range(places):
        for row, ref in enumerate((first_ref, last_ref)):
            copies.append(pltpu.make_async_copy(blocks[k].at[0, row], ref.at[k], sem.at[k, row]))
    for copy in copies:
        copy.start()
    for copy in copies:
        copy.wait()


def edge_rows(places, blocks):
    return pl.pallas_call(
        lambda *refs: edge_kernel(places, *refs),
        in_specs=[ANYWHERE] * places,
        out_specs=[WHOLE] * 2,
        out_shape=[jax.ShapeDtypeStruct((places, LINES, LANES), jnp.bfloat16)] * 2,
        scratch_shapes=[pltpu.SemaphoreType.DMA((places, 2))],
        compiler_params=PARAMS,
    )(*blocks)


def grad_kernel(places, count, place_ref, start_ref, bias_ref, *refs):
    groups = [refs[n * places : (n + 1) * places] for n in range(count)]
    (from_above, from_below), outs = refs[count * places :][:2], refs[count * places + 2 :]
    dq_refs, acc_out, above_ref, below_ref = outs[:places], *outs[places : places + 3]
    kv, own_rows, acc, dq, scores, low, in_sem, halo_sem, out_sem = outs[places + 3 :]
    frames = places // TILE
    scale = D_HEAD**-0.5
    copies = []
    for k in range(places):
        seat = place_ref[0] ^ k
        spot = (seat // TILE, seat % TILE)
        copies += [
            pltpu.make_async_copy(groups[0][k].at[0], kv.at[pl.ds(1, 2), *spot], in_sem.at[k, 0]),
            pltpu.make_async_copy(groups[-1][k].at[2 - count], own_rows.at[:, *spot], in_sem.at[k, 1]),
            pltpu.make_async_copy(from_above.at[k], kv.at[0, *spot], halo_sem.at[k, 0]),
            pltpu.make_async_copy(from_below.at[k], kv.at[3, *spot], halo_sem.at[k, 1]),
        ]
    for copy in copies:
        copy.start()
    acc[...] = jnp.zeros(acc.shape, acc.dtype)
    for copy in copies:
        copy.wait()
    part = places * SPAN * TOK
    piece = SPAN * TOK

    def diagonal(own):
        cells = own.shape[0] // frames
        blank = jnp.zeros((cells, D_HEAD), own.dtype)
        lines = []
        for frame in range(frames):
            line = [blank] * frames
            line[frame] = own[frame * cells : (frame + 1) * cells, :]
            lines.append(jnp.concatenate(line, axis=1))
        return jnp.concatenate(lines, axis=0)

    def group(col, _):
        here = pl.multiple_of(col * TOK, TOK)
        queries, grads, windows, tops = [], [], [], []

        def near_keys(row, near, lanes):
            return jnp.concatenate(
                [
                    kv[row + near, :, :, window, lanes].reshape(part, D_HEAD)
                    for window in windows[row]
                ],
                axis=1,
            )

        for row in range(2):
            windows.append(
                [
                    pl.ds(pl.multiple_of(start_ref[(row * TW + col) * frames + f] * TOK, TOK), piece)
                    for f in range(frames)
                ]
            )
            own = own_rows[row, :, :, pl.ds(here, TOK), :].reshape(-1, LANES)
            queries.append(diagonal(own[:, :D_HEAD]))
            grads.append(diagonal(own[:, D_HEAD:]))
            top = None
            for near in range(3):
                score_raw = lax.dot_general(
                    near_keys(row, near, slice(0, D_HEAD)), queries[row], NT,
                    preferred_element_type=jnp.float32,
                )
                scores[row, near, :, D_HEAD:] = lax.dot_general(
                    near_keys(row, near, slice(D_HEAD, LANES)), grads[row], NT,
                    preferred_element_type=jnp.float32,
                )
                for frame in range(frames):
                    first = (near * frames + frame) * SPAN
                    bias = jnp.concatenate(
                        [
                            jnp.broadcast_to(
                                bias_ref[row, col, first + c : first + c + 1, :], (TOK, D_HEAD)
                            )
                            for c in range(SPAN)
                        ],
                        axis=0,
                    )
                    for sub in range(TILE):
                        at = (frame * TILE + sub) * piece
                        score = score_raw[at : at + piece, :] * (scale * LOG2_E) + bias
                        scores[row, near, at : at + piece, :D_HEAD] = score
                        most = jnp.max(score.reshape(-1, 8, D_HEAD), axis=0)
                        top = most if top is None else jnp.maximum(top, most)
            tops.append(jnp.max(top, axis=0, keepdims=True))
        sums = []
        for row in range(2):
            total = jnp.zeros((8, D_HEAD), jnp.float32)
            delta = jnp.zeros((8, D_HEAD), jnp.float32)
            for near in range(3):
                for at in range(0, part, piece):
                    prob = jnp.exp2(scores[row, near, at : at + piece, :D_HEAD] - tops[row])
                    total = total + jnp.sum(prob.reshape(-1, 8, D_HEAD), axis=0)
                    grad = prob * scores[row, near, at : at + piece, D_HEAD:]
                    delta = delta + jnp.sum(grad.reshape(-1, 8, D_HEAD), axis=0)
            total = jnp.sum(total, axis=0, keepdims=True)
            delta = jnp.sum(delta, axis=0, keepdims=True) / total
            sums.append((tops[row] + jnp.log2(total), delta))
        for row in range(2):
            log_total, delta = sums[row]
            query_grad = None
            for near in range(3):
                for at in range(0, part, piece):
                    weight = jnp.exp2(scores[row, near, at : at + piece, :D_HEAD] - log_total)
                    dscore = weight * (scores[row, near, at : at + piece, D_HEAD:] - delta)
                    low[row, near, at : at + piece, :D_HEAD] = dscore.astype(jnp.bfloat16)
                    low[row, near, at : at + piece, D_HEAD:] = weight.astype(jnp.bfloat16)
                key_part = lax.dot_general(
                    low[row, near, :, :D_HEAD], queries[row], NN, preferred_element_type=jnp.float32
                )
                value_part = lax.dot_general(
                    low[row, near, :, D_HEAD:], grads[row], NN, preferred_element_type=jnp.float32
                )
                for f in range(frames):
                    lanes = slice(f * D_HEAD, (f + 1) * D_HEAD)
                    added = jnp.concatenate([key_part[:, lanes], value_part[:, lanes]], axis=1)
                    spot = (row + near, slice(None), slice(None), windows[row][f], slice(None))
                    acc[spot] = acc[spot] + added.reshape(frames, TILE, piece, LANES)
                more = lax.dot_general(
                    low[row, near, :, :D_HEAD],
                    near_keys(row, near, slice(0, D_HEAD)),
                    TN,
                    preferred_element_type=jnp.float32,
                )
                query_grad = more if query_grad is None else query_grad + more
            for f in range(frames):
                cells = query_grad.shape[0] // frames
                mine = query_grad[f * cells : (f + 1) * cells, f * D_HEAD : (f + 1) * D_HEAD]
                dq[row, f, :, pl.ds(here, TOK), :] = (
                    (mine * scale).astype(jnp.bfloat16).reshape(TILE, TOK, D_HEAD)
                )
        return 0

    lax.fori_loop(0, TW, group, 0)
    copies = []
    for k in range(places):
        seat = place_ref[0] ^ k
        spot = (seat // TILE, seat % TILE)
        copies += [
            pltpu.make_async_copy(dq.at[:, *spot], dq_refs[k], out_sem.at[k, 0]),
            pltpu.make_async_copy(acc.at[pl.ds(1, 2), *spot], acc_out.at[k], out_sem.at[k, 1]),
        ]
    for copy in copies:
        copy.start()
    for k in range(places):
        seat = place_ref[0] ^ k
        spot = (seat // TILE, seat % TILE)
        above_ref[k] = acc[0, *spot].astype(jnp.bfloat16)
        below_ref[k] = acc[3, *spot].astype(jnp.bfloat16)
    for copy in copies:
        copy.wait()


def head_grads(places, place, starts, bias, groups, from_above, from_below):
    frames = places // TILE
    part = places * SPAN * TOK
    results = pl.pallas_call(
        lambda *refs: grad_kernel(places, len(groups), *refs),
        in_specs=[SCALARS, SCALARS, WHOLE] + [ANYWHERE] * (len(groups) * places + 2),
        out_specs=[ANYWHERE] * (places + 1) + [WHOLE] * 2,
        out_shape=[jax.ShapeDtypeStruct((2, LINES, D_HEAD), jnp.bfloat16)] * places
        + [jax.ShapeDtypeStruct((places, 2, LINES, LANES), jnp.float32)]
        + [jax.ShapeDtypeStruct((places, LINES, LANES), jnp.bfloat16)] * 2,
        scratch_shapes=[
            pltpu.VMEM((4, frames, TILE, LINES, LANES), jnp.bfloat16),
            pltpu.VMEM((2, frames, TILE, LINES, LANES), jnp.bfloat16),
            pltpu.VMEM((4, frames, TILE, LINES, LANES), jnp.float32),
            pltpu.VMEM((2, frames, TILE, LINES, D_HEAD), jnp.bfloat16),
            pltpu.VMEM((2, 3, part, LANES), jnp.float32),
            pltpu.VMEM((2, 3, part, LANES), jnp.bfloat16),
            pltpu.SemaphoreType.DMA((places, 2)),
            pltpu.SemaphoreType.DMA((places, 2)),
            pltpu.SemaphoreType.DMA((places, 2)),
        ],
        compiler_params=PARAMS,
        cost_estimate=pl.CostEstimate(
            flops=60_000_000_000, bytes_accessed=0, transcendentals=0
        ),
    )(place, starts, bias, *[block for group in groups for block in group], from_above, from_below)
    return results[:places], *results[places:]


def finish_kernel(places, acc_ref, above_ref, below_ref, *refs):
    with_query = len(refs) > places
    outs = refs[-places:]
    lane = lax.broadcasted_iota(jnp.int32, (1, LANES), 1)
    factor = jnp.where(lane < D_HEAD, D_HEAD**-0.5, 1.0)
    for k in range(places):
        for row, ref in enumerate((above_ref, below_ref)):
            total = acc_ref[k, row] + ref[k].astype(jnp.float32)
            outs[k][row, :, :LANES] = (total * factor).astype(jnp.bfloat16)
        if with_query:
            outs[k][:, :, LANES:] = refs[k][...]


def finish_pairs(places, acc, above, below, query=()):
    lanes = LANES + (D_HEAD if query else 0)
    return pl.pallas_call(
        lambda *refs: finish_kernel(places, *refs),
        in_specs=[WHOLE] * (3 + len(query)),
        out_specs=[WHOLE] * places,
        out_shape=[jax.ShapeDtypeStruct((2, LINES, lanes), jnp.bfloat16)] * places,
        compiler_params=PARAMS,
    )(acc, above, below, *query)


def window_tables(tile_valid, width_shift, first_row):
    frames, _, cols = tile_valid.shape
    shift_own = lax.dynamic_slice_in_dim(width_shift, first_row, 2, 1)
    first = jnp.clip(jnp.arange(cols) + shift_own - 1, 0, cols - SPAN)
    valid = lax.dynamic_slice_in_dim(
        jnp.pad(tile_valid, ((0, 0), (1, 1), (2, 2))), first_row, 4, 1
    )
    near = jnp.stack([valid[:, n : n + 2] for n in range(3)])[:, :, None]
    moved = jnp.stack([near[..., d : d + cols] for d in range(5)])
    shift = first - (jnp.arange(cols) - 1)
    chosen = jnp.where(shift == -1, moved[0:3], jnp.where(shift == 0, moved[1:4], moved[2:5]))
    place_of = jnp.arange(3).reshape(-1, 1, 1, 1, 1, 1)
    near_of = jnp.arange(3).reshape(1, -1, 1, 1, 1, 1)
    key_frame = jnp.arange(frames).reshape(1, 1, -1, 1, 1, 1)
    frame = jnp.arange(frames).reshape(1, 1, 1, -1, 1, 1)
    own = (near_of == 1) & (key_frame == frame) & (place_of + shift == 1)
    bias = jnp.where((chosen == 1) | own, 0.0, MASKED_SCORE).astype(jnp.float32)
    bias = bias.transpose(4, 5, 1, 2, 0, 3).reshape(2, cols, 3 * frames * SPAN, frames, 1)
    bias = jnp.broadcast_to(bias, bias.shape[:4] + (TILE**3,))
    return (
        first.transpose(1, 2, 0).reshape(-1),
        bias.reshape(2, cols, 3 * frames * SPAN, frames * TILE**3),
    )


def place_shards(queries, key_states, value_states, out_grad, tile_valid, width_shift):
    frames = tile_valid.shape[0]
    places = frames * TILE
    turns = HEADS // places
    seq_count = lax.axis_size("seq")
    heights = lax.axis_size("height")
    seq_index = lax.axis_index("seq")
    place = (lax.axis_index("tm") * TILE + seq_index // 2).reshape(1)
    first_row = lax.axis_index("height") * TH_DEV + seq_index % 2 * 2
    starts, bias = window_tables(tile_valid, width_shift, first_row)
    chain = [
        [h * seq_count + frame * 2 + half for h in range(heights) for half in range(2)]
        for frame in range(TILE)
    ]
    down = [pair for line in chain for pair in zip(line[:-1], line[1:])]
    up = [(b, a) for a, b in down]

    def send(block, k):
        return lax.ppermute(block, ("tm", "seq"), [(i, i ^ (2 * k)) for i in range(2 * places)])

    def step(block, route):
        return lax.ppermute(block, ("height", "seq"), route)

    def exchange(blocks, order):
        moved = dict(enumerate(blocks))
        for k in order:
            moved[k] = send(blocks[k], k)
        return [moved[k] for k in range(places)]

    natural = list(range(1, places))
    far, near = [k for k in natural if k & 2], [k for k in natural if not k & 2]
    held = [far[-1], near[0]]
    mixed = far[:-1] + near[1:] + held

    def after(blocks, results):
        kept, results = lax.optimization_barrier(([blocks[k] for k in held], results))
        blocks = list(blocks)
        for k, block in zip(held, kept):
            blocks[k] = block
        return blocks, results

    def ordered(first, then):
        return lax.optimization_barrier((first, then))

    def ordered(first, then):
        return lax.optimization_barrier((first, then))

    def ordered(first, then):
        return lax.optimization_barrier((first, then))

    arrays = (key_states, value_states, queries, out_grad)
    outs = ()
    groups = [exchange(split_heads(places, 0, place, arrays), natural)]
    leaving = None
    for turn in range(turns):
        more = turn + 1 < turns
        if more:
            coming = split_heads(places, turn + 1, place, arrays)
            groups[-1][1:6], coming = ordered(groups[-1][1:6], coming)
        first, last = edge_rows(places, groups[0])
        grads = head_grads(places, place, starts, bias, groups, step(last, down), step(first, up))
        if leaving is not None:
            leaving, grads = after(leaving, grads)
            left = exchange(leaving, mixed)
            passed, grads = ordered([left[k] for k in mixed[:-2]], grads)
            for k, block in zip(mixed, passed):
                left[k] = block
            outs = join_heads(places, turn - 1, place, [left], outs)
        if more:
            coming, grads = after(coming, grads)
            groups = [exchange(coming, mixed)]
        dq, acc, above, below = grads
        leaving = finish_pairs(places, acc, step(below, down), step(above, up), dq)
    outs = join_heads(places, turns - 1, place, [exchange(leaving, natural)], outs)
    key_out, value_out, query_out = outs
    return query_out, key_out, value_out


def solution(mesh):
    frames, seq_count = mesh.shape["tm"], mesh.shape["seq"]
    by_place = frames == 2 and seq_count == 2 * TILE
    placed = (
        P(("tm", "height", "seq"), None),
        P(("tm", "height", "seq"), None),
        P(("tm", "height", "seq"), None),
        P(("tm", "height", "seq"), None),
        P(),
        P(),
    )
    return jax.shard_map(
        place_shards if by_place else shards,
        mesh=mesh,
        in_specs=placed,
        out_specs=(
            P(("tm", "height", "seq"), None),
            P(("tm", "height", "seq"), None),
            P(("tm", "height", "seq"), None),
        ),
        check_vma=False,
    )
```

```python
from functools import partial

import jax
import jax.numpy as jnp
from jax import lax
from jax.experimental import pallas as pl
from jax.experimental.pallas import tpu as pltpu
from jax.sharding import PartitionSpec as P

D_HEAD = 128
HEADS = 16
TILE = 4
TH_DEV = 4
TW = 16


MASKED_SCORE = -1e30


def passed_along(block, axis, distance):
    devices = range(lax.axis_size(axis))
    route = [((i - distance) % len(devices), i) for i in devices]
    return lax.ppermute(block, axis, route)


def with_halo(cells, sides, width):
    for axis, dim in sides:
        count = lax.axis_size(axis)
        ends = count - 1
        head = lax.slice_in_dim(cells, 0, width, axis=dim)
        tail = lax.slice_in_dim(cells, cells.shape[dim] - width, cells.shape[dim], axis=dim)
        cells = jnp.concatenate(
            [
                lax.ppermute(tail, axis, [(i, (i + 1) % count) for i in range(ends)]),
                cells,
                lax.ppermute(head, axis, [((i + 1) % count, i) for i in range(ends)]),
            ],
            axis=dim,
        )
    return cells


def shifted(value, axis, steps):
    count = lax.axis_size(axis)
    initial, last = (max(0, -steps), min(count, count - steps))
    return lax.ppermute(value, axis, [(source, source + steps) for source in range(initial, last)])


def to_tiles(grid_in, tile_edge):
    groups, frames, grid_rows, grid_cols = grid_in.shape[:4]
    trailing = grid_in.shape[4:]
    split_grid = grid_in.reshape(
        (
            groups,
            frames // tile_edge,
            tile_edge,
            grid_rows // tile_edge,
            tile_edge,
            grid_cols // tile_edge,
            tile_edge,
        )
        + trailing
    )
    axis_order = (0, 1, 3, 5, 2, 4, 6) + tuple(range(7, 7 + len(trailing)))
    return split_grid.transpose(axis_order).reshape(
        (groups, frames // tile_edge, grid_rows // tile_edge, grid_cols // tile_edge, tile_edge**3)
        + trailing
    )


def from_tiles(tiles_in, tile_edge):
    groups, frame_tiles, row_tiles, col_tiles = tiles_in.shape[:4]
    trailing = tiles_in.shape[5:]
    split_grid = tiles_in.reshape(
        (groups, frame_tiles, row_tiles, col_tiles, tile_edge, tile_edge, tile_edge) + trailing
    )
    axis_order = (0, 1, 4, 2, 5, 3, 6) + tuple(range(7, 7 + len(trailing)))
    return split_grid.transpose(axis_order).reshape(
        (groups, frame_tiles * tile_edge, row_tiles * tile_edge, col_tiles * tile_edge) + trailing
    )


def edge_tiles(piece_own, half_index):
    return jnp.where(half_index == 0, piece_own[:, :, :, -2:], piece_own[:, :, :, :2])


def widen_rim(piece_own, received, half_index):
    left_side = jnp.concatenate([piece_own, received], axis=3)
    right_side = jnp.concatenate([received, piece_own], axis=3)
    return jnp.where(half_index == 0, left_side, right_side)


def shards(queries, key_states, value_states, out_grad, tile_valid, width_shift):
    seq_count = lax.axis_size("seq")
    groups = 2 * HEADS // seq_count
    half_width = TW * TILE // 2
    lines_dev = queries.shape[0] // (TW * TILE)
    tiles_half = TW // 2
    tile_cells = TILE**3
    score_scale = D_HEAD ** (-0.5)
    time_index = lax.axis_index("tm")
    height_index = lax.axis_index("height")
    half_index = lax.axis_index("seq") * groups // HEADS
    anchor = half_index * (tiles_half - 2)

    def to_heads(rows_in):
        split_rows = rows_in.reshape(lines_dev, 2, half_width, HEADS, D_HEAD)
        return split_rows.transpose(1, 3, 0, 2, 4).reshape(2 * HEADS, lines_dev, half_width, D_HEAD)

    moved = (
        lax.all_to_all(to_heads(queries), "seq", split_axis=0, concat_axis=1, tiled=True),
        lax.all_to_all(to_heads(key_states), "seq", split_axis=0, concat_axis=1, tiled=True),
        lax.all_to_all(to_heads(value_states), "seq", split_axis=0, concat_axis=1, tiled=True),
        lax.all_to_all(to_heads(out_grad), "seq", split_axis=0, concat_axis=1, tiled=True),
    )

    def own_tiles(grid_part):
        return to_tiles(grid_part.reshape(groups, TILE, TILE * TH_DEV, half_width, D_HEAD), TILE)

    query_own, keys_own, values_own, grads_own = [own_tiles(grid_part) for grid_part in moved]
    key_edges = passed_along(
        (edge_tiles(keys_own, half_index), edge_tiles(values_own, half_index)),
        "seq",
        seq_count // 2,
    )
    keys_wide = widen_rim(keys_own, key_edges[0], half_index)
    values_wide = widen_rim(values_own, key_edges[1], half_index)
    keys_ext, values_ext = (
        with_halo(keys_wide, (("tm", 1), ("height", 2)), 1),
        with_halo(values_wide, (("tm", 1), ("height", 2)), 1),
    )
    table_start = (time_index, height_index * TH_DEV, anchor)
    table_span = (3, TH_DEV + 2, tiles_half + 2)
    table_pad = ((1, 1), (1, 1), (0, 0))
    valid_ext = lax.dynamic_slice(jnp.pad(tile_valid, table_pad), table_start, table_span)
    shift_ext = lax.dynamic_slice(jnp.pad(width_shift, table_pad), table_start, table_span)
    triple = jnp.arange(3)
    query_cols = jnp.arange(tiles_half) + 2 * half_index

    def query_row(keep_grads, carry, row_index):
        query_tiles = lax.dynamic_index_in_dim(query_own[:, 0], row_index, 1, keepdims=False)
        grad_tiles = lax.dynamic_index_in_dim(grads_own[:, 0], row_index, 1, keepdims=False)
        key_rows = lax.dynamic_slice_in_dim(keys_ext, row_index, 3, 2)
        value_rows = lax.dynamic_slice_in_dim(values_ext, row_index, 3, 2)
        shift_row = lax.dynamic_index_in_dim(shift_ext[1], row_index + 1, 0, keepdims=False)
        starts = query_cols + lax.dynamic_slice_in_dim(shift_row, 2 * half_index, tiles_half) - 1
        window_cols = starts[:, None] + triple[None, :]
        key_win = key_rows[:, :, :, window_cols].transpose(0, 3, 1, 2, 4, 5, 6)
        key_win = key_win.reshape(groups, tiles_half, 27 * tile_cells, D_HEAD)
        value_win = value_rows[:, :, :, window_cols].transpose(0, 3, 1, 2, 4, 5, 6)
        value_win = value_win.reshape(groups, tiles_half, 27 * tile_cells, D_HEAD)
        valid_rows = lax.dynamic_slice_in_dim(valid_ext, row_index, 3, 1)[:, :, window_cols]
        own_tile = (
            (triple[:, None, None, None] == 1)
            & (triple[None, :, None, None] == 1)
            & (window_cols[None, None] == query_cols[None, None, :, None])
        )
        allowed = ((valid_rows == 1) | own_tile).transpose(2, 0, 1, 3)
        tile_bias = jnp.where(allowed.reshape(tiles_half, 27, 1), 0.0, MASKED_SCORE).astype(
            jnp.float32
        )
        mask_bias = jnp.broadcast_to(tile_bias, (tiles_half, 27, tile_cells)).reshape(
            1, tiles_half, 1, 27 * tile_cells
        )
        scores = (
            score_scale
            * jnp.einsum(
                "gwid,gwjd->gwij", query_tiles, key_win, preferred_element_type=jnp.float32
            )
            + mask_bias
        )
        row_max = jnp.max(scores, axis=-1, keepdims=True)
        probs = jnp.exp(scores - row_max)
        exp_total = jnp.sum(probs, axis=-1, keepdims=True)
        log_total = row_max + jnp.log(exp_total)
        weights = probs / exp_total
        grad_weights = jnp.einsum(
            "gwid,gwjd->gwij", grad_tiles, value_win, preferred_element_type=jnp.float32
        )
        delta_row = jnp.sum(weights * grad_weights, axis=-1, keepdims=True)
        dscore = (weights * (grad_weights - delta_row)).astype(jnp.bfloat16)
        query_part = score_scale * jnp.einsum(
            "gwij,gwjd->gwid", dscore, key_win, preferred_element_type=jnp.float32
        )
        key_acc, value_acc = carry
        key_part = score_scale * jnp.einsum(
            "gwij,gwid->gwjd", dscore, query_tiles, preferred_element_type=jnp.float32
        )
        value_part = jnp.einsum(
            "gwij,gwid->gwjd",
            weights.astype(jnp.bfloat16),
            grad_tiles,
            preferred_element_type=jnp.float32,
        )
        time_pick = triple[None, :, None, None]
        row_pick = triple[None, None, :, None]
        col_pick = window_cols[:, None, None, :]

        def spread(acc_grid, part_grad):
            shaped = part_grad.reshape(groups, tiles_half, 3, 3, 3, tile_cells, D_HEAD)
            rows_now = lax.dynamic_slice_in_dim(acc_grid, row_index, 3, 2)
            rows_now = rows_now.at[:, time_pick, row_pick, col_pick].add(shaped)
            return lax.dynamic_update_slice_in_dim(acc_grid, rows_now, row_index, 2)

        carry = (spread(key_acc, key_part), spread(value_acc, value_part))
        return (carry, (query_part, log_total[..., 0], delta_row[..., 0]))

    zero_grads = jnp.zeros(keys_ext.shape, jnp.float32)
    (key_acc, value_acc), row_outputs = lax.scan(
        partial(query_row, True), (zero_grads, zero_grads), jnp.arange(TH_DEV)
    )
    from_below = (
        shifted(key_acc[:, :, -1:].astype(jnp.bfloat16), "height", 1).astype(jnp.float32),
        shifted(value_acc[:, :, -1:].astype(jnp.bfloat16), "height", 1).astype(jnp.float32),
    )
    from_above = (
        shifted(key_acc[:, :, :1].astype(jnp.bfloat16), "height", -1).astype(jnp.float32),
        shifted(value_acc[:, :, :1].astype(jnp.bfloat16), "height", -1).astype(jnp.float32),
    )

    def fold_rows(acc_grid, lower_in, upper_in):
        acc_grid = acc_grid.at[:, :, 1:2].add(lower_in)
        acc_grid = acc_grid.at[:, :, TH_DEV : TH_DEV + 1].add(upper_in)
        return acc_grid[:, :, 1 : TH_DEV + 1]

    key_core = fold_rows(key_acc, from_below[0], from_above[0])
    value_core = fold_rows(value_acc, from_below[1], from_above[1])
    from_before = shifted((key_core[:, 2:3], value_core[:, 2:3]), "tm", 1)
    from_after = shifted((key_core[:, 0:1], value_core[:, 0:1]), "tm", -1)
    key_mid = key_core[:, 1] + from_before[0][:, 0] + from_after[0][:, 0]
    value_mid = value_core[:, 1] + from_before[1][:, 0] + from_after[1][:, 0]

    def rim_of(mid_grid):
        return jnp.where(half_index == 0, mid_grid[:, :, -2:], mid_grid[:, :, :2])

    rim_back = (
        passed_along(rim_of(key_mid).astype(jnp.bfloat16), "seq", seq_count // 2).astype(
            jnp.float32
        ),
        passed_along(rim_of(value_mid).astype(jnp.bfloat16), "seq", seq_count // 2).astype(
            jnp.float32
        ),
    )

    def settle(mid_grid, received):
        left_side = jnp.concatenate(
            [
                mid_grid[:, :, : tiles_half - 2],
                mid_grid[:, :, tiles_half - 2 : tiles_half] + received,
            ],
            axis=2,
        )
        right_side = jnp.concatenate([mid_grid[:, :, 2:4] + received, mid_grid[:, :, 4:]], axis=2)
        return jnp.where(half_index == 0, left_side, right_side)

    key_grid = from_tiles(settle(key_mid, rim_back[0])[:, None], TILE).astype(jnp.bfloat16)
    value_grid = from_tiles(settle(value_mid, rim_back[1])[:, None], TILE).astype(jnp.bfloat16)
    query_grid = from_tiles(jnp.moveaxis(row_outputs[0], 0, 1)[:, None], TILE).astype(jnp.bfloat16)

    def to_lines(grid_part):
        return grid_part.reshape(groups, TILE * TILE * TH_DEV, half_width, D_HEAD)

    returned = (
        lax.all_to_all(to_lines(query_grid), "seq", split_axis=1, concat_axis=0, tiled=True),
        lax.all_to_all(to_lines(key_grid), "seq", split_axis=1, concat_axis=0, tiled=True),
        lax.all_to_all(to_lines(value_grid), "seq", split_axis=1, concat_axis=0, tiled=True),
    )

    def to_rows(grid_part):
        split_rows = grid_part.reshape(2, HEADS, lines_dev, half_width, D_HEAD)
        return split_rows.transpose(2, 0, 3, 1, 4).reshape(
            lines_dev * 2 * half_width, HEADS * D_HEAD
        )

    return (to_rows(returned[0]), to_rows(returned[1]), to_rows(returned[2]))


TOK = TILE * TILE
SPAN = 3
SLOTS = 4
PLAN = ((1, 0), (1, 1), (1, 2), (1, 3), (2, 0), (2, 1), (2, 2), (2, 3), (3, 0), (3, 1), (3, 2), (3, 3))
LANES = 2 * D_HEAD
LINES = TW * TOK
LOG2_E = 1.4426950408889634
VMEM_BYTES = 56 * 1024 * 1024
NT = (((1,), (1,)), ((), ()))
NN = (((1,), (0,)), ((), ()))
TN = (((0,), (0,)), ((), ()))
ANYWHERE = pl.BlockSpec(memory_space=pl.ANY)
SCALARS = pl.BlockSpec(memory_space=pltpu.SMEM)
WHOLE = pl.BlockSpec(memory_space=pltpu.VMEM)
PARAMS = pltpu.CompilerParams(vmem_limit_bytes=VMEM_BYTES)


def row_order(inverse):
    target = lax.broadcasted_iota(jnp.int32, (LINES, LINES), 0)
    source = lax.broadcasted_iota(jnp.int32, (LINES, LINES), 1)
    if inverse:
        target, source = source, target
    col, line, x = target // TOK, (target // TILE) % TILE, target % TILE
    return (source == line * (TW * TILE) + col * TILE + x).astype(jnp.bfloat16)


def split_kernel(places, turn, pairs, place_ref, *refs):
    arrays, outs = refs[: 2 * pairs], refs[2 * pairs : 2 * pairs + places]
    taken, ready, in_sem, out_sem = refs[2 * pairs + places :]
    turns = HEADS // places
    loads = []
    for k in range(places):
        first = pl.multiple_of(((place_ref[0] ^ k) * turns + turn) * D_HEAD, D_HEAD)
        loads.append(
            [
                pltpu.make_async_copy(
                    ref.at[:, pl.ds(first, D_HEAD)], taken.at[k, which], in_sem.at[k, which]
                )
                for which, ref in enumerate(arrays)
            ]
        )
        for copy in loads[k]:
            copy.start()
    order = row_order(False)
    stores = []
    for k in range(places):
        for copy in loads[k]:
            copy.wait()
        for pair in range(pairs):
            for row in range(2):
                lines = slice(row * LINES, (row + 1) * LINES)
                rows = jnp.concatenate(
                    [taken[k, 2 * pair, lines, :], taken[k, 2 * pair + 1, lines, :]], axis=1
                )
                moved = lax.dot_general(order, rows, NN, preferred_element_type=jnp.float32)
                ready[k, pair, row] = moved.astype(jnp.bfloat16)
        stores.append(pltpu.make_async_copy(ready.at[k], outs[k], out_sem.at[k]))
        stores[k].start()
    for copy in stores:
        copy.wait()


def split_heads(places, turn, place, arrays):
    rows, pairs = arrays[0].shape[0], len(arrays) // 2
    return pl.pallas_call(
        lambda *refs: split_kernel(places, turn, pairs, *refs),
        in_specs=[SCALARS] + [ANYWHERE] * (2 * pairs),
        out_specs=[ANYWHERE] * places,
        out_shape=[jax.ShapeDtypeStruct((pairs, 2, LINES, LANES), jnp.bfloat16)] * places,
        scratch_shapes=[
            pltpu.VMEM((places, 2 * pairs, rows, D_HEAD), jnp.bfloat16),
            pltpu.VMEM((places, pairs, 2, LINES, LANES), jnp.bfloat16),
            pltpu.SemaphoreType.DMA((places, 2 * pairs)),
            pltpu.SemaphoreType.DMA((places,)),
        ],
        compiler_params=PARAMS,
    )(place, *arrays)


def join_kernel(seats, turn, turns, kept, place_ref, *refs):
    count = len(seats)
    blocks, outs = refs[:count], refs[count + kept : count + kept + 3]
    taken, ready, in_sem, out_sem = refs[count + kept + 3 :]
    loads = []
    for n in range(count):
        loads.append(pltpu.make_async_copy(blocks[n], taken.at[n], in_sem.at[n]))
        loads[n].start()
    order = row_order(True)
    stores = []
    for n, k in enumerate(seats):
        loads[n].wait()
        for row in range(2):
            back = lax.dot_general(
                order, taken[n, row], NN, preferred_element_type=jnp.float32
            ).astype(jnp.bfloat16)
            for which in range(3):
                ready[n, which, row * LINES : (row + 1) * LINES, :] = back[
                    :, which * D_HEAD : (which + 1) * D_HEAD
                ]
        first = pl.multiple_of(((place_ref[0] ^ k) * turns + turn) * D_HEAD, D_HEAD)
        for which in range(3):
            copy = pltpu.make_async_copy(
                ready.at[n, which], outs[which].at[:, pl.ds(first, D_HEAD)], out_sem.at[n, which]
            )
            copy.start()
            stores.append(copy)
    for copy in stores:
        copy.wait()


def join_heads(seats, turn, turns, place, blocks, earlier):
    count, rows, lanes = len(seats), 2 * LINES, blocks[0].shape[-1]
    return pl.pallas_call(
        lambda *refs: join_kernel(seats, turn, turns, len(earlier), *refs),
        in_specs=[SCALARS] + [ANYWHERE] * (count + len(earlier)),
        out_specs=[ANYWHERE] * 3,
        out_shape=[jax.ShapeDtypeStruct((rows, HEADS * D_HEAD), jnp.bfloat16)] * 3,
        scratch_shapes=[
            pltpu.VMEM((count, 2, LINES, lanes), jnp.bfloat16),
            pltpu.VMEM((count, 3, rows, D_HEAD), jnp.bfloat16),
            pltpu.SemaphoreType.DMA((count,)),
            pltpu.SemaphoreType.DMA((count, 3)),
        ],
        input_output_aliases={1 + count + n: n for n in range(len(earlier))},
        compiler_params=PARAMS,
    )(place, *blocks, *earlier)


def edge_kernel(places, *refs):
    blocks, (first_ref, last_ref), sem = refs[:places], refs[places : places + 2], refs[-1]
    copies = []
    for k in range(places):
        for row, ref in enumerate((first_ref, last_ref)):
            copies.append(pltpu.make_async_copy(blocks[k].at[0, row], ref.at[k], sem.at[k, row]))
    for copy in copies:
        copy.start()
    for copy in copies:
        copy.wait()


def edge_rows(places, blocks):
    return pl.pallas_call(
        lambda *refs: edge_kernel(places, *refs),
        in_specs=[ANYWHERE] * places,
        out_specs=[WHOLE] * 2,
        out_shape=[jax.ShapeDtypeStruct((places, LINES, LANES), jnp.bfloat16)] * 2,
        scratch_shapes=[pltpu.SemaphoreType.DMA((places, 2))],
        compiler_params=PARAMS,
    )(*blocks)


def grad_kernel(places, count, place_ref, start_ref, bias_ref, *refs):
    groups = [refs[n * places : (n + 1) * places] for n in range(count)]
    (from_above, from_below), outs = refs[count * places :][:2], refs[count * places + 2 :]
    dq_refs, acc_out, above_ref, below_ref = outs[:places], *outs[places : places + 3]
    kv, own_rows, acc, dq, scores, low, in_sem, halo_sem, out_sem = outs[places + 3 :]
    frames = places // TILE
    scale = D_HEAD**-0.5
    copies = []
    for k in range(places):
        seat = place_ref[0] ^ k
        spot = (seat // TILE, seat % TILE)
        copies += [
            pltpu.make_async_copy(groups[0][k].at[0], kv.at[pl.ds(1, 2), *spot], in_sem.at[k, 0]),
            pltpu.make_async_copy(groups[-1][k].at[2 - count], own_rows.at[:, *spot], in_sem.at[k, 1]),
            pltpu.make_async_copy(from_above.at[k], kv.at[0, *spot], halo_sem.at[k, 0]),
            pltpu.make_async_copy(from_below.at[k], kv.at[3, *spot], halo_sem.at[k, 1]),
        ]
    for copy in copies:
        copy.start()
    acc[...] = jnp.zeros(acc.shape, acc.dtype)
    for copy in copies:
        copy.wait()
    part = places * SPAN * TOK
    piece = SPAN * TOK

    def diagonal(own):
        cells = own.shape[0] // frames
        blank = jnp.zeros((cells, D_HEAD), own.dtype)
        lines = []
        for frame in range(frames):
            line = [blank] * frames
            line[frame] = own[frame * cells : (frame + 1) * cells, :]
            lines.append(jnp.concatenate(line, axis=1))
        return jnp.concatenate(lines, axis=0)

    def near_keys(row, near, windows, lanes):
        return jnp.concatenate(
            [kv[row + near, :, :, window, lanes].reshape(part, D_HEAD) for window in windows],
            axis=1,
        )

    def score_phase(slot, row, col):
        here = pl.multiple_of(col * TOK, TOK)
        windows = [
            pl.ds(pl.multiple_of(start_ref[(row * TW + col) * frames + f] * TOK, TOK), piece)
            for f in range(frames)
        ]
        own = own_rows[row, :, :, pl.ds(here, TOK), :].reshape(-1, LANES)
        query, grad = diagonal(own[:, :D_HEAD]), diagonal(own[:, D_HEAD:])
        top = None
        for near in range(3):
            score_raw = lax.dot_general(
                near_keys(row, near, windows, slice(0, D_HEAD)), query, NT,
                preferred_element_type=jnp.float32,
            )
            scores[slot, near, :, D_HEAD:] = lax.dot_general(
                near_keys(row, near, windows, slice(D_HEAD, LANES)), grad, NT,
                preferred_element_type=jnp.float32,
            )
            for frame in range(frames):
                first = (near * frames + frame) * SPAN
                bias = jnp.concatenate(
                    [
                        jnp.broadcast_to(
                            bias_ref[row, col, first + c : first + c + 1, :], (TOK, D_HEAD)
                        )
                        for c in range(SPAN)
                    ],
                    axis=0,
                )
                for sub in range(TILE):
                    at = (frame * TILE + sub) * piece
                    score = score_raw[at : at + piece, :] * (scale * LOG2_E) + bias
                    scores[slot, near, at : at + piece, :D_HEAD] = score
                    most = jnp.max(score.reshape(-1, 8, D_HEAD), axis=0)
                    top = most if top is None else jnp.maximum(top, most)
        return here, windows, query, grad, jnp.max(top, axis=0, keepdims=True)

    def total_phase(slot, top):
        total = jnp.zeros((8, D_HEAD), jnp.float32)
        delta = jnp.zeros((8, D_HEAD), jnp.float32)
        for near in range(3):
            for at in range(0, part, piece):
                prob = jnp.exp2(scores[slot, near, at : at + piece, :D_HEAD] - top)
                total = total + jnp.sum(prob.reshape(-1, 8, D_HEAD), axis=0)
                grad = prob * scores[slot, near, at : at + piece, D_HEAD:]
                delta = delta + jnp.sum(grad.reshape(-1, 8, D_HEAD), axis=0)
        total = jnp.sum(total, axis=0, keepdims=True)
        delta = jnp.sum(delta, axis=0, keepdims=True) / total
        return top + jnp.log2(total), delta

    def grad_phase(slot, row, here, windows, query, grad, log_total, delta):
        query_grad = None
        for near in range(3):
            for at in range(0, part, piece):
                weight = jnp.exp2(scores[slot, near, at : at + piece, :D_HEAD] - log_total)
                dscore = weight * (scores[slot, near, at : at + piece, D_HEAD:] - delta)
                low[slot, near, at : at + piece, :D_HEAD] = dscore.astype(jnp.bfloat16)
                low[slot, near, at : at + piece, D_HEAD:] = weight.astype(jnp.bfloat16)
            key_part = lax.dot_general(
                low[slot, near, :, :D_HEAD], query, NN, preferred_element_type=jnp.float32
            )
            value_part = lax.dot_general(
                low[slot, near, :, D_HEAD:], grad, NN, preferred_element_type=jnp.float32
            )
            for f in range(frames):
                lanes = slice(f * D_HEAD, (f + 1) * D_HEAD)
                added = jnp.concatenate([key_part[:, lanes], value_part[:, lanes]], axis=1)
                spot = (row + near, slice(None), slice(None), windows[f], slice(None))
                acc[spot] = acc[spot] + added.reshape(frames, TILE, piece, LANES)
            more = lax.dot_general(
                low[slot, near, :, :D_HEAD],
                near_keys(row, near, windows, slice(0, D_HEAD)),
                TN,
                preferred_element_type=jnp.float32,
            )
            query_grad = more if query_grad is None else query_grad + more
        for f in range(frames):
            cells = query_grad.shape[0] // frames
            mine = query_grad[f * cells : (f + 1) * cells, f * D_HEAD : (f + 1) * D_HEAD]
            dq[row, f, :, pl.ds(here, TOK), :] = (
                (mine * scale).astype(jnp.bfloat16).reshape(TILE, TOK, D_HEAD)
            )

    def group(step, _):
        known, sums = {}, {}
        for phase, slot in PLAN:
            row = slot % 2
            if phase == 1:
                known[slot] = score_phase(slot, row, step * (SLOTS // 2) + slot // 2)
            elif phase == 2:
                sums[slot] = total_phase(slot, known[slot][-1])
            else:
                grad_phase(slot, row, *known[slot][:-1], *sums[slot])
        return 0

    lax.fori_loop(0, 2 * TW // SLOTS, group, 0)
    copies = []
    for k in range(places):
        seat = place_ref[0] ^ k
        spot = (seat // TILE, seat % TILE)
        copies += [
            pltpu.make_async_copy(dq.at[:, *spot], dq_refs[k], out_sem.at[k, 0]),
            pltpu.make_async_copy(acc.at[pl.ds(1, 2), *spot], acc_out.at[k], out_sem.at[k, 1]),
        ]
    for copy in copies:
        copy.start()
    for k in range(places):
        seat = place_ref[0] ^ k
        spot = (seat // TILE, seat % TILE)
        above_ref[k] = acc[0, *spot].astype(jnp.bfloat16)
        below_ref[k] = acc[3, *spot].astype(jnp.bfloat16)
    for copy in copies:
        copy.wait()


def head_grads(places, place, starts, bias, groups, from_above, from_below):
    frames = places // TILE
    part = places * SPAN * TOK
    results = pl.pallas_call(
        lambda *refs: grad_kernel(places, len(groups), *refs),
        in_specs=[SCALARS, SCALARS, WHOLE] + [ANYWHERE] * (len(groups) * places + 2),
        out_specs=[ANYWHERE] * (places + 1) + [WHOLE] * 2,
        out_shape=[jax.ShapeDtypeStruct((2, LINES, D_HEAD), jnp.bfloat16)] * places
        + [jax.ShapeDtypeStruct((places, 2, LINES, LANES), jnp.float32)]
        + [jax.ShapeDtypeStruct((places, LINES, LANES), jnp.bfloat16)] * 2,
        scratch_shapes=[
            pltpu.VMEM((4, frames, TILE, LINES, LANES), jnp.bfloat16),
            pltpu.VMEM((2, frames, TILE, LINES, LANES), jnp.bfloat16),
            pltpu.VMEM((4, frames, TILE, LINES, LANES), jnp.float32),
            pltpu.VMEM((2, frames, TILE, LINES, D_HEAD), jnp.bfloat16),
            pltpu.VMEM((SLOTS, 3, part, LANES), jnp.float32),
            pltpu.VMEM((SLOTS, 3, part, LANES), jnp.bfloat16),
            pltpu.SemaphoreType.DMA((places, 2)),
            pltpu.SemaphoreType.DMA((places, 2)),
            pltpu.SemaphoreType.DMA((places, 2)),
        ],
        compiler_params=PARAMS,
        cost_estimate=pl.CostEstimate(
            flops=1_000_000, bytes_accessed=0, transcendentals=0
        ),
    )(place, starts, bias, *[block for group in groups for block in group], from_above, from_below)
    return results[:places], *results[places:]


def finish_kernel(places, acc_ref, above_ref, below_ref, *refs):
    with_query = len(refs) > places
    outs = refs[-places:]
    lane = lax.broadcasted_iota(jnp.int32, (1, LANES), 1)
    factor = jnp.where(lane < D_HEAD, D_HEAD**-0.5, 1.0)
    for k in range(places):
        for row, ref in enumerate((above_ref, below_ref)):
            total = acc_ref[k, row] + ref[k].astype(jnp.float32)
            outs[k][row, :, :LANES] = (total * factor).astype(jnp.bfloat16)
        if with_query:
            outs[k][:, :, LANES:] = refs[k][...]


def finish_pairs(places, acc, above, below, query=()):
    lanes = LANES + (D_HEAD if query else 0)
    return pl.pallas_call(
        lambda *refs: finish_kernel(places, *refs),
        in_specs=[WHOLE] * (3 + len(query)),
        out_specs=[WHOLE] * places,
        out_shape=[jax.ShapeDtypeStruct((2, LINES, lanes), jnp.bfloat16)] * places,
        compiler_params=PARAMS,
    )(acc, above, below, *query)


def window_tables(tile_valid, width_shift, first_row):
    frames, _, cols = tile_valid.shape
    shift_own = lax.dynamic_slice_in_dim(width_shift, first_row, 2, 1)
    first = jnp.clip(jnp.arange(cols) + shift_own - 1, 0, cols - SPAN)
    valid = lax.dynamic_slice_in_dim(
        jnp.pad(tile_valid, ((0, 0), (1, 1), (2, 2))), first_row, 4, 1
    )
    near = jnp.stack([valid[:, n : n + 2] for n in range(3)])[:, :, None]
    moved = jnp.stack([near[..., d : d + cols] for d in range(5)])
    shift = first - (jnp.arange(cols) - 1)
    chosen = jnp.where(shift == -1, moved[0:3], jnp.where(shift == 0, moved[1:4], moved[2:5]))
    place_of = jnp.arange(3).reshape(-1, 1, 1, 1, 1, 1)
    near_of = jnp.arange(3).reshape(1, -1, 1, 1, 1, 1)
    key_frame = jnp.arange(frames).reshape(1, 1, -1, 1, 1, 1)
    frame = jnp.arange(frames).reshape(1, 1, 1, -1, 1, 1)
    own = (near_of == 1) & (key_frame == frame) & (place_of + shift == 1)
    bias = jnp.where((chosen == 1) | own, 0.0, MASKED_SCORE).astype(jnp.float32)
    bias = bias.transpose(4, 5, 1, 2, 0, 3).reshape(2, cols, 3 * frames * SPAN, frames, 1)
    bias = jnp.broadcast_to(bias, bias.shape[:4] + (TILE**3,))
    return (
        first.transpose(1, 2, 0).reshape(-1),
        bias.reshape(2, cols, 3 * frames * SPAN, frames * TILE**3),
    )


def place_shards(queries, key_states, value_states, out_grad, tile_valid, width_shift):
    frames = tile_valid.shape[0]
    places = frames * TILE
    turns = HEADS // places
    seq_count = lax.axis_size("seq")
    heights = lax.axis_size("height")
    seq_index = lax.axis_index("seq")
    place = (lax.axis_index("tm") * TILE + seq_index // 2).reshape(1)
    first_row = lax.axis_index("height") * TH_DEV + seq_index % 2 * 2
    starts, bias = window_tables(tile_valid, width_shift, first_row)
    chain = [
        [h * seq_count + frame * 2 + half for h in range(heights) for half in range(2)]
        for frame in range(TILE)
    ]
    down = [pair for line in chain for pair in zip(line[:-1], line[1:])]
    up = [(b, a) for a, b in down]

    def send(block, k):
        return lax.ppermute(block, ("tm", "seq"), [(i, i ^ (2 * k)) for i in range(2 * places)])

    def step(block, route):
        return lax.ppermute(block, ("height", "seq"), route)

    def exchange(blocks, order):
        moved = dict(enumerate(blocks))
        for k in order:
            moved[k] = send(blocks[k], k)
        return [moved[k] for k in range(places)]

    natural = list(range(1, places))
    far, near = [k for k in natural if k & 2], [k for k in natural if not k & 2]
    held = [far[-1], near[0]]
    mixed = far[:-1] + near[1:] + held

    def after(blocks, results):
        kept, results = lax.optimization_barrier(([blocks[k] for k in held], results))
        blocks = list(blocks)
        for k, block in zip(held, kept):
            blocks[k] = block
        return blocks, results

    def ordered(first, then):
        return lax.optimization_barrier((first, then))

    def ordered(first, then):
        return lax.optimization_barrier((first, then))

    def ordered(first, then):
        return lax.optimization_barrier((first, then))

    arrays = (key_states, value_states, queries, out_grad)
    outs = ()
    groups = [exchange(split_heads(places, 0, place, arrays), natural)]
    leaving = None
    for turn in range(turns):
        more = turn + 1 < turns
        if more:
            coming = split_heads(places, turn + 1, place, arrays)
            groups[-1][1:6], coming = ordered(groups[-1][1:6], coming)
        first, last = edge_rows(places, groups[0])
        grads = head_grads(places, place, starts, bias, groups, step(last, down), step(first, up))
        if leaving is not None:
            leaving, grads = after(leaving, grads)
            left = exchange(leaving, mixed)
            passed, grads = ordered([left[k] for k in mixed[:-2]], grads)
            for k, block in zip(mixed, passed):
                left[k] = block
            outs = join_heads(range(places), turn - 1, turns, place, left, outs)
        if more:
            coming, grads = after(coming, grads)
            groups = [exchange(coming, mixed)]
        dq, acc, above, below = grads
        leaving = finish_pairs(places, acc, step(below, down), step(above, up), dq)
    left = exchange(leaving, natural)
    for seats in (range(places - 2), range(places - 2, places)):
        outs = join_heads(seats, turns - 1, turns, place, [left[k] for k in seats], outs)
    key_out, value_out, query_out = outs
    return query_out, key_out, value_out


def solution(mesh):
    frames, seq_count = mesh.shape["tm"], mesh.shape["seq"]
    by_place = frames == 2 and seq_count == 2 * TILE
    placed = (
        P(("tm", "height", "seq"), None),
        P(("tm", "height", "seq"), None),
        P(("tm", "height", "seq"), None),
        P(("tm", "height", "seq"), None),
        P(),
        P(),
    )
    return jax.shard_map(
        place_shards if by_place else shards,
        mesh=mesh,
        in_specs=placed,
        out_specs=(
            P(("tm", "height", "seq"), None),
            P(("tm", "height", "seq"), None),
            P(("tm", "height", "seq"), None),
        ),
        check_vma=False,
    )
```

```python
from functools import partial

import jax
import jax.numpy as jnp
from jax import lax
from jax.experimental import pallas as pl
from jax.experimental.pallas import tpu as pltpu
from jax.sharding import PartitionSpec as P

D_HEAD = 128
HEADS = 16
TILE = 4
TH_DEV = 4
TW = 16


MASKED_SCORE = -1e30


def passed_along(block, axis, distance):
    devices = range(lax.axis_size(axis))
    route = [((i - distance) % len(devices), i) for i in devices]
    return lax.ppermute(block, axis, route)


def with_halo(cells, sides, width):
    for axis, dim in sides:
        count = lax.axis_size(axis)
        ends = count - 1
        head = lax.slice_in_dim(cells, 0, width, axis=dim)
        tail = lax.slice_in_dim(cells, cells.shape[dim] - width, cells.shape[dim], axis=dim)
        cells = jnp.concatenate(
            [
                lax.ppermute(tail, axis, [(i, (i + 1) % count) for i in range(ends)]),
                cells,
                lax.ppermute(head, axis, [((i + 1) % count, i) for i in range(ends)]),
            ],
            axis=dim,
        )
    return cells


def shifted(value, axis, steps):
    count = lax.axis_size(axis)
    initial, last = (max(0, -steps), min(count, count - steps))
    return lax.ppermute(value, axis, [(source, source + steps) for source in range(initial, last)])


def to_tiles(grid_in, tile_edge):
    groups, frames, grid_rows, grid_cols = grid_in.shape[:4]
    trailing = grid_in.shape[4:]
    split_grid = grid_in.reshape(
        (
            groups,
            frames // tile_edge,
            tile_edge,
            grid_rows // tile_edge,
            tile_edge,
            grid_cols // tile_edge,
            tile_edge,
        )
        + trailing
    )
    axis_order = (0, 1, 3, 5, 2, 4, 6) + tuple(range(7, 7 + len(trailing)))
    return split_grid.transpose(axis_order).reshape(
        (groups, frames // tile_edge, grid_rows // tile_edge, grid_cols // tile_edge, tile_edge**3)
        + trailing
    )


def from_tiles(tiles_in, tile_edge):
    groups, frame_tiles, row_tiles, col_tiles = tiles_in.shape[:4]
    trailing = tiles_in.shape[5:]
    split_grid = tiles_in.reshape(
        (groups, frame_tiles, row_tiles, col_tiles, tile_edge, tile_edge, tile_edge) + trailing
    )
    axis_order = (0, 1, 4, 2, 5, 3, 6) + tuple(range(7, 7 + len(trailing)))
    return split_grid.transpose(axis_order).reshape(
        (groups, frame_tiles * tile_edge, row_tiles * tile_edge, col_tiles * tile_edge) + trailing
    )


def edge_tiles(piece_own, half_index):
    return jnp.where(half_index == 0, piece_own[:, :, :, -2:], piece_own[:, :, :, :2])


def widen_rim(piece_own, received, half_index):
    left_side = jnp.concatenate([piece_own, received], axis=3)
    right_side = jnp.concatenate([received, piece_own], axis=3)
    return jnp.where(half_index == 0, left_side, right_side)


def shards(queries, key_states, value_states, out_grad, tile_valid, width_shift):
    seq_count = lax.axis_size("seq")
    groups = 2 * HEADS // seq_count
    half_width = TW * TILE // 2
    lines_dev = queries.shape[0] // (TW * TILE)
    tiles_half = TW // 2
    tile_cells = TILE**3
    score_scale = D_HEAD ** (-0.5)
    time_index = lax.axis_index("tm")
    height_index = lax.axis_index("height")
    half_index = lax.axis_index("seq") * groups // HEADS
    anchor = half_index * (tiles_half - 2)

    def to_heads(rows_in):
        split_rows = rows_in.reshape(lines_dev, 2, half_width, HEADS, D_HEAD)
        return split_rows.transpose(1, 3, 0, 2, 4).reshape(2 * HEADS, lines_dev, half_width, D_HEAD)

    moved = (
        lax.all_to_all(to_heads(queries), "seq", split_axis=0, concat_axis=1, tiled=True),
        lax.all_to_all(to_heads(key_states), "seq", split_axis=0, concat_axis=1, tiled=True),
        lax.all_to_all(to_heads(value_states), "seq", split_axis=0, concat_axis=1, tiled=True),
        lax.all_to_all(to_heads(out_grad), "seq", split_axis=0, concat_axis=1, tiled=True),
    )

    def own_tiles(grid_part):
        return to_tiles(grid_part.reshape(groups, TILE, TILE * TH_DEV, half_width, D_HEAD), TILE)

    query_own, keys_own, values_own, grads_own = [own_tiles(grid_part) for grid_part in moved]
    key_edges = passed_along(
        (edge_tiles(keys_own, half_index), edge_tiles(values_own, half_index)),
        "seq",
        seq_count // 2,
    )
    keys_wide = widen_rim(keys_own, key_edges[0], half_index)
    values_wide = widen_rim(values_own, key_edges[1], half_index)
    keys_ext, values_ext = (
        with_halo(keys_wide, (("tm", 1), ("height", 2)), 1),
        with_halo(values_wide, (("tm", 1), ("height", 2)), 1),
    )
    table_start = (time_index, height_index * TH_DEV, anchor)
    table_span = (3, TH_DEV + 2, tiles_half + 2)
    table_pad = ((1, 1), (1, 1), (0, 0))
    valid_ext = lax.dynamic_slice(jnp.pad(tile_valid, table_pad), table_start, table_span)
    shift_ext = lax.dynamic_slice(jnp.pad(width_shift, table_pad), table_start, table_span)
    triple = jnp.arange(3)
    query_cols = jnp.arange(tiles_half) + 2 * half_index

    def query_row(keep_grads, carry, row_index):
        query_tiles = lax.dynamic_index_in_dim(query_own[:, 0], row_index, 1, keepdims=False)
        grad_tiles = lax.dynamic_index_in_dim(grads_own[:, 0], row_index, 1, keepdims=False)
        key_rows = lax.dynamic_slice_in_dim(keys_ext, row_index, 3, 2)
        value_rows = lax.dynamic_slice_in_dim(values_ext, row_index, 3, 2)
        shift_row = lax.dynamic_index_in_dim(shift_ext[1], row_index + 1, 0, keepdims=False)
        starts = query_cols + lax.dynamic_slice_in_dim(shift_row, 2 * half_index, tiles_half) - 1
        window_cols = starts[:, None] + triple[None, :]
        key_win = key_rows[:, :, :, window_cols].transpose(0, 3, 1, 2, 4, 5, 6)
        key_win = key_win.reshape(groups, tiles_half, 27 * tile_cells, D_HEAD)
        value_win = value_rows[:, :, :, window_cols].transpose(0, 3, 1, 2, 4, 5, 6)
        value_win = value_win.reshape(groups, tiles_half, 27 * tile_cells, D_HEAD)
        valid_rows = lax.dynamic_slice_in_dim(valid_ext, row_index, 3, 1)[:, :, window_cols]
        own_tile = (
            (triple[:, None, None, None] == 1)
            & (triple[None, :, None, None] == 1)
            & (window_cols[None, None] == query_cols[None, None, :, None])
        )
        allowed = ((valid_rows == 1) | own_tile).transpose(2, 0, 1, 3)
        tile_bias = jnp.where(allowed.reshape(tiles_half, 27, 1), 0.0, MASKED_SCORE).astype(
            jnp.float32
        )
        mask_bias = jnp.broadcast_to(tile_bias, (tiles_half, 27, tile_cells)).reshape(
            1, tiles_half, 1, 27 * tile_cells
        )
        scores = (
            score_scale
            * jnp.einsum(
                "gwid,gwjd->gwij", query_tiles, key_win, preferred_element_type=jnp.float32
            )
            + mask_bias
        )
        row_max = jnp.max(scores, axis=-1, keepdims=True)
        probs = jnp.exp(scores - row_max)
        exp_total = jnp.sum(probs, axis=-1, keepdims=True)
        log_total = row_max + jnp.log(exp_total)
        weights = probs / exp_total
        grad_weights = jnp.einsum(
            "gwid,gwjd->gwij", grad_tiles, value_win, preferred_element_type=jnp.float32
        )
        delta_row = jnp.sum(weights * grad_weights, axis=-1, keepdims=True)
        dscore = (weights * (grad_weights - delta_row)).astype(jnp.bfloat16)
        query_part = score_scale * jnp.einsum(
            "gwij,gwjd->gwid", dscore, key_win, preferred_element_type=jnp.float32
        )
        key_acc, value_acc = carry
        key_part = score_scale * jnp.einsum(
            "gwij,gwid->gwjd", dscore, query_tiles, preferred_element_type=jnp.float32
        )
        value_part = jnp.einsum(
            "gwij,gwid->gwjd",
            weights.astype(jnp.bfloat16),
            grad_tiles,
            preferred_element_type=jnp.float32,
        )
        time_pick = triple[None, :, None, None]
        row_pick = triple[None, None, :, None]
        col_pick = window_cols[:, None, None, :]

        def spread(acc_grid, part_grad):
            shaped = part_grad.reshape(groups, tiles_half, 3, 3, 3, tile_cells, D_HEAD)
            rows_now = lax.dynamic_slice_in_dim(acc_grid, row_index, 3, 2)
            rows_now = rows_now.at[:, time_pick, row_pick, col_pick].add(shaped)
            return lax.dynamic_update_slice_in_dim(acc_grid, rows_now, row_index, 2)

        carry = (spread(key_acc, key_part), spread(value_acc, value_part))
        return (carry, (query_part, log_total[..., 0], delta_row[..., 0]))

    zero_grads = jnp.zeros(keys_ext.shape, jnp.float32)
    (key_acc, value_acc), row_outputs = lax.scan(
        partial(query_row, True), (zero_grads, zero_grads), jnp.arange(TH_DEV)
    )
    from_below = (
        shifted(key_acc[:, :, -1:].astype(jnp.bfloat16), "height", 1).astype(jnp.float32),
        shifted(value_acc[:, :, -1:].astype(jnp.bfloat16), "height", 1).astype(jnp.float32),
    )
    from_above = (
        shifted(key_acc[:, :, :1].astype(jnp.bfloat16), "height", -1).astype(jnp.float32),
        shifted(value_acc[:, :, :1].astype(jnp.bfloat16), "height", -1).astype(jnp.float32),
    )

    def fold_rows(acc_grid, lower_in, upper_in):
        acc_grid = acc_grid.at[:, :, 1:2].add(lower_in)
        acc_grid = acc_grid.at[:, :, TH_DEV : TH_DEV + 1].add(upper_in)
        return acc_grid[:, :, 1 : TH_DEV + 1]

    key_core = fold_rows(key_acc, from_below[0], from_above[0])
    value_core = fold_rows(value_acc, from_below[1], from_above[1])
    from_before = shifted((key_core[:, 2:3], value_core[:, 2:3]), "tm", 1)
    from_after = shifted((key_core[:, 0:1], value_core[:, 0:1]), "tm", -1)
    key_mid = key_core[:, 1] + from_before[0][:, 0] + from_after[0][:, 0]
    value_mid = value_core[:, 1] + from_before[1][:, 0] + from_after[1][:, 0]

    def rim_of(mid_grid):
        return jnp.where(half_index == 0, mid_grid[:, :, -2:], mid_grid[:, :, :2])

    rim_back = (
        passed_along(rim_of(key_mid).astype(jnp.bfloat16), "seq", seq_count // 2).astype(
            jnp.float32
        ),
        passed_along(rim_of(value_mid).astype(jnp.bfloat16), "seq", seq_count // 2).astype(
            jnp.float32
        ),
    )

    def settle(mid_grid, received):
        left_side = jnp.concatenate(
            [
                mid_grid[:, :, : tiles_half - 2],
                mid_grid[:, :, tiles_half - 2 : tiles_half] + received,
            ],
            axis=2,
        )
        right_side = jnp.concatenate([mid_grid[:, :, 2:4] + received, mid_grid[:, :, 4:]], axis=2)
        return jnp.where(half_index == 0, left_side, right_side)

    key_grid = from_tiles(settle(key_mid, rim_back[0])[:, None], TILE).astype(jnp.bfloat16)
    value_grid = from_tiles(settle(value_mid, rim_back[1])[:, None], TILE).astype(jnp.bfloat16)
    query_grid = from_tiles(jnp.moveaxis(row_outputs[0], 0, 1)[:, None], TILE).astype(jnp.bfloat16)

    def to_lines(grid_part):
        return grid_part.reshape(groups, TILE * TILE * TH_DEV, half_width, D_HEAD)

    returned = (
        lax.all_to_all(to_lines(query_grid), "seq", split_axis=1, concat_axis=0, tiled=True),
        lax.all_to_all(to_lines(key_grid), "seq", split_axis=1, concat_axis=0, tiled=True),
        lax.all_to_all(to_lines(value_grid), "seq", split_axis=1, concat_axis=0, tiled=True),
    )

    def to_rows(grid_part):
        split_rows = grid_part.reshape(2, HEADS, lines_dev, half_width, D_HEAD)
        return split_rows.transpose(2, 0, 3, 1, 4).reshape(
            lines_dev * 2 * half_width, HEADS * D_HEAD
        )

    return (to_rows(returned[0]), to_rows(returned[1]), to_rows(returned[2]))


TOK = TILE * TILE
SPAN = 3
SLOTS = 4
PLAN = ((1, 0), (1, 1), (1, 2), (1, 3), (2, 0), (2, 1), (2, 2), (2, 3), (3, 0), (3, 1), (3, 2), (3, 3))
LANES = 2 * D_HEAD
LINES = TW * TOK
LOG2_E = 1.4426950408889634
VMEM_BYTES = 56 * 1024 * 1024
NT = (((1,), (1,)), ((), ()))
NN = (((1,), (0,)), ((), ()))
TN = (((0,), (0,)), ((), ()))
ANYWHERE = pl.BlockSpec(memory_space=pl.ANY)
SCALARS = pl.BlockSpec(memory_space=pltpu.SMEM)
WHOLE = pl.BlockSpec(memory_space=pltpu.VMEM)
PARAMS = pltpu.CompilerParams(vmem_limit_bytes=VMEM_BYTES)


def row_order(inverse):
    target = lax.broadcasted_iota(jnp.int32, (LINES, LINES), 0)
    source = lax.broadcasted_iota(jnp.int32, (LINES, LINES), 1)
    if inverse:
        target, source = source, target
    col, line, x = target // TOK, (target // TILE) % TILE, target % TILE
    return (source == line * (TW * TILE) + col * TILE + x).astype(jnp.bfloat16)


def split_kernel(seats, turn, turns, pairs, place_ref, *refs):
    count = len(seats)
    arrays, outs = refs[: 2 * pairs], refs[2 * pairs : 2 * pairs + count]
    taken, ready, in_sem, out_sem = refs[2 * pairs + count :]
    loads = []
    for k in range(count):
        first = pl.multiple_of(((place_ref[0] ^ seats[k]) * turns + turn) * D_HEAD, D_HEAD)
        loads.append(
            [
                pltpu.make_async_copy(
                    ref.at[:, pl.ds(first, D_HEAD)], taken.at[k, which], in_sem.at[k, which]
                )
                for which, ref in enumerate(arrays)
            ]
        )
        for copy in loads[k]:
            copy.start()
    order = row_order(False)
    stores = []
    for k in range(count):
        for copy in loads[k]:
            copy.wait()
        for pair in range(pairs):
            for row in range(2):
                lines = slice(row * LINES, (row + 1) * LINES)
                rows = jnp.concatenate(
                    [taken[k, 2 * pair, lines, :], taken[k, 2 * pair + 1, lines, :]], axis=1
                )
                moved = lax.dot_general(order, rows, NN, preferred_element_type=jnp.float32)
                ready[k, pair, row] = moved.astype(jnp.bfloat16)
        stores.append(pltpu.make_async_copy(ready.at[k], outs[k], out_sem.at[k]))
        stores[k].start()
    for copy in stores:
        copy.wait()


def split_heads(seats, turn, turns, place, arrays):
    count, rows, pairs = len(seats), arrays[0].shape[0], len(arrays) // 2
    return pl.pallas_call(
        lambda *refs: split_kernel(seats, turn, turns, pairs, *refs),
        in_specs=[SCALARS] + [ANYWHERE] * (2 * pairs),
        out_specs=[ANYWHERE] * count,
        out_shape=[jax.ShapeDtypeStruct((pairs, 2, LINES, LANES), jnp.bfloat16)] * count,
        scratch_shapes=[
            pltpu.VMEM((count, 2 * pairs, rows, D_HEAD), jnp.bfloat16),
            pltpu.VMEM((count, pairs, 2, LINES, LANES), jnp.bfloat16),
            pltpu.SemaphoreType.DMA((count, 2 * pairs)),
            pltpu.SemaphoreType.DMA((count,)),
        ],
        compiler_params=PARAMS,
    )(place, *arrays)


def join_kernel(seats, turn, turns, kept, place_ref, *refs):
    count = len(seats)
    blocks, outs = refs[:count], refs[count + kept : count + kept + 3]
    taken, ready, in_sem, out_sem = refs[count + kept + 3 :]
    loads = []
    for n in range(count):
        loads.append(pltpu.make_async_copy(blocks[n], taken.at[n], in_sem.at[n]))
        loads[n].start()
    order = row_order(True)
    stores = []
    for n, k in enumerate(seats):
        loads[n].wait()
        for row in range(2):
            back = lax.dot_general(
                order, taken[n, row], NN, preferred_element_type=jnp.float32
            ).astype(jnp.bfloat16)
            for which in range(3):
                ready[n, which, row * LINES : (row + 1) * LINES, :] = back[
                    :, which * D_HEAD : (which + 1) * D_HEAD
                ]
        first = pl.multiple_of(((place_ref[0] ^ k) * turns + turn) * D_HEAD, D_HEAD)
        for which in range(3):
            copy = pltpu.make_async_copy(
                ready.at[n, which], outs[which].at[:, pl.ds(first, D_HEAD)], out_sem.at[n, which]
            )
            copy.start()
            stores.append(copy)
    for copy in stores:
        copy.wait()


def join_heads(seats, turn, turns, place, blocks, earlier):
    count, rows, lanes = len(seats), 2 * LINES, blocks[0].shape[-1]
    return pl.pallas_call(
        lambda *refs: join_kernel(seats, turn, turns, len(earlier), *refs),
        in_specs=[SCALARS] + [ANYWHERE] * (count + len(earlier)),
        out_specs=[ANYWHERE] * 3,
        out_shape=[jax.ShapeDtypeStruct((rows, HEADS * D_HEAD), jnp.bfloat16)] * 3,
        scratch_shapes=[
            pltpu.VMEM((count, 2, LINES, lanes), jnp.bfloat16),
            pltpu.VMEM((count, 3, rows, D_HEAD), jnp.bfloat16),
            pltpu.SemaphoreType.DMA((count,)),
            pltpu.SemaphoreType.DMA((count, 3)),
        ],
        input_output_aliases={1 + count + n: n for n in range(len(earlier))},
        compiler_params=PARAMS,
    )(place, *blocks, *earlier)


def edge_kernel(places, *refs):
    blocks, (first_ref, last_ref), sem = refs[:places], refs[places : places + 2], refs[-1]
    copies = []
    for k in range(places):
        for row, ref in enumerate((first_ref, last_ref)):
            copies.append(pltpu.make_async_copy(blocks[k].at[0, row], ref.at[k], sem.at[k, row]))
    for copy in copies:
        copy.start()
    for copy in copies:
        copy.wait()


def edge_rows(places, blocks):
    return pl.pallas_call(
        lambda *refs: edge_kernel(places, *refs),
        in_specs=[ANYWHERE] * places,
        out_specs=[WHOLE] * 2,
        out_shape=[jax.ShapeDtypeStruct((places, LINES, LANES), jnp.bfloat16)] * 2,
        scratch_shapes=[pltpu.SemaphoreType.DMA((places, 2))],
        compiler_params=PARAMS,
    )(*blocks)


def grad_kernel(places, count, place_ref, start_ref, bias_ref, *refs):
    groups = [refs[n * places : (n + 1) * places] for n in range(count)]
    (from_above, from_below), outs = refs[count * places :][:2], refs[count * places + 2 :]
    dq_refs, acc_out, above_ref, below_ref = outs[:places], *outs[places : places + 3]
    kv, own_rows, acc, dq, scores, low, in_sem, halo_sem, out_sem = outs[places + 3 :]
    frames = places // TILE
    scale = D_HEAD**-0.5
    copies = []
    for k in range(places):
        seat = place_ref[0] ^ k
        spot = (seat // TILE, seat % TILE)
        copies += [
            pltpu.make_async_copy(groups[0][k].at[0], kv.at[pl.ds(1, 2), *spot], in_sem.at[k, 0]),
            pltpu.make_async_copy(groups[-1][k].at[2 - count], own_rows.at[:, *spot], in_sem.at[k, 1]),
            pltpu.make_async_copy(from_above.at[k], kv.at[0, *spot], halo_sem.at[k, 0]),
            pltpu.make_async_copy(from_below.at[k], kv.at[3, *spot], halo_sem.at[k, 1]),
        ]
    for copy in copies:
        copy.start()
    acc[...] = jnp.zeros(acc.shape, acc.dtype)
    for copy in copies:
        copy.wait()
    part = places * SPAN * TOK
    piece = SPAN * TOK

    def diagonal(own):
        cells = own.shape[0] // frames
        blank = jnp.zeros((cells, D_HEAD), own.dtype)
        lines = []
        for frame in range(frames):
            line = [blank] * frames
            line[frame] = own[frame * cells : (frame + 1) * cells, :]
            lines.append(jnp.concatenate(line, axis=1))
        return jnp.concatenate(lines, axis=0)

    def near_keys(row, near, windows, lanes):
        return jnp.concatenate(
            [kv[row + near, :, :, window, lanes].reshape(part, D_HEAD) for window in windows],
            axis=1,
        )

    def score_phase(slot, row, col):
        here = pl.multiple_of(col * TOK, TOK)
        windows = [
            pl.ds(pl.multiple_of(start_ref[(row * TW + col) * frames + f] * TOK, TOK), piece)
            for f in range(frames)
        ]
        own = own_rows[row, :, :, pl.ds(here, TOK), :].reshape(-1, LANES)
        query, grad = diagonal(own[:, :D_HEAD]), diagonal(own[:, D_HEAD:])
        top = None
        for near in range(3):
            score_raw = lax.dot_general(
                near_keys(row, near, windows, slice(0, D_HEAD)), query, NT,
                preferred_element_type=jnp.float32,
            )
            scores[slot, near, :, D_HEAD:] = lax.dot_general(
                near_keys(row, near, windows, slice(D_HEAD, LANES)), grad, NT,
                preferred_element_type=jnp.float32,
            )
            for frame in range(frames):
                first = (near * frames + frame) * SPAN
                bias = jnp.concatenate(
                    [
                        jnp.broadcast_to(
                            bias_ref[row, col, first + c : first + c + 1, :], (TOK, D_HEAD)
                        )
                        for c in range(SPAN)
                    ],
                    axis=0,
                )
                for sub in range(TILE):
                    at = (frame * TILE + sub) * piece
                    score = score_raw[at : at + piece, :] * (scale * LOG2_E) + bias
                    scores[slot, near, at : at + piece, :D_HEAD] = score
                    most = jnp.max(score.reshape(-1, 8, D_HEAD), axis=0)
                    top = most if top is None else jnp.maximum(top, most)
        return here, windows, query, grad, jnp.max(top, axis=0, keepdims=True)

    def total_phase(slot, top):
        total = jnp.zeros((8, D_HEAD), jnp.float32)
        delta = jnp.zeros((8, D_HEAD), jnp.float32)
        for near in range(3):
            for at in range(0, part, piece):
                prob = jnp.exp2(scores[slot, near, at : at + piece, :D_HEAD] - top)
                total = total + jnp.sum(prob.reshape(-1, 8, D_HEAD), axis=0)
                grad = prob * scores[slot, near, at : at + piece, D_HEAD:]
                delta = delta + jnp.sum(grad.reshape(-1, 8, D_HEAD), axis=0)
        total = jnp.sum(total, axis=0, keepdims=True)
        delta = jnp.sum(delta, axis=0, keepdims=True) / total
        return top + jnp.log2(total), delta

    def grad_phase(slot, row, here, windows, query, grad, log_total, delta):
        query_grad = None
        for near in range(3):
            for at in range(0, part, piece):
                weight = jnp.exp2(scores[slot, near, at : at + piece, :D_HEAD] - log_total)
                dscore = weight * (scores[slot, near, at : at + piece, D_HEAD:] - delta)
                low[slot, near, at : at + piece, :D_HEAD] = dscore.astype(jnp.bfloat16)
                low[slot, near, at : at + piece, D_HEAD:] = weight.astype(jnp.bfloat16)
            key_part = lax.dot_general(
                low[slot, near, :, :D_HEAD], query, NN, preferred_element_type=jnp.float32
            )
            value_part = lax.dot_general(
                low[slot, near, :, D_HEAD:], grad, NN, preferred_element_type=jnp.float32
            )
            for f in range(frames):
                lanes = slice(f * D_HEAD, (f + 1) * D_HEAD)
                added = jnp.concatenate([key_part[:, lanes], value_part[:, lanes]], axis=1)
                spot = (row + near, slice(None), slice(None), windows[f], slice(None))
                acc[spot] = acc[spot] + added.reshape(frames, TILE, piece, LANES)
            more = lax.dot_general(
                low[slot, near, :, :D_HEAD],
                near_keys(row, near, windows, slice(0, D_HEAD)),
                TN,
                preferred_element_type=jnp.float32,
            )
            query_grad = more if query_grad is None else query_grad + more
        for f in range(frames):
            cells = query_grad.shape[0] // frames
            mine = query_grad[f * cells : (f + 1) * cells, f * D_HEAD : (f + 1) * D_HEAD]
            dq[row, f, :, pl.ds(here, TOK), :] = (
                (mine * scale).astype(jnp.bfloat16).reshape(TILE, TOK, D_HEAD)
            )

    def group(step, _):
        known, sums = {}, {}
        for phase, slot in PLAN:
            row = slot % 2
            if phase == 1:
                known[slot] = score_phase(slot, row, step * (SLOTS // 2) + slot // 2)
            elif phase == 2:
                sums[slot] = total_phase(slot, known[slot][-1])
            else:
                grad_phase(slot, row, *known[slot][:-1], *sums[slot])
        return 0

    lax.fori_loop(0, 2 * TW // SLOTS, group, 0)
    copies = []
    for k in range(places):
        seat = place_ref[0] ^ k
        spot = (seat // TILE, seat % TILE)
        copies += [
            pltpu.make_async_copy(dq.at[:, *spot], dq_refs[k], out_sem.at[k, 0]),
            pltpu.make_async_copy(acc.at[pl.ds(1, 2), *spot], acc_out.at[k], out_sem.at[k, 1]),
        ]
    for copy in copies:
        copy.start()
    for k in range(places):
        seat = place_ref[0] ^ k
        spot = (seat // TILE, seat % TILE)
        above_ref[k] = acc[0, *spot].astype(jnp.bfloat16)
        below_ref[k] = acc[3, *spot].astype(jnp.bfloat16)
    for copy in copies:
        copy.wait()


def head_grads(places, place, starts, bias, groups, from_above, from_below):
    frames = places // TILE
    part = places * SPAN * TOK
    results = pl.pallas_call(
        lambda *refs: grad_kernel(places, len(groups), *refs),
        in_specs=[SCALARS, SCALARS, WHOLE] + [ANYWHERE] * (len(groups) * places + 2),
        out_specs=[ANYWHERE] * (places + 1) + [WHOLE] * 2,
        out_shape=[jax.ShapeDtypeStruct((2, LINES, D_HEAD), jnp.bfloat16)] * places
        + [jax.ShapeDtypeStruct((places, 2, LINES, LANES), jnp.float32)]
        + [jax.ShapeDtypeStruct((places, LINES, LANES), jnp.bfloat16)] * 2,
        scratch_shapes=[
            pltpu.VMEM((4, frames, TILE, LINES, LANES), jnp.bfloat16),
            pltpu.VMEM((2, frames, TILE, LINES, LANES), jnp.bfloat16),
            pltpu.VMEM((4, frames, TILE, LINES, LANES), jnp.float32),
            pltpu.VMEM((2, frames, TILE, LINES, D_HEAD), jnp.bfloat16),
            pltpu.VMEM((SLOTS, 3, part, LANES), jnp.float32),
            pltpu.VMEM((SLOTS, 3, part, LANES), jnp.bfloat16),
            pltpu.SemaphoreType.DMA((places, 2)),
            pltpu.SemaphoreType.DMA((places, 2)),
            pltpu.SemaphoreType.DMA((places, 2)),
        ],
        compiler_params=PARAMS,
        cost_estimate=pl.CostEstimate(
            flops=1_000_000, bytes_accessed=0, transcendentals=0
        ),
    )(place, starts, bias, *[block for group in groups for block in group], from_above, from_below)
    return results[:places], *results[places:]


def finish_kernel(count, acc_ref, above_ref, below_ref, *refs):
    queries, outs = refs[:count], refs[count:]
    lane = lax.broadcasted_iota(jnp.int32, (1, LANES), 1)
    factor = jnp.where(lane < D_HEAD, D_HEAD**-0.5, 1.0)
    for k in range(count):
        for row, ref in enumerate((above_ref, below_ref)):
            total = acc_ref[k, row] + ref[k].astype(jnp.float32)
            outs[k][row, :, :LANES] = (total * factor).astype(jnp.bfloat16)
        outs[k][:, :, LANES:] = queries[k][...]


def finish_pairs(seats, acc, above, below, query):
    count, lanes = len(seats), LANES + D_HEAD
    at = seats[0] // count
    halo = pl.BlockSpec((count, LINES, LANES), lambda g: (at, 0, 0))
    block = pl.BlockSpec((2, LINES, D_HEAD), lambda g: (0, 0, 0))
    return pl.pallas_call(
        lambda *refs: finish_kernel(count, *refs),
        grid=(1,),
        in_specs=[pl.BlockSpec((count, 2, LINES, LANES), lambda g: (at, 0, 0, 0)), halo, halo]
        + [block] * count,
        out_specs=[pl.BlockSpec((2, LINES, lanes), lambda g: (0, 0, 0))] * count,
        out_shape=[jax.ShapeDtypeStruct((2, LINES, lanes), jnp.bfloat16)] * count,
        compiler_params=PARAMS,
    )(acc, above, below, *[query[k] for k in seats])


def window_tables(tile_valid, width_shift, first_row):
    frames, _, cols = tile_valid.shape
    shift_own = lax.dynamic_slice_in_dim(width_shift, first_row, 2, 1)
    first = jnp.clip(jnp.arange(cols) + shift_own - 1, 0, cols - SPAN)
    valid = lax.dynamic_slice_in_dim(
        jnp.pad(tile_valid, ((0, 0), (1, 1), (2, 2))), first_row, 4, 1
    )
    near = jnp.stack([valid[:, n : n + 2] for n in range(3)])[:, :, None]
    moved = jnp.stack([near[..., d : d + cols] for d in range(5)])
    shift = first - (jnp.arange(cols) - 1)
    chosen = jnp.where(shift == -1, moved[0:3], jnp.where(shift == 0, moved[1:4], moved[2:5]))
    place_of = jnp.arange(3).reshape(-1, 1, 1, 1, 1, 1)
    near_of = jnp.arange(3).reshape(1, -1, 1, 1, 1, 1)
    key_frame = jnp.arange(frames).reshape(1, 1, -1, 1, 1, 1)
    frame = jnp.arange(frames).reshape(1, 1, 1, -1, 1, 1)
    own = (near_of == 1) & (key_frame == frame) & (place_of + shift == 1)
    bias = jnp.where((chosen == 1) | own, 0.0, MASKED_SCORE).astype(jnp.float32)
    bias = bias.transpose(4, 5, 1, 2, 0, 3).reshape(2, cols, 3 * frames * SPAN, frames, 1)
    bias = jnp.broadcast_to(bias, bias.shape[:4] + (TILE**3,))
    return (
        first.transpose(1, 2, 0).reshape(-1),
        bias.reshape(2, cols, 3 * frames * SPAN, frames * TILE**3),
    )


def place_shards(queries, key_states, value_states, out_grad, tile_valid, width_shift):
    frames = tile_valid.shape[0]
    places = frames * TILE
    turns = HEADS // places
    seq_count = lax.axis_size("seq")
    heights = lax.axis_size("height")
    seq_index = lax.axis_index("seq")
    place = (lax.axis_index("tm") * TILE + seq_index // 2).reshape(1)
    first_row = lax.axis_index("height") * TH_DEV + seq_index % 2 * 2
    starts, bias = window_tables(tile_valid, width_shift, first_row)
    chain = [
        [h * seq_count + frame * 2 + half for h in range(heights) for half in range(2)]
        for frame in range(TILE)
    ]
    down = [pair for line in chain for pair in zip(line[:-1], line[1:])]
    up = [(b, a) for a, b in down]

    def send(block, k):
        return lax.ppermute(block, ("tm", "seq"), [(i, i ^ (2 * k)) for i in range(2 * places)])

    def step(block, route):
        return lax.ppermute(block, ("height", "seq"), route)

    def exchange(blocks, order):
        moved = dict(enumerate(blocks))
        for k in order:
            moved[k] = send(blocks[k], k)
        return [moved[k] for k in range(places)]

    natural = list(range(1, places))
    halves = (range(places // 2), range(places // 2, places))
    far, near = [k for k in natural if k & 2], [k for k in natural if not k & 2]
    held = [far[-1], near[0]]
    mixed = far[:-1] + near[1:] + held

    def after(blocks, results):
        kept, results = lax.optimization_barrier(([blocks[k] for k in held], results))
        blocks = list(blocks)
        for k, block in zip(held, kept):
            blocks[k] = block
        return blocks, results

    def ordered(first, then):
        return lax.optimization_barrier((first, then))

    def ordered(first, then):
        return lax.optimization_barrier((first, then))

    def ordered(first, then):
        return lax.optimization_barrier((first, then))

    arrays = (key_states, value_states, queries, out_grad)
    outs = ()
    blocks = []
    for seats in halves:
        blocks += split_heads(seats, 0, turns, place, arrays)
    groups = [exchange(blocks, natural)]
    leaving = None
    for turn in range(turns):
        more = turn + 1 < turns
        if more:
            coming = split_heads(range(places), turn + 1, turns, place, arrays)
            groups[-1][1:6], coming = ordered(groups[-1][1:6], coming)
        first, last = edge_rows(places, groups[0])
        grads = head_grads(places, place, starts, bias, groups, step(last, down), step(first, up))
        if leaving is not None:
            leaving, grads = after(leaving, grads)
            left = exchange(leaving, mixed)
            passed, grads = ordered([left[k] for k in mixed[:-2]], grads)
            for k, block in zip(mixed, passed):
                left[k] = block
            outs = join_heads(range(places), turn - 1, turns, place, left, outs)
        if more:
            coming, grads = after(coming, grads)
            groups = [exchange(coming, mixed)]
        dq, acc, above, below = grads
        from_above, from_below = step(below, down), step(above, up)
        leaving = []
        for seats in [range(places)]:
            leaving += finish_pairs(seats, acc, from_above, from_below, dq)
    left = exchange(leaving, natural)
    for seats in (range(places - 2), range(places - 2, places)):
        outs = join_heads(seats, turns - 1, turns, place, [left[k] for k in seats], outs)
    key_out, value_out, query_out = outs
    return query_out, key_out, value_out


def solution(mesh):
    frames, seq_count = mesh.shape["tm"], mesh.shape["seq"]
    by_place = frames == 2 and seq_count == 2 * TILE
    placed = (
        P(("tm", "height", "seq"), None),
        P(("tm", "height", "seq"), None),
        P(("tm", "height", "seq"), None),
        P(("tm", "height", "seq"), None),
        P(),
        P(),
    )
    return jax.shard_map(
        place_shards if by_place else shards,
        mesh=mesh,
        in_specs=placed,
        out_specs=(
            P(("tm", "height", "seq"), None),
            P(("tm", "height", "seq"), None),
            P(("tm", "height", "seq"), None),
        ),
        check_vma=False,
    )
```

```python
from functools import partial

import jax
import jax.numpy as jnp
from jax import lax
from jax.experimental import pallas as pl
from jax.experimental.pallas import tpu as pltpu
from jax.sharding import PartitionSpec as P

D_HEAD = 128
HEADS = 16
TILE = 4
TH_DEV = 4
TW = 16


MASKED_SCORE = -1e30


def passed_along(block, axis, distance):
    devices = range(lax.axis_size(axis))
    route = [((i - distance) % len(devices), i) for i in devices]
    return lax.ppermute(block, axis, route)


def with_halo(cells, sides, width):
    for axis, dim in sides:
        count = lax.axis_size(axis)
        ends = count - 1
        head = lax.slice_in_dim(cells, 0, width, axis=dim)
        tail = lax.slice_in_dim(cells, cells.shape[dim] - width, cells.shape[dim], axis=dim)
        cells = jnp.concatenate(
            [
                lax.ppermute(tail, axis, [(i, (i + 1) % count) for i in range(ends)]),
                cells,
                lax.ppermute(head, axis, [((i + 1) % count, i) for i in range(ends)]),
            ],
            axis=dim,
        )
    return cells


def shifted(value, axis, steps):
    count = lax.axis_size(axis)
    initial, last = (max(0, -steps), min(count, count - steps))
    return lax.ppermute(value, axis, [(source, source + steps) for source in range(initial, last)])


def to_tiles(grid_in, tile_edge):
    groups, frames, grid_rows, grid_cols = grid_in.shape[:4]
    trailing = grid_in.shape[4:]
    split_grid = grid_in.reshape(
        (
            groups,
            frames // tile_edge,
            tile_edge,
            grid_rows // tile_edge,
            tile_edge,
            grid_cols // tile_edge,
            tile_edge,
        )
        + trailing
    )
    axis_order = (0, 1, 3, 5, 2, 4, 6) + tuple(range(7, 7 + len(trailing)))
    return split_grid.transpose(axis_order).reshape(
        (groups, frames // tile_edge, grid_rows // tile_edge, grid_cols // tile_edge, tile_edge**3)
        + trailing
    )


def from_tiles(tiles_in, tile_edge):
    groups, frame_tiles, row_tiles, col_tiles = tiles_in.shape[:4]
    trailing = tiles_in.shape[5:]
    split_grid = tiles_in.reshape(
        (groups, frame_tiles, row_tiles, col_tiles, tile_edge, tile_edge, tile_edge) + trailing
    )
    axis_order = (0, 1, 4, 2, 5, 3, 6) + tuple(range(7, 7 + len(trailing)))
    return split_grid.transpose(axis_order).reshape(
        (groups, frame_tiles * tile_edge, row_tiles * tile_edge, col_tiles * tile_edge) + trailing
    )


def edge_tiles(piece_own, half_index):
    return jnp.where(half_index == 0, piece_own[:, :, :, -2:], piece_own[:, :, :, :2])


def widen_rim(piece_own, received, half_index):
    left_side = jnp.concatenate([piece_own, received], axis=3)
    right_side = jnp.concatenate([received, piece_own], axis=3)
    return jnp.where(half_index == 0, left_side, right_side)


def shards(queries, key_states, value_states, out_grad, tile_valid, width_shift):
    seq_count = lax.axis_size("seq")
    groups = 2 * HEADS // seq_count
    half_width = TW * TILE // 2
    lines_dev = queries.shape[0] // (TW * TILE)
    tiles_half = TW // 2
    tile_cells = TILE**3
    score_scale = D_HEAD ** (-0.5)
    time_index = lax.axis_index("tm")
    height_index = lax.axis_index("height")
    half_index = lax.axis_index("seq") * groups // HEADS
    anchor = half_index * (tiles_half - 2)

    def to_heads(rows_in):
        split_rows = rows_in.reshape(lines_dev, 2, half_width, HEADS, D_HEAD)
        return split_rows.transpose(1, 3, 0, 2, 4).reshape(2 * HEADS, lines_dev, half_width, D_HEAD)

    moved = (
        lax.all_to_all(to_heads(queries), "seq", split_axis=0, concat_axis=1, tiled=True),
        lax.all_to_all(to_heads(key_states), "seq", split_axis=0, concat_axis=1, tiled=True),
        lax.all_to_all(to_heads(value_states), "seq", split_axis=0, concat_axis=1, tiled=True),
        lax.all_to_all(to_heads(out_grad), "seq", split_axis=0, concat_axis=1, tiled=True),
    )

    def own_tiles(grid_part):
        return to_tiles(grid_part.reshape(groups, TILE, TILE * TH_DEV, half_width, D_HEAD), TILE)

    query_own, keys_own, values_own, grads_own = [own_tiles(grid_part) for grid_part in moved]
    key_edges = passed_along(
        (edge_tiles(keys_own, half_index), edge_tiles(values_own, half_index)),
        "seq",
        seq_count // 2,
    )
    keys_wide = widen_rim(keys_own, key_edges[0], half_index)
    values_wide = widen_rim(values_own, key_edges[1], half_index)
    keys_ext, values_ext = (
        with_halo(keys_wide, (("tm", 1), ("height", 2)), 1),
        with_halo(values_wide, (("tm", 1), ("height", 2)), 1),
    )
    table_start = (time_index, height_index * TH_DEV, anchor)
    table_span = (3, TH_DEV + 2, tiles_half + 2)
    table_pad = ((1, 1), (1, 1), (0, 0))
    valid_ext = lax.dynamic_slice(jnp.pad(tile_valid, table_pad), table_start, table_span)
    shift_ext = lax.dynamic_slice(jnp.pad(width_shift, table_pad), table_start, table_span)
    triple = jnp.arange(3)
    query_cols = jnp.arange(tiles_half) + 2 * half_index

    def query_row(keep_grads, carry, row_index):
        query_tiles = lax.dynamic_index_in_dim(query_own[:, 0], row_index, 1, keepdims=False)
        grad_tiles = lax.dynamic_index_in_dim(grads_own[:, 0], row_index, 1, keepdims=False)
        key_rows = lax.dynamic_slice_in_dim(keys_ext, row_index, 3, 2)
        value_rows = lax.dynamic_slice_in_dim(values_ext, row_index, 3, 2)
        shift_row = lax.dynamic_index_in_dim(shift_ext[1], row_index + 1, 0, keepdims=False)
        starts = query_cols + lax.dynamic_slice_in_dim(shift_row, 2 * half_index, tiles_half) - 1
        window_cols = starts[:, None] + triple[None, :]
        key_win = key_rows[:, :, :, window_cols].transpose(0, 3, 1, 2, 4, 5, 6)
        key_win = key_win.reshape(groups, tiles_half, 27 * tile_cells, D_HEAD)
        value_win = value_rows[:, :, :, window_cols].transpose(0, 3, 1, 2, 4, 5, 6)
        value_win = value_win.reshape(groups, tiles_half, 27 * tile_cells, D_HEAD)
        valid_rows = lax.dynamic_slice_in_dim(valid_ext, row_index, 3, 1)[:, :, window_cols]
        own_tile = (
            (triple[:, None, None, None] == 1)
            & (triple[None, :, None, None] == 1)
            & (window_cols[None, None] == query_cols[None, None, :, None])
        )
        allowed = ((valid_rows == 1) | own_tile).transpose(2, 0, 1, 3)
        tile_bias = jnp.where(allowed.reshape(tiles_half, 27, 1), 0.0, MASKED_SCORE).astype(
            jnp.float32
        )
        mask_bias = jnp.broadcast_to(tile_bias, (tiles_half, 27, tile_cells)).reshape(
            1, tiles_half, 1, 27 * tile_cells
        )
        scores = (
            score_scale
            * jnp.einsum(
                "gwid,gwjd->gwij", query_tiles, key_win, preferred_element_type=jnp.float32
            )
            + mask_bias
        )
        row_max = jnp.max(scores, axis=-1, keepdims=True)
        probs = jnp.exp(scores - row_max)
        exp_total = jnp.sum(probs, axis=-1, keepdims=True)
        log_total = row_max + jnp.log(exp_total)
        weights = probs / exp_total
        grad_weights = jnp.einsum(
            "gwid,gwjd->gwij", grad_tiles, value_win, preferred_element_type=jnp.float32
        )
        delta_row = jnp.sum(weights * grad_weights, axis=-1, keepdims=True)
        dscore = (weights * (grad_weights - delta_row)).astype(jnp.bfloat16)
        query_part = score_scale * jnp.einsum(
            "gwij,gwjd->gwid", dscore, key_win, preferred_element_type=jnp.float32
        )
        key_acc, value_acc = carry
        key_part = score_scale * jnp.einsum(
            "gwij,gwid->gwjd", dscore, query_tiles, preferred_element_type=jnp.float32
        )
        value_part = jnp.einsum(
            "gwij,gwid->gwjd",
            weights.astype(jnp.bfloat16),
            grad_tiles,
            preferred_element_type=jnp.float32,
        )
        time_pick = triple[None, :, None, None]
        row_pick = triple[None, None, :, None]
        col_pick = window_cols[:, None, None, :]

        def spread(acc_grid, part_grad):
            shaped = part_grad.reshape(groups, tiles_half, 3, 3, 3, tile_cells, D_HEAD)
            rows_now = lax.dynamic_slice_in_dim(acc_grid, row_index, 3, 2)
            rows_now = rows_now.at[:, time_pick, row_pick, col_pick].add(shaped)
            return lax.dynamic_update_slice_in_dim(acc_grid, rows_now, row_index, 2)

        carry = (spread(key_acc, key_part), spread(value_acc, value_part))
        return (carry, (query_part, log_total[..., 0], delta_row[..., 0]))

    zero_grads = jnp.zeros(keys_ext.shape, jnp.float32)
    (key_acc, value_acc), row_outputs = lax.scan(
        partial(query_row, True), (zero_grads, zero_grads), jnp.arange(TH_DEV)
    )
    from_below = (
        shifted(key_acc[:, :, -1:].astype(jnp.bfloat16), "height", 1).astype(jnp.float32),
        shifted(value_acc[:, :, -1:].astype(jnp.bfloat16), "height", 1).astype(jnp.float32),
    )
    from_above = (
        shifted(key_acc[:, :, :1].astype(jnp.bfloat16), "height", -1).astype(jnp.float32),
        shifted(value_acc[:, :, :1].astype(jnp.bfloat16), "height", -1).astype(jnp.float32),
    )

    def fold_rows(acc_grid, lower_in, upper_in):
        acc_grid = acc_grid.at[:, :, 1:2].add(lower_in)
        acc_grid = acc_grid.at[:, :, TH_DEV : TH_DEV + 1].add(upper_in)
        return acc_grid[:, :, 1 : TH_DEV + 1]

    key_core = fold_rows(key_acc, from_below[0], from_above[0])
    value_core = fold_rows(value_acc, from_below[1], from_above[1])
    from_before = shifted((key_core[:, 2:3], value_core[:, 2:3]), "tm", 1)
    from_after = shifted((key_core[:, 0:1], value_core[:, 0:1]), "tm", -1)
    key_mid = key_core[:, 1] + from_before[0][:, 0] + from_after[0][:, 0]
    value_mid = value_core[:, 1] + from_before[1][:, 0] + from_after[1][:, 0]

    def rim_of(mid_grid):
        return jnp.where(half_index == 0, mid_grid[:, :, -2:], mid_grid[:, :, :2])

    rim_back = (
        passed_along(rim_of(key_mid).astype(jnp.bfloat16), "seq", seq_count // 2).astype(
            jnp.float32
        ),
        passed_along(rim_of(value_mid).astype(jnp.bfloat16), "seq", seq_count // 2).astype(
            jnp.float32
        ),
    )

    def settle(mid_grid, received):
        left_side = jnp.concatenate(
            [
                mid_grid[:, :, : tiles_half - 2],
                mid_grid[:, :, tiles_half - 2 : tiles_half] + received,
            ],
            axis=2,
        )
        right_side = jnp.concatenate([mid_grid[:, :, 2:4] + received, mid_grid[:, :, 4:]], axis=2)
        return jnp.where(half_index == 0, left_side, right_side)

    key_grid = from_tiles(settle(key_mid, rim_back[0])[:, None], TILE).astype(jnp.bfloat16)
    value_grid = from_tiles(settle(value_mid, rim_back[1])[:, None], TILE).astype(jnp.bfloat16)
    query_grid = from_tiles(jnp.moveaxis(row_outputs[0], 0, 1)[:, None], TILE).astype(jnp.bfloat16)

    def to_lines(grid_part):
        return grid_part.reshape(groups, TILE * TILE * TH_DEV, half_width, D_HEAD)

    returned = (
        lax.all_to_all(to_lines(query_grid), "seq", split_axis=1, concat_axis=0, tiled=True),
        lax.all_to_all(to_lines(key_grid), "seq", split_axis=1, concat_axis=0, tiled=True),
        lax.all_to_all(to_lines(value_grid), "seq", split_axis=1, concat_axis=0, tiled=True),
    )

    def to_rows(grid_part):
        split_rows = grid_part.reshape(2, HEADS, lines_dev, half_width, D_HEAD)
        return split_rows.transpose(2, 0, 3, 1, 4).reshape(
            lines_dev * 2 * half_width, HEADS * D_HEAD
        )

    return (to_rows(returned[0]), to_rows(returned[1]), to_rows(returned[2]))


TOK = TILE * TILE
SPAN = 3
SLOTS = 4
PLAN = ((1, 0), (1, 1), (1, 2), (1, 3), (2, 0), (2, 1), (2, 2), (2, 3), (3, 0), (3, 1), (3, 2), (3, 3))
LANES = 2 * D_HEAD
LINES = TW * TOK
LOG2_E = 1.4426950408889634
VMEM_BYTES = 56 * 1024 * 1024
NT = (((1,), (1,)), ((), ()))
NN = (((1,), (0,)), ((), ()))
TN = (((0,), (0,)), ((), ()))
ANYWHERE = pl.BlockSpec(memory_space=pl.ANY)
SCALARS = pl.BlockSpec(memory_space=pltpu.SMEM)
WHOLE = pl.BlockSpec(memory_space=pltpu.VMEM)
PARAMS = pltpu.CompilerParams(vmem_limit_bytes=VMEM_BYTES)


def row_order(inverse):
    target = lax.broadcasted_iota(jnp.int32, (LINES, LINES), 0)
    source = lax.broadcasted_iota(jnp.int32, (LINES, LINES), 1)
    if inverse:
        target, source = source, target
    col, line, x = target // TOK, (target // TILE) % TILE, target % TILE
    return (source == line * (TW * TILE) + col * TILE + x).astype(jnp.bfloat16)


def split_kernel(seats, turn, turns, pairs, place_ref, *refs):
    count = len(seats)
    arrays, outs = refs[: 2 * pairs], refs[2 * pairs : 2 * pairs + count]
    taken, ready, in_sem, out_sem = refs[2 * pairs + count :]
    loads = []
    for k in range(count):
        first = pl.multiple_of(((place_ref[0] ^ seats[k]) * turns + turn) * D_HEAD, D_HEAD)
        loads.append(
            [
                pltpu.make_async_copy(
                    ref.at[:, pl.ds(first, D_HEAD)], taken.at[k, which], in_sem.at[k, which]
                )
                for which, ref in enumerate(arrays)
            ]
        )
        for copy in loads[k]:
            copy.start()
    order = row_order(False)
    stores = []
    for k in range(count):
        for copy in loads[k]:
            copy.wait()
        for pair in range(pairs):
            for row in range(2):
                lines = slice(row * LINES, (row + 1) * LINES)
                rows = jnp.concatenate(
                    [taken[k, 2 * pair, lines, :], taken[k, 2 * pair + 1, lines, :]], axis=1
                )
                moved = lax.dot_general(order, rows, NN, preferred_element_type=jnp.float32)
                ready[k, pair, row] = moved.astype(jnp.bfloat16)
        stores.append(pltpu.make_async_copy(ready.at[k], outs[k], out_sem.at[k]))
        stores[k].start()
    for copy in stores:
        copy.wait()


def split_heads(seats, turn, turns, place, arrays):
    count, rows, pairs = len(seats), arrays[0].shape[0], len(arrays) // 2
    return pl.pallas_call(
        lambda *refs: split_kernel(seats, turn, turns, pairs, *refs),
        in_specs=[SCALARS] + [ANYWHERE] * (2 * pairs),
        out_specs=[ANYWHERE] * count,
        out_shape=[jax.ShapeDtypeStruct((pairs, 2, LINES, LANES), jnp.bfloat16)] * count,
        scratch_shapes=[
            pltpu.VMEM((count, 2 * pairs, rows, D_HEAD), jnp.bfloat16),
            pltpu.VMEM((count, pairs, 2, LINES, LANES), jnp.bfloat16),
            pltpu.SemaphoreType.DMA((count, 2 * pairs)),
            pltpu.SemaphoreType.DMA((count,)),
        ],
        compiler_params=PARAMS,
    )(place, *arrays)


def join_kernel(seats, turn, turns, kept, place_ref, *refs):
    count = len(seats)
    blocks, outs = refs[:count], refs[count + kept : count + kept + 3]
    taken, ready, in_sem, out_sem = refs[count + kept + 3 :]
    loads = []
    for n in range(count):
        loads.append(pltpu.make_async_copy(blocks[n], taken.at[n], in_sem.at[n]))
        loads[n].start()
    order = row_order(True)
    stores = []
    for n, k in enumerate(seats):
        loads[n].wait()
        for row in range(2):
            back = lax.dot_general(
                order, taken[n, row], NN, preferred_element_type=jnp.float32
            ).astype(jnp.bfloat16)
            for which in range(3):
                ready[n, which, row * LINES : (row + 1) * LINES, :] = back[
                    :, which * D_HEAD : (which + 1) * D_HEAD
                ]
        first = pl.multiple_of(((place_ref[0] ^ k) * turns + turn) * D_HEAD, D_HEAD)
        for which in range(3):
            copy = pltpu.make_async_copy(
                ready.at[n, which], outs[which].at[:, pl.ds(first, D_HEAD)], out_sem.at[n, which]
            )
            copy.start()
            stores.append(copy)
    for copy in stores:
        copy.wait()


def join_heads(seats, turn, turns, place, blocks, earlier):
    count, rows, lanes = len(seats), 2 * LINES, blocks[0].shape[-1]
    return pl.pallas_call(
        lambda *refs: join_kernel(seats, turn, turns, len(earlier), *refs),
        in_specs=[SCALARS] + [ANYWHERE] * (count + len(earlier)),
        out_specs=[ANYWHERE] * 3,
        out_shape=[jax.ShapeDtypeStruct((rows, HEADS * D_HEAD), jnp.bfloat16)] * 3,
        scratch_shapes=[
            pltpu.VMEM((count, 2, LINES, lanes), jnp.bfloat16),
            pltpu.VMEM((count, 3, rows, D_HEAD), jnp.bfloat16),
            pltpu.SemaphoreType.DMA((count,)),
            pltpu.SemaphoreType.DMA((count, 3)),
        ],
        input_output_aliases={1 + count + n: n for n in range(len(earlier))},
        compiler_params=PARAMS,
    )(place, *blocks, *earlier)


def edge_kernel(places, *refs):
    blocks, edges = refs[:places], refs[places : places + 2]
    rows, in_sem, out_sem = refs[places + 2 :]
    loads = [pltpu.make_async_copy(blocks[k].at[0], rows.at[k], in_sem.at[k]) for k in range(places)]
    for copy in loads:
        copy.start()
    stores = []
    for k in range(places):
        loads[k].wait()
        for row in range(2):
            copy = pltpu.make_async_copy(rows.at[k, row], edges[row].at[k], out_sem.at[k, row])
            copy.start()
            stores.append(copy)
    for copy in stores:
        copy.wait()


def edge_rows(places, blocks):
    return pl.pallas_call(
        lambda *refs: edge_kernel(places, *refs),
        in_specs=[ANYWHERE] * places,
        out_specs=[ANYWHERE] * 2,
        out_shape=[jax.ShapeDtypeStruct((places, LINES, LANES), jnp.bfloat16)] * 2,
        scratch_shapes=[
            pltpu.VMEM((places, 2, LINES, LANES), jnp.bfloat16),
            pltpu.SemaphoreType.DMA((places,)),
            pltpu.SemaphoreType.DMA((places, 2)),
        ],
        compiler_params=PARAMS,
    )(*blocks)


def grad_kernel(places, count, place_ref, start_ref, bias_ref, *refs):
    groups = [refs[n * places : (n + 1) * places] for n in range(count)]
    (from_above, from_below), outs = refs[count * places :][:2], refs[count * places + 2 :]
    dq_refs, acc_out, above_ref, below_ref = outs[:places], *outs[places : places + 3]
    kv, own_rows, acc, dq, scores, low, in_sem, halo_sem, out_sem = outs[places + 3 :]
    frames = places // TILE
    scale = D_HEAD**-0.5
    copies = []
    for k in range(places):
        seat = place_ref[0] ^ k
        spot = (seat // TILE, seat % TILE)
        copies += [
            pltpu.make_async_copy(groups[0][k].at[0], kv.at[pl.ds(1, 2), *spot], in_sem.at[k, 0]),
            pltpu.make_async_copy(groups[-1][k].at[2 - count], own_rows.at[:, *spot], in_sem.at[k, 1]),
            pltpu.make_async_copy(from_above.at[k], kv.at[0, *spot], halo_sem.at[k, 0]),
            pltpu.make_async_copy(from_below.at[k], kv.at[3, *spot], halo_sem.at[k, 1]),
        ]
    for copy in copies:
        copy.start()
    acc[...] = jnp.zeros(acc.shape, acc.dtype)
    for copy in copies:
        copy.wait()
    part = places * SPAN * TOK
    piece = SPAN * TOK

    def diagonal(own):
        cells = own.shape[0] // frames
        blank = jnp.zeros((cells, D_HEAD), own.dtype)
        lines = []
        for frame in range(frames):
            line = [blank] * frames
            line[frame] = own[frame * cells : (frame + 1) * cells, :]
            lines.append(jnp.concatenate(line, axis=1))
        return jnp.concatenate(lines, axis=0)

    def near_keys(row, near, windows, lanes):
        return jnp.concatenate(
            [kv[row + near, :, :, window, lanes].reshape(part, D_HEAD) for window in windows],
            axis=1,
        )

    def score_phase(slot, row, col):
        here = pl.multiple_of(col * TOK, TOK)
        windows = [
            pl.ds(pl.multiple_of(start_ref[(row * TW + col) * frames + f] * TOK, TOK), piece)
            for f in range(frames)
        ]
        own = own_rows[row, :, :, pl.ds(here, TOK), :].reshape(-1, LANES)
        query, grad = diagonal(own[:, :D_HEAD]), diagonal(own[:, D_HEAD:])
        top = None
        for near in range(3):
            score_raw = lax.dot_general(
                near_keys(row, near, windows, slice(0, D_HEAD)), query, NT,
                preferred_element_type=jnp.float32,
            )
            scores[slot, near, :, D_HEAD:] = lax.dot_general(
                near_keys(row, near, windows, slice(D_HEAD, LANES)), grad, NT,
                preferred_element_type=jnp.float32,
            )
            for frame in range(frames):
                first = (near * frames + frame) * SPAN
                bias = jnp.concatenate(
                    [
                        jnp.broadcast_to(
                            bias_ref[row, col, first + c : first + c + 1, :], (TOK, D_HEAD)
                        )
                        for c in range(SPAN)
                    ],
                    axis=0,
                )
                for sub in range(TILE):
                    at = (frame * TILE + sub) * piece
                    score = score_raw[at : at + piece, :] * (scale * LOG2_E) + bias
                    scores[slot, near, at : at + piece, :D_HEAD] = score
                    most = jnp.max(score.reshape(-1, 8, D_HEAD), axis=0)
                    top = most if top is None else jnp.maximum(top, most)
        return here, windows, query, grad, jnp.max(top, axis=0, keepdims=True)

    def total_phase(slot, top):
        total = jnp.zeros((8, D_HEAD), jnp.float32)
        delta = jnp.zeros((8, D_HEAD), jnp.float32)
        for near in range(3):
            for at in range(0, part, piece):
                prob = jnp.exp2(scores[slot, near, at : at + piece, :D_HEAD] - top)
                total = total + jnp.sum(prob.reshape(-1, 8, D_HEAD), axis=0)
                grad = prob * scores[slot, near, at : at + piece, D_HEAD:]
                delta = delta + jnp.sum(grad.reshape(-1, 8, D_HEAD), axis=0)
        total = jnp.sum(total, axis=0, keepdims=True)
        delta = jnp.sum(delta, axis=0, keepdims=True) / total
        return top + jnp.log2(total), delta

    def grad_phase(slot, row, here, windows, query, grad, log_total, delta):
        query_grad = None
        for near in range(3):
            for at in range(0, part, piece):
                weight = jnp.exp2(scores[slot, near, at : at + piece, :D_HEAD] - log_total)
                dscore = weight * (scores[slot, near, at : at + piece, D_HEAD:] - delta)
                low[slot, near, at : at + piece, :D_HEAD] = dscore.astype(jnp.bfloat16)
                low[slot, near, at : at + piece, D_HEAD:] = weight.astype(jnp.bfloat16)
            key_part = lax.dot_general(
                low[slot, near, :, :D_HEAD], query, NN, preferred_element_type=jnp.float32
            )
            value_part = lax.dot_general(
                low[slot, near, :, D_HEAD:], grad, NN, preferred_element_type=jnp.float32
            )
            for f in range(frames):
                lanes = slice(f * D_HEAD, (f + 1) * D_HEAD)
                added = jnp.concatenate([key_part[:, lanes], value_part[:, lanes]], axis=1)
                spot = (row + near, slice(None), slice(None), windows[f], slice(None))
                acc[spot] = acc[spot] + added.reshape(frames, TILE, piece, LANES)
            more = lax.dot_general(
                low[slot, near, :, :D_HEAD],
                near_keys(row, near, windows, slice(0, D_HEAD)),
                TN,
                preferred_element_type=jnp.float32,
            )
            query_grad = more if query_grad is None else query_grad + more
        for f in range(frames):
            cells = query_grad.shape[0] // frames
            mine = query_grad[f * cells : (f + 1) * cells, f * D_HEAD : (f + 1) * D_HEAD]
            dq[row, f, :, pl.ds(here, TOK), :] = (
                (mine * scale).astype(jnp.bfloat16).reshape(TILE, TOK, D_HEAD)
            )

    def group(step, _):
        known, sums = {}, {}
        for phase, slot in PLAN:
            row = slot % 2
            if phase == 1:
                known[slot] = score_phase(slot, row, step * (SLOTS // 2) + slot // 2)
            elif phase == 2:
                sums[slot] = total_phase(slot, known[slot][-1])
            else:
                grad_phase(slot, row, *known[slot][:-1], *sums[slot])
        return 0

    lax.fori_loop(0, 2 * TW // SLOTS, group, 0)
    copies = []
    for k in range(places):
        seat = place_ref[0] ^ k
        spot = (seat // TILE, seat % TILE)
        copies += [
            pltpu.make_async_copy(dq.at[:, *spot], dq_refs[k], out_sem.at[k, 0]),
            pltpu.make_async_copy(acc.at[pl.ds(1, 2), *spot], acc_out.at[k], out_sem.at[k, 1]),
        ]
    for copy in copies:
        copy.start()
    for k in range(places):
        seat = place_ref[0] ^ k
        spot = (seat // TILE, seat % TILE)
        above_ref[k] = acc[0, *spot].astype(jnp.bfloat16)
        below_ref[k] = acc[3, *spot].astype(jnp.bfloat16)
    for copy in copies:
        copy.wait()


def head_grads(places, place, starts, bias, groups, from_above, from_below):
    frames = places // TILE
    part = places * SPAN * TOK
    results = pl.pallas_call(
        lambda *refs: grad_kernel(places, len(groups), *refs),
        in_specs=[SCALARS, SCALARS, WHOLE] + [ANYWHERE] * (len(groups) * places + 2),
        out_specs=[ANYWHERE] * (places + 1) + [WHOLE] * 2,
        out_shape=[jax.ShapeDtypeStruct((2, LINES, D_HEAD), jnp.bfloat16)] * places
        + [jax.ShapeDtypeStruct((places, 2, LINES, LANES), jnp.float32)]
        + [jax.ShapeDtypeStruct((places, LINES, LANES), jnp.bfloat16)] * 2,
        scratch_shapes=[
            pltpu.VMEM((4, frames, TILE, LINES, LANES), jnp.bfloat16),
            pltpu.VMEM((2, frames, TILE, LINES, LANES), jnp.bfloat16),
            pltpu.VMEM((4, frames, TILE, LINES, LANES), jnp.float32),
            pltpu.VMEM((2, frames, TILE, LINES, D_HEAD), jnp.bfloat16),
            pltpu.VMEM((SLOTS, 3, part, LANES), jnp.float32),
            pltpu.VMEM((SLOTS, 3, part, LANES), jnp.bfloat16),
            pltpu.SemaphoreType.DMA((places, 2)),
            pltpu.SemaphoreType.DMA((places, 2)),
            pltpu.SemaphoreType.DMA((places, 2)),
        ],
        compiler_params=PARAMS,
        cost_estimate=pl.CostEstimate(
            flops=1_000_000, bytes_accessed=0, transcendentals=0
        ),
    )(place, starts, bias, *[block for group in groups for block in group], from_above, from_below)
    return results[:places], *results[places:]


def finish_kernel(count, acc_ref, above_ref, below_ref, *refs):
    queries, outs = refs[:count], refs[count:]
    lane = lax.broadcasted_iota(jnp.int32, (1, LANES), 1)
    factor = jnp.where(lane < D_HEAD, D_HEAD**-0.5, 1.0)
    for k in range(count):
        for row, ref in enumerate((above_ref, below_ref)):
            total = acc_ref[k, row] + ref[k].astype(jnp.float32)
            outs[k][row, :, :LANES] = (total * factor).astype(jnp.bfloat16)
        outs[k][:, :, LANES:] = queries[k][...]


def finish_pairs(seats, acc, above, below, query):
    count, lanes = len(seats), LANES + D_HEAD
    at = seats[0] // count
    halo = pl.BlockSpec((count, LINES, LANES), lambda g: (at, 0, 0))
    block = pl.BlockSpec((2, LINES, D_HEAD), lambda g: (0, 0, 0))
    return pl.pallas_call(
        lambda *refs: finish_kernel(count, *refs),
        grid=(1,),
        in_specs=[pl.BlockSpec((count, 2, LINES, LANES), lambda g: (at, 0, 0, 0)), halo, halo]
        + [block] * count,
        out_specs=[pl.BlockSpec((2, LINES, lanes), lambda g: (0, 0, 0))] * count,
        out_shape=[jax.ShapeDtypeStruct((2, LINES, lanes), jnp.bfloat16)] * count,
        compiler_params=PARAMS,
    )(acc, above, below, *[query[k] for k in seats])


def window_tables(tile_valid, width_shift, first_row):
    frames, _, cols = tile_valid.shape
    shift_own = lax.dynamic_slice_in_dim(width_shift, first_row, 2, 1)
    first = jnp.clip(jnp.arange(cols) + shift_own - 1, 0, cols - SPAN)
    valid = lax.dynamic_slice_in_dim(
        jnp.pad(tile_valid, ((0, 0), (1, 1), (2, 2))), first_row, 4, 1
    )
    near = jnp.stack([valid[:, n : n + 2] for n in range(3)])[:, :, None]
    moved = jnp.stack([near[..., d : d + cols] for d in range(5)])
    shift = first - (jnp.arange(cols) - 1)
    chosen = jnp.where(shift == -1, moved[0:3], jnp.where(shift == 0, moved[1:4], moved[2:5]))
    place_of = jnp.arange(3).reshape(-1, 1, 1, 1, 1, 1)
    near_of = jnp.arange(3).reshape(1, -1, 1, 1, 1, 1)
    key_frame = jnp.arange(frames).reshape(1, 1, -1, 1, 1, 1)
    frame = jnp.arange(frames).reshape(1, 1, 1, -1, 1, 1)
    own = (near_of == 1) & (key_frame == frame) & (place_of + shift == 1)
    bias = jnp.where((chosen == 1) | own, 0.0, MASKED_SCORE).astype(jnp.float32)
    bias = bias.transpose(4, 5, 1, 2, 0, 3).reshape(2, cols, 3 * frames * SPAN, frames, 1)
    bias = jnp.broadcast_to(bias, bias.shape[:4] + (TILE**3,))
    return (
        first.transpose(1, 2, 0).reshape(-1),
        bias.reshape(2, cols, 3 * frames * SPAN, frames * TILE**3),
    )


def place_shards(queries, key_states, value_states, out_grad, tile_valid, width_shift):
    frames = tile_valid.shape[0]
    places = frames * TILE
    turns = HEADS // places
    seq_count = lax.axis_size("seq")
    heights = lax.axis_size("height")
    seq_index = lax.axis_index("seq")
    place = (lax.axis_index("tm") * TILE + seq_index // 2).reshape(1)
    first_row = lax.axis_index("height") * TH_DEV + seq_index % 2 * 2
    starts, bias = window_tables(tile_valid, width_shift, first_row)
    chain = [
        [h * seq_count + frame * 2 + half for h in range(heights) for half in range(2)]
        for frame in range(TILE)
    ]
    down = [pair for line in chain for pair in zip(line[:-1], line[1:])]
    up = [(b, a) for a, b in down]

    def send(block, k):
        return lax.ppermute(block, ("tm", "seq"), [(i, i ^ (2 * k)) for i in range(2 * places)])

    def step(block, route):
        return lax.ppermute(block, ("height", "seq"), route)

    def exchange(blocks, order):
        moved = dict(enumerate(blocks))
        for k in order:
            moved[k] = send(blocks[k], k)
        return [moved[k] for k in range(places)]

    natural = list(range(1, places))
    halves = (range(places // 2), range(places // 2, places))
    far, near = [k for k in natural if k & 2], [k for k in natural if not k & 2]
    held = [far[-1], near[0]]
    mixed = far[:-1] + near[1:] + held

    def after(blocks, results):
        kept, results = lax.optimization_barrier(([blocks[k] for k in held], results))
        blocks = list(blocks)
        for k, block in zip(held, kept):
            blocks[k] = block
        return blocks, results

    def ordered(first, then):
        return lax.optimization_barrier((first, then))

    def ordered(first, then):
        return lax.optimization_barrier((first, then))

    def ordered(first, then):
        return lax.optimization_barrier((first, then))

    arrays = (key_states, value_states, queries, out_grad)
    outs = ()
    blocks = []
    for seats in halves:
        blocks += split_heads(seats, 0, turns, place, arrays)
    groups = [exchange(blocks, natural)]
    leaving = None
    for turn in range(turns):
        more = turn + 1 < turns
        if more:
            coming = split_heads(range(places), turn + 1, turns, place, arrays)
            groups[-1][1:6], coming = ordered(groups[-1][1:6], coming)
        first, last = edge_rows(places, groups[0])
        grads = head_grads(places, place, starts, bias, groups, step(last, down), step(first, up))
        if leaving is not None:
            leaving, grads = after(leaving, grads)
            left = exchange(leaving, mixed)
            passed, grads = ordered([left[k] for k in mixed[:-2]], grads)
            for k, block in zip(mixed, passed):
                left[k] = block
            outs = join_heads(range(places), turn - 1, turns, place, left, outs)
        if more:
            coming, grads = after(coming, grads)
            groups = [exchange(coming, mixed)]
        dq, acc, above, below = grads
        from_above, from_below = step(below, down), step(above, up)
        leaving = []
        for seats in [range(places)] if more else halves:
            leaving += finish_pairs(seats, acc, from_above, from_below, dq)
    left = exchange(leaving, natural)
    for seats in (range(places - 2), range(places - 2, places)):
        outs = join_heads(seats, turns - 1, turns, place, [left[k] for k in seats], outs)
    key_out, value_out, query_out = outs
    return query_out, key_out, value_out


def solution(mesh):
    frames, seq_count = mesh.shape["tm"], mesh.shape["seq"]
    by_place = frames == 2 and seq_count == 2 * TILE
    placed = (
        P(("tm", "height", "seq"), None),
        P(("tm", "height", "seq"), None),
        P(("tm", "height", "seq"), None),
        P(("tm", "height", "seq"), None),
        P(),
        P(),
    )
    return jax.shard_map(
        place_shards if by_place else shards,
        mesh=mesh,
        in_specs=placed,
        out_specs=(
            P(("tm", "height", "seq"), None),
            P(("tm", "height", "seq"), None),
            P(("tm", "height", "seq"), None),
        ),
        check_vma=False,
    )
```
